128 devices in a mesh: tiles: 32 (over x, y, core), views: 4 (over z).
Axes of the slice: x: 4, y: 4, z: 4, core: 2. Of those that a mesh axis runs over, the one named last changes fastest.
Arguments:
- params: float32 [59, 262144], P(None, 'tiles'), may hold values from -7 to 5, as said below
- camera: float32 [4, 4], P('views'), may hold values from -0.03 to 0.03
- tile_lists: int32 [4, 256, 1024], P('views', 'tiles'), may hold values from 0 to 262143, as said below
- tile_counts: int32 [4, 256], P('views', 'tiles'), may hold values from 256 to 1024
- d_image: float32 [4, 256, 3, 256], P('views', 'tiles'), may hold values from -6 to 6
Outputs:
- image: float32 [4, 256, 3, 256], P('views', 'tiles')
- grads: float32 [59, 262144], P(None, ('tiles', 'views'))
The draws below stay inside these ranges and needn't reach their ends.
Inputs may be any that keep to these rules, and one draw needn't show every extreme that they name: `params`: each column is one Gaussian: mean (rows 0 to 2, the third 3 or more), log scales (rows 3 to 5), a quaternion (rows 6 to 9) whose first entry is 1 or more, an opacity logit (row 10), and 16 spherical-harmonic coefficients for each of 3 colors (row 11 + 3 k + c for coefficient k of color c). `tile_lists`: gaussian g belongs to shard g // 8192. Entries past a tile's count are 0. Among the live entries of the 8 tiles of one device, at most 384 name Gaussians of one shard; in every view one shard is named exactly 384 times by every device.
All inputs are finite; a program needn't handle non-finite values.
Results may differ from the reference program's by a relative error of at most 0.0003.
Values sent between devices are 32-bit elements; how exact they have to be, the bound alone decides.
No kernel may reach another device: no remote copies, remote signals or barrier semaphores. Data moves between devices by JAX's collectives and lax.ppermute only.
A program may use at most 128 MiB of HBM per device.

```python
import math
import jax
import jax.numpy as jnp
from jax import lax

PIX = 256
TILES_DEV = 8
G_DEV = 8192
SLOTS = 1024
VIEWS = 4
TILES = 256
GAUSS = 262144
PER_TILE = 32
CAPACITY = 384


focal_px = 600.0


def draw_params(key, part):
    key = jax.random.fold_in(key, 5)
    subkeys = jax.random.split(key, 8)
    gauss_index = jnp.arange(GAUSS, dtype=jnp.int32)
    home_tile = gauss_index % G_DEV // PER_TILE
    tile_row = (home_tile // TILES_DEV).astype(jnp.float32)
    tile_col = (home_tile % TILES_DEV).astype(jnp.float32)
    jitter = jax.random.uniform(subkeys[0], (2, GAUSS), jnp.float32, -8.0, 8.0)
    pix_x = (tile_col + 0.5) * 16.0 + jitter[0]
    pix_y = (tile_row + 0.5) * 16.0 + jitter[1]
    depth_z = jax.random.uniform(subkeys[1], (GAUSS,), jnp.float32, 3.0, 5.0)
    mean_x = (pix_x - TILES_DEV * 8.0) * depth_z / focal_px
    mean_y = (pix_y - TILES // TILES_DEV * 8.0) * depth_z / focal_px
    log_scale = jax.random.uniform(subkeys[2], (3, GAUSS), jnp.float32, math.log(0.012), math.log(0.2))
    logit = jax.random.uniform(subkeys[3], (1, GAUSS), jnp.float32, -7.0, -2.5)
    dc_boost = jnp.where(jnp.arange(48, dtype=jnp.int32) < 3, 2.5, 1.0)[:, None]
    quat_head = 1.0 + jax.random.uniform(subkeys[4], (1, GAUSS), jnp.float32, 0.0, 1.0)
    quat_tail = jax.random.uniform(subkeys[5], (3, GAUSS), jnp.float32, -1.0, 1.0)
    harmonic = 0.4 * jax.random.truncated_normal(subkeys[6], -2.5, 2.5, (48, GAUSS), jnp.float32) * dc_boost
    return jnp.concatenate([mean_x[None], mean_y[None], depth_z[None], log_scale, quat_head, quat_tail, logit, harmonic], axis=0)


def lists_and_counts(key):
    key = jax.random.fold_in(key, 17)
    subkeys = jax.random.split(key, 8)
    owners = TILES // TILES_DEV
    slot_total = TILES_DEV * SLOTS
    counts = jax.random.randint(subkeys[0], (VIEWS, owners, TILES_DEV), SLOTS // 4, SLOTS + 1, dtype=jnp.int32)
    full_tile = jax.random.randint(subkeys[1], (VIEWS, owners, 1), 0, TILES_DEV, dtype=jnp.int32)
    column = jnp.arange(TILES_DEV, dtype=jnp.int32)
    counts = jnp.where(column == full_tile, SLOTS, counts)
    counts = jnp.where(column == (full_tile + 1) % TILES_DEV, SLOTS // 4, counts)
    live_slot = (jnp.arange(SLOTS, dtype=jnp.int32) < counts[..., None]).reshape(VIEWS, owners, slot_total)
    star_owner = jax.random.randint(subkeys[2], (VIEWS, 1, 1), 0, owners, dtype=jnp.int32)
    star_owner = star_owner.at[0].set(owners - 1)
    others = jnp.arange((owners - 1) * CAPACITY, dtype=jnp.int32) // CAPACITY
    shuffle_keys = jax.random.split(subkeys[3], VIEWS * owners)
    shuffled = jax.vmap(lambda one_key: jax.random.permutation(one_key, others))(shuffle_keys).astype(jnp.int32)
    shuffled = shuffled.reshape(VIEWS, owners, (owners - 1) * CAPACITY)
    shuffled = shuffled + (shuffled >= star_owner).astype(jnp.int32)
    sequence = jnp.concatenate([jnp.broadcast_to(star_owner, (VIEWS, owners, CAPACITY)), shuffled], axis=2)[:, :, :slot_total]
    priority_keys = jax.random.split(subkeys[4], VIEWS * owners)
    priority = jax.vmap(lambda one_key: jax.random.permutation(one_key, slot_total))(priority_keys).astype(jnp.int32)
    priority = priority.reshape(VIEWS, owners, slot_total)
    priority = jnp.where(live_slot, priority, priority + slot_total)
    priority = priority.at[0, owners - 1, (TILES_DEV - 1) * SLOTS].set(-1)
    ordering = jnp.argsort(priority, axis=2, stable=True).astype(jnp.int32)
    position = jnp.argsort(ordering, axis=2, stable=True).astype(jnp.int32)
    owner_label = jnp.take_along_axis(sequence, position, axis=2)
    row_offsets = jax.random.randint(subkeys[5], (VIEWS, owners, slot_total), -3, 4, dtype=jnp.int32)
    col_offsets = jax.random.randint(subkeys[7], (VIEWS, owners, slot_total), -1, 2, dtype=jnp.int32)
    slot_tile = jnp.arange(slot_total, dtype=jnp.int32) // SLOTS
    device_row = jnp.arange(owners, dtype=jnp.int32)[None, :, None]
    home_row = jnp.clip(device_row + row_offsets, 0, owners - 1)
    home_col = jnp.clip(slot_tile + col_offsets, 0, TILES_DEV - 1)
    within_home = jax.random.randint(subkeys[6], (VIEWS, owners, slot_total), 0, PER_TILE, dtype=jnp.int32)
    local_index = (home_row * TILES_DEV + home_col) * PER_TILE + within_home
    local_index = local_index.at[0, owners - 1, (TILES_DEV - 1) * SLOTS].set(G_DEV - 1)
    gauss_ids = jnp.where(live_slot, owner_label * G_DEV + local_index, 0)
    return (gauss_ids.reshape(VIEWS, TILES, SLOTS), counts.reshape(VIEWS, TILES))


def draw_tile_lists(key, part):
    return lists_and_counts(key)[0]


def draw_tile_counts(key, part):
    return lists_and_counts(key)[1]


def steps_of(key, dims, shards, smallest, largest):
    def one(dim, shards_of):
        steps = jax.random.uniform(jax.random.fold_in(jax.random.fold_in(key, 6), dim), (shards_of,), jnp.float32, smallest / len(shards), largest / len(shards))
        return jnp.repeat(jnp.exp(steps), dims[dim] // shards_of).reshape((-1,) + (1,) * (len(dims) - dim - 1))

    loudness = one(*shards[0])
    for cut in shards[1:]:
        loudness = loudness * one(*cut)
    return loudness


def bell_draw(stream_key, dims, scale, bound, pieces=(), held_as=jnp.bfloat16):
    array = scale * jax.random.normal(stream_key, dims, jnp.float32)
    if pieces:
        array = array * steps_of(stream_key, dims, pieces, -0.22, 0.18)
    return jnp.clip(array, -bound, bound).astype(held_as)


def setup_inputs(seed: int = 0) -> dict:
    key_list = jax.random.split(jax.random.key(seed), 6)
    return {
        "params": draw_params(jax.random.fold_in(key_list[5], 71), 0),
        "camera": jnp.clip(jax.random.uniform(key_list[1], (VIEWS, 4), jnp.float32, -0.03, 0.03) * steps_of(key_list[1], (VIEWS, 4), ((0, 4),), -0.4, 0.0), -0.03, 0.03),
        "tile_lists": draw_tile_lists(jax.random.fold_in(key_list[5], 71), 0),
        "tile_counts": draw_tile_counts(jax.random.fold_in(key_list[5], 71), 0),
        "d_image": bell_draw(key_list[4], (VIEWS, TILES, 3, PIX), 1.0, 6.0, ((0, 4), (1, 32)), jnp.float32),
    }


focal_px = 600.0
lowpass = 0.3
highest = lax.Precision.HIGHEST
harmonic_zero = 0.28209479177387814
harmonic_one = 0.4886025119029199
harmonic_two = (1.0925484305920792, -1.0925484305920792, 0.31539156525252005, -1.0925484305920792, 0.5462742152960396)
harmonic_three = (-0.5900435899266435, 2.890611442640554, -0.4570457994644658, 0.3731763325901154, -0.4570457994644658, 1.445305721320277, -0.5900435899266435)

def project(gauss_rows, camera_row, center_x, center_y):
    cosine = jnp.cos(camera_row[0])
    sine_val = jnp.sin(camera_row[0])
    cam_x = cosine * gauss_rows[0] + sine_val * gauss_rows[2] + camera_row[1]
    cam_y = gauss_rows[1] + camera_row[2]
    cam_z = cosine * gauss_rows[2] - sine_val * gauss_rows[0] + camera_row[3]
    inverse_z = 1.0 / cam_z
    pos_u = focal_px * cam_x * inverse_z + center_x
    pos_v = focal_px * cam_y * inverse_z + center_y
    jac_a = focal_px * inverse_z
    jac_b = -focal_px * cam_x * inverse_z * inverse_z
    jac_c = -focal_px * cam_y * inverse_z * inverse_z
    first_row = (jac_a * cosine - jac_b * sine_val, jac_a * sine_val + jac_b * cosine)
    second_row = (-jac_c * sine_val, jac_a, jac_c * cosine)
    quaternion = gauss_rows[6:10]
    quaternion = quaternion / jnp.sqrt(lax.optimization_barrier(jnp.sum(quaternion * quaternion, axis=0)))
    quat_w, quat_x, quat_y, quat_z = (quaternion[0], quaternion[1], quaternion[2], quaternion[3])
    rotation = ((1.0 - 2.0 * (quat_y * quat_y + quat_z * quat_z), 2.0 * (quat_x * quat_y - quat_w * quat_z), 2.0 * (quat_x * quat_z + quat_w * quat_y)), (2.0 * (quat_x * quat_y + quat_w * quat_z), 1.0 - 2.0 * (quat_x * quat_x + quat_z * quat_z), 2.0 * (quat_y * quat_z - quat_w * quat_x)), (2.0 * (quat_x * quat_z - quat_w * quat_y), 2.0 * (quat_y * quat_z + quat_w * quat_x), 1.0 - 2.0 * (quat_x * quat_x + quat_y * quat_y)))
    scales = jnp.exp(gauss_rows[3:6])
    upper_a = [(first_row[0] * rotation[0][entry] + first_row[1] * rotation[2][entry]) * scales[entry] for entry in range(3)]
    lower_a = [(second_row[0] * rotation[0][entry] + second_row[1] * rotation[1][entry] + second_row[2] * rotation[2][entry]) * scales[entry] for entry in range(3)]
    cov_a = upper_a[0] * upper_a[0] + upper_a[1] * upper_a[1] + upper_a[2] * upper_a[2] + lowpass
    cov_b = upper_a[0] * lower_a[0] + upper_a[1] * lower_a[1] + upper_a[2] * lower_a[2]
    cov_c = lower_a[0] * lower_a[0] + lower_a[1] * lower_a[1] + lower_a[2] * lower_a[2] + lowpass
    determinant = cov_a * cov_c - cov_b * cov_b
    conic_a = cov_c / determinant
    conic_b = -cov_b / determinant
    conic_c = cov_a / determinant
    opacity = jax.nn.sigmoid(gauss_rows[10])
    dir_x = cosine * cam_x - sine_val * cam_z
    dir_y = cam_y
    dir_z = sine_val * cam_x + cosine * cam_z
    inv_len = 1.0 / jnp.sqrt(dir_x * dir_x + dir_y * dir_y + dir_z * dir_z)
    dir_x = dir_x * inv_len
    dir_y = dir_y * inv_len
    dir_z = dir_z * inv_len
    sq_x = dir_x * dir_x
    sq_y = dir_y * dir_y
    sq_z = dir_z * dir_z
    harmonics = jnp.stack([jnp.full_like(dir_x, harmonic_zero), -harmonic_one * dir_y, harmonic_one * dir_z, -harmonic_one * dir_x, harmonic_two[0] * dir_x * dir_y, harmonic_two[1] * dir_y * dir_z, harmonic_two[2] * (2.0 * sq_z - sq_x - sq_y), harmonic_two[3] * dir_x * dir_z, harmonic_two[4] * (sq_x - sq_y), harmonic_three[0] * dir_y * (3.0 * sq_x - sq_y), harmonic_three[1] * dir_x * dir_y * dir_z, harmonic_three[2] * dir_y * (4.0 * sq_z - sq_x - sq_y), harmonic_three[3] * dir_z * (2.0 * sq_z - 3.0 * sq_x - 3.0 * sq_y), harmonic_three[4] * dir_x * (4.0 * sq_z - sq_x - sq_y), harmonic_three[5] * dir_z * (sq_x - sq_y), harmonic_three[6] * dir_x * (sq_x - 3.0 * sq_y)])
    coeffs = gauss_rows[11:59].reshape(16, 3, gauss_rows.shape[1])
    colors = lax.optimization_barrier(jnp.sum(harmonics[:, None, :] * coeffs, axis=0)) + 0.5
    return jnp.concatenate([jnp.stack([pos_u, pos_v, conic_a, conic_b, conic_c, opacity]), colors], axis=0)

def strictly_upper(length):
    steps_idx = jnp.arange(length, dtype=jnp.int32)
    return (steps_idx[:, None] < steps_idx[None, :]).astype(jnp.float32)

def render(compact, live_count, tile_row, tile_col):
    slot_count = compact.shape[1]
    pixel_index = jnp.arange(256, dtype=jnp.int32)
    pix_x = (tile_col * 16 + pixel_index % 16).astype(jnp.float32) + 0.5
    pix_y = (tile_row * 16 + pixel_index // 16).astype(jnp.float32) + 0.5
    delta_x = pix_x[:, None] - compact[0][None, :]
    delta_y = pix_y[:, None] - compact[1][None, :]
    exponent = -0.5 * (compact[2][None, :] * delta_x * delta_x + 2.0 * compact[3][None, :] * delta_x * delta_y + compact[4][None, :] * delta_y * delta_y)
    live_slot = jnp.arange(slot_count, dtype=jnp.int32) < live_count
    alphas = jnp.where(live_slot[None, :], compact[5][None, :] * jnp.exp(exponent), 0.0)
    log_keep = jnp.log1p(-alphas).reshape(256, slot_count // 128, 128)
    within = jnp.einsum('pbj,ji->pbi', log_keep, strictly_upper(128), precision=highest)
    totals = lax.optimization_barrier(jnp.sum(log_keep, axis=2))
    before = jnp.einsum('pb,bc->pc', totals, strictly_upper(slot_count // 128), precision=highest)
    transmit = jnp.exp((within + before[:, :, None]).reshape(256, slot_count))
    weight = transmit * alphas
    return jnp.einsum('pi,ci->cp', weight, compact[6:9], precision=highest)

def reference(params, camera, tile_lists, tile_counts, d_image):
    view_count = tile_lists.shape[0]
    tile_count = tile_lists.shape[1]
    slot_count = tile_lists.shape[2]
    channels = params.shape[0]
    center_x = TILES_DEV * 8.0
    center_y = TILES // TILES_DEV * 8.0
    tile_ids = jnp.arange(tile_count, dtype=jnp.int32)
    grad_sum = jnp.zeros_like(params)
    images = []
    for view_id in range(view_count):
        gauss_ids = tile_lists[view_id].reshape(tile_count * slot_count)
        view_rows = params[:, gauss_ids]
        camera_row = camera[view_id]
        counts_row = tile_counts[view_id]

        def one_tile(tile_args):
            tile_rows, live_count, tile_id = tile_args
            compact = project(tile_rows, camera_row, center_x, center_y)
            return render(compact, live_count, tile_id // TILES_DEV, tile_id % TILES_DEV)

        def draw_view(rows_in):
            stacked = jnp.transpose(rows_in.reshape(channels, tile_count, slot_count), (1, 0, 2))
            return lax.map(jax.checkpoint(one_tile), (stacked, counts_row, tile_ids))
        view_image, pull_view = jax.vjp(draw_view, view_rows)
        row_grads, = pull_view(d_image[view_id])
        grad_sum = grad_sum.at[:, gauss_ids].add(row_grads)
        images.append(view_image)
    return (jnp.stack(images), grad_sum)
```

```python
import functools
import math

import jax
import jax.numpy as jnp
from jax import lax
from jax.experimental import pallas as pl
from jax.experimental.pallas import tpu as pltpu
from jax.sharding import PartitionSpec as P

focal_px = 600.0
lowpass = 0.3
harmonic_zero = 0.28209479177387814
harmonic_one = 0.4886025119029199
harmonic_two = (
    1.0925484305920792,
    -1.0925484305920792,
    0.31539156525252005,
    -1.0925484305920792,
    0.5462742152960396,
)
harmonic_three = (
    -0.5900435899266435,
    2.890611442640554,
    -0.4570457994644658,
    0.3731763325901154,
    -0.4570457994644658,
    1.445305721320277,
    -0.5900435899266435,
)
bf16 = jnp.bfloat16
f32 = jnp.float32
i32 = jnp.int32
log2_e = 1.0 / math.log(2.0)
ln_2 = math.log(2.0)
nt_dims = (((1,), (1,)), ((), ()))
vmem_bytes = 56 * 1024 * 1024
fields = 9


def split_two(values):
    upper = values.astype(bf16)
    lower = (values - upper.astype(f32)).astype(bf16)
    return upper, lower


def split_three(values):
    upper = values.astype(bf16)
    rest = values - upper.astype(f32)
    middle = rest.astype(bf16)
    lower = (rest - middle.astype(f32)).astype(bf16)
    return upper, middle, lower


def project(gauss_rows, camera_row, center_x, center_y):
    cosine, sine_val, shift_x, shift_y, shift_z = camera_row
    cam_x = cosine * gauss_rows[0] + sine_val * gauss_rows[2] + shift_x
    cam_y = gauss_rows[1] + shift_y
    cam_z = cosine * gauss_rows[2] - sine_val * gauss_rows[0] + shift_z
    inverse_z = 1.0 / cam_z
    jac_a = focal_px * inverse_z
    pos_u = jac_a * cam_x + center_x
    pos_v = jac_a * cam_y + center_y
    jac_b = -jac_a * cam_x * inverse_z
    jac_c = -jac_a * cam_y * inverse_z
    first_row = (jac_a * cosine - jac_b * sine_val, jac_a * sine_val + jac_b * cosine)
    second_row = (-jac_c * sine_val, jac_a, jac_c * cosine)
    quaternion = gauss_rows[6:10]
    inv_norm = lax.rsqrt(
        quaternion[0] * quaternion[0]
        + quaternion[1] * quaternion[1]
        + quaternion[2] * quaternion[2]
        + quaternion[3] * quaternion[3]
    )
    quat_w, quat_x, quat_y, quat_z = (entry * inv_norm for entry in quaternion)
    rotation = (
        (
            1.0 - 2.0 * (quat_y * quat_y + quat_z * quat_z),
            2.0 * (quat_x * quat_y - quat_w * quat_z),
            2.0 * (quat_x * quat_z + quat_w * quat_y),
        ),
        (
            2.0 * (quat_x * quat_y + quat_w * quat_z),
            1.0 - 2.0 * (quat_x * quat_x + quat_z * quat_z),
            2.0 * (quat_y * quat_z - quat_w * quat_x),
        ),
        (
            2.0 * (quat_x * quat_z - quat_w * quat_y),
            2.0 * (quat_y * quat_z + quat_w * quat_x),
            1.0 - 2.0 * (quat_x * quat_x + quat_y * quat_y),
        ),
    )
    scales = [jnp.exp(entry) for entry in gauss_rows[3:6]]
    upper_a = [
        (first_row[0] * rotation[0][entry] + first_row[1] * rotation[2][entry]) * scales[entry]
        for entry in range(3)
    ]
    lower_a = [
        (
            second_row[0] * rotation[0][entry]
            + second_row[1] * rotation[1][entry]
            + second_row[2] * rotation[2][entry]
        )
        * scales[entry]
        for entry in range(3)
    ]
    cov_a = upper_a[0] * upper_a[0] + upper_a[1] * upper_a[1] + upper_a[2] * upper_a[2] + lowpass
    cov_b = upper_a[0] * lower_a[0] + upper_a[1] * lower_a[1] + upper_a[2] * lower_a[2]
    cov_c = lower_a[0] * lower_a[0] + lower_a[1] * lower_a[1] + lower_a[2] * lower_a[2] + lowpass
    inv_det = 1.0 / (cov_a * cov_c - cov_b * cov_b)
    coef_a = (-0.5 * log2_e) * cov_c * inv_det
    coef_b = log2_e * cov_b * inv_det
    coef_c = (-0.5 * log2_e) * cov_a * inv_det
    log_opacity = -log2_e * jnp.log(1.0 + jnp.exp(-gauss_rows[10]))
    dir_x = cosine * cam_x - sine_val * cam_z
    dir_y = cam_y
    dir_z = sine_val * cam_x + cosine * cam_z
    inv_len = lax.rsqrt(dir_x * dir_x + dir_y * dir_y + dir_z * dir_z)
    dir_x = dir_x * inv_len
    dir_y = dir_y * inv_len
    dir_z = dir_z * inv_len
    sq_x = dir_x * dir_x
    sq_y = dir_y * dir_y
    sq_z = dir_z * dir_z
    harmonics = (
        harmonic_zero,
        -harmonic_one * dir_y,
        harmonic_one * dir_z,
        -harmonic_one * dir_x,
        harmonic_two[0] * dir_x * dir_y,
        harmonic_two[1] * dir_y * dir_z,
        harmonic_two[2] * (2.0 * sq_z - sq_x - sq_y),
        harmonic_two[3] * dir_x * dir_z,
        harmonic_two[4] * (sq_x - sq_y),
        harmonic_three[0] * dir_y * (3.0 * sq_x - sq_y),
        harmonic_three[1] * dir_x * dir_y * dir_z,
        harmonic_three[2] * dir_y * (4.0 * sq_z - sq_x - sq_y),
        harmonic_three[3] * dir_z * (2.0 * sq_z - 3.0 * sq_x - 3.0 * sq_y),
        harmonic_three[4] * dir_x * (4.0 * sq_z - sq_x - sq_y),
        harmonic_three[5] * dir_z * (sq_x - sq_y),
        harmonic_three[6] * dir_x * (sq_x - 3.0 * sq_y),
    )
    colors = []
    for channel in range(3):
        total = harmonics[0] * gauss_rows[11 + channel] + 0.5
        for basis in range(1, 16):
            total = total + harmonics[basis] * gauss_rows[11 + 3 * basis + channel]
        colors.append(total)
    return (pos_u, pos_v, coef_a, coef_b, coef_c, log_opacity, *colors)


def project_kernel(camera_ref, params_ref, table_ref):
    rows = params_ref.shape[1]
    camera_row = [camera_ref[entry] for entry in range(5)]
    center_x, center_y = camera_ref[5], camera_ref[6]

    def step(part, carry):
        at = pl.multiple_of(part * 16, 16)
        gauss_rows = [params_ref[channel, pl.ds(at, 16), :] for channel in range(params_ref.shape[0])]
        outputs = project(gauss_rows, camera_row, center_x, center_y)
        for field, values in enumerate(outputs):
            pieces = split_three(values)
            table_ref[pl.ds(field * rows + at, 16), :] = pieces[0]
            table_ref[pl.ds((fields + field) * rows + at, 16), :] = pieces[1]
            if field < 2:
                table_ref[pl.ds((2 * fields + field) * rows + at, 16), :] = pieces[2]
        return carry

    lax.fori_loop(0, rows // 16, step, 0)


def bucket_kernel(counts_ref, lists_ref, requests_ref, rank_ref, hits_ref, earlier_ref, *, owners, capacity, shift):
    tiles, slots = lists_ref.shape
    blocks = slots // 256
    upper = (
        lax.broadcasted_iota(i32, (256, 256), 0) < lax.broadcasted_iota(i32, (256, 256), 1)
    ).astype(f32).astype(bf16)
    owner_rows = lax.broadcasted_iota(i32, (owners, 256), 0)
    lane = lax.broadcasted_iota(i32, (1, 256), 1)
    for tile in range(tiles):
        for block in range(blocks):
            ids = lists_ref[tile : tile + 1, block * 256 : block * 256 + 256]
            owner = jnp.where(lane + block * 256 < counts_ref[tile], ids >> shift, -1)
            at = (tile * blocks + block) * owners
            hits_ref[at : at + owners, :] = jnp.where(owner_rows == owner, 1.0, 0.0).astype(bf16)
    earlier_ref[...] = jnp.dot(hits_ref[...], upper, preferred_element_type=f32)
    rank_rows = lax.broadcasted_iota(i32, (capacity, 256), 0)
    carry = jnp.zeros((owners, 1), f32)
    total = jnp.zeros((2 * owners, capacity), f32)
    for tile in range(tiles):
        for block in range(blocks):
            at = (tile * blocks + block) * owners
            hits = hits_ref[at : at + owners, :].astype(f32)
            earlier = earlier_ref[at : at + owners, :]
            rank = jnp.sum(hits * (earlier + carry), axis=0, keepdims=True)
            live = lane + block * 256 < counts_ref[tile]
            rank = jnp.where(live, rank, -1.0).astype(i32)
            rank_ref[tile : tile + 1, block * 256 : block * 256 + 256] = rank
            carry = carry + earlier[:, 255:256] + hits[:, 255:256]
            ids = lists_ref[tile : tile + 1, block * 256 : block * 256 + 256]
            local = (ids & ((1 << shift) - 1)) + 1
            coarse = (local >> 7).astype(f32)
            fine = (local & 127).astype(f32)
            placed = jnp.concatenate([hits * coarse, hits * fine], axis=0).astype(bf16)
            at_rank = jnp.where(rank_rows == rank, 1.0, 0.0).astype(bf16)
            total = total + lax.dot_general(placed, at_rank, nt_dims, preferred_element_type=f32)
    requests = (total[:owners] * 128.0 + total[owners:]).astype(i32) - 1
    for owner in range(owners):
        requests_ref[owner] = requests[owner : owner + 1]


def lookup_kernel(asked_ref, table_ref, found_ref, *, group):
    askers, _, capacity = asked_ref.shape
    rows = table_ref.shape[0] // (2 * fields + 2)
    width = group * capacity
    low_rows = lax.broadcasted_iota(i32, (256, width), 0)
    high_rows = lax.broadcasted_iota(i32, (rows, width), 0)

    def step(part, carry):
        asked = jnp.concatenate([asked_ref[group * part + k] for k in range(group)], axis=1)
        pick = jnp.where(low_rows == (asked & 255), 1.0, 0.0).astype(bf16)
        mask = high_rows == (asked >> 8)
        result = jnp.dot(table_ref[...], pick, preferred_element_type=f32)
        for field in range(fields):
            values = result[field * rows : (field + 1) * rows]
            values = values + result[(fields + field) * rows : (fields + field + 1) * rows]
            if field < 2:
                at = (2 * fields + field) * rows
                values = values + result[at : at + rows]
            found = jnp.sum(jnp.where(mask, values, 0.0), axis=0, keepdims=True)
            for k in range(group):
                found_ref[group * part + k, :, field * capacity : (field + 1) * capacity] = found[
                    :, k * capacity : (k + 1) * capacity
                ]
        return carry

    lax.fori_loop(0, askers // group, step, 0)


def collect_kernel(camera_ref, asked_ref, returned_ref, sums_ref, total_ref, *, rows, group):
    askers, _, capacity = asked_ref.shape
    views = sums_ref.shape[0]
    width = group * capacity
    low_rows = lax.broadcasted_iota(i32, (256, width), 0)
    high_rows = lax.broadcasted_iota(i32, (rows, width), 0)
    total_ref[...] = jnp.zeros_like(total_ref)

    def step(part, carry):
        asked = jnp.concatenate([asked_ref[group * part + k] for k in range(group)], axis=1)
        pick = jnp.where(low_rows == (asked & 255), 1.0, 0.0).astype(bf16)
        mask = high_rows == (asked >> 8)
        uppers = []
        lowers = []
        for field in range(fields):
            values = jnp.concatenate(
                [
                    returned_ref[group * part + k, :, field * capacity : (field + 1) * capacity]
                    for k in range(group)
                ],
                axis=1,
            )
            upper = values.astype(bf16).astype(f32)
            uppers.append(jnp.where(mask, upper, 0.0).astype(bf16))
            lowers.append(jnp.where(mask, values - upper, 0.0).astype(bf16))
        placed = jnp.concatenate(uppers + lowers, axis=0)
        total_ref[...] += lax.dot_general(placed, pick, nt_dims, preferred_element_type=f32)
        return carry

    lax.fori_loop(0, askers // group, step, 0)
    part_rows = rows // views
    for view in range(views):
        for field in range(fields):
            at = field * rows + view * part_rows
            sums_ref[view, field * part_rows : (field + 1) * part_rows, :] = (
                total_ref[at : at + part_rows, :]
                + total_ref[fields * rows + at : fields * rows + at + part_rows, :]
            )
        for entry in range(8):
            at = fields * part_rows + entry
            sums_ref[view, at : at + 1, :] = jnp.full((1, 256), camera_ref[entry], f32)


def pull_kernel(place_ref, sums_ref, params_ref, grads_ref):
    views = sums_ref.shape[0]
    part_rows = params_ref.shape[1]
    channels = params_ref.shape[0]
    gauss_rows = [params_ref[channel] for channel in range(channels)]
    totals = None
    for view in range(views):
        at = fields * part_rows
        camera_row = [
            jnp.broadcast_to(sums_ref[view, at + entry : at + entry + 1, :], (part_rows, 256))
            for entry in range(5)
        ]
        _, pull = jax.vjp(lambda rows_in: project(rows_in, camera_row, 0.0, 0.0), gauss_rows)
        (one,) = pull(
            tuple(
                sums_ref[view, field * part_rows : (field + 1) * part_rows, :]
                for field in range(fields)
            )
        )
        totals = one if totals is None else [x + y for x, y in zip(totals, one)]
    for channel in range(channels):
        for row in range(part_rows):
            grads_ref[channel : channel + 1, row * 256 : row * 256 + 256] = totals[channel][
                row : row + 1
            ]


def monomial(index, pix_x, pix_y):
    pix_x = pix_x.astype(f32) - 7.5
    pix_y = pix_y.astype(f32) - 7.5
    values = jnp.where(index == 0, 1.0, 0.0)
    values = jnp.where(index == 1, pix_x, values)
    values = jnp.where(index == 2, pix_y, values)
    values = jnp.where(index == 3, pix_x * pix_x, values)
    values = jnp.where(index == 4, pix_x * pix_y, values)
    return jnp.where(index == 5, pix_y * pix_y, values)


def render_kernel(
    counts_ref,
    place_ref,
    lists_ref,
    rank_ref,
    fetched_ref,
    d_image_ref,
    image_ref,
    outgoing_ref,
    fetch_ref,
    value_ref,
    blend_ref,
    ratio_ref,
    color_grad_ref,
    placed_ref,
    at_rank_ref,
    outgo_ref,
    *,
    shift,
):
    tiles, slots = lists_ref.shape
    owners, _, width = fetched_ref.shape
    capacity = width // fields
    blocks = slots // 256
    pixels = d_image_ref.shape[2]
    for field in range(fields):
        values = fetched_ref[:, 0, field * capacity : (field + 1) * capacity]
        pieces = split_three(values)
        fetch_ref[field * owners : (field + 1) * owners, :] = pieces[0]
        fetch_ref[(fields + field) * owners : (fields + field + 1) * owners, :] = pieces[1]
        if field < 2:
            at = (2 * fields + field) * owners
            fetch_ref[at : at + owners, :] = pieces[2]
    outgo_ref[...] = jnp.zeros_like(outgo_ref)
    row_index = lax.broadcasted_iota(i32, (256, 256), 0)
    lane_index = lax.broadcasted_iota(i32, (256, 256), 1)
    before = (row_index < lane_index).astype(f32).astype(bf16)
    after = (row_index > lane_index).astype(f32).astype(bf16)
    pixel_row = lax.broadcasted_iota(i32, (pixels, 24), 0)
    monomials = monomial(
        lax.broadcasted_iota(i32, (pixels, 24), 1) & 7, pixel_row & 15, pixel_row >> 4
    ).astype(bf16)
    pixel_lane = lax.broadcasted_iota(i32, (16, pixels), 1)
    moments_of = monomial(
        lax.broadcasted_iota(i32, (16, pixels), 0), pixel_lane & 15, pixel_lane >> 4
    ).astype(bf16)
    rank_rows = lax.broadcasted_iota(i32, (capacity, 256), 0)
    owner_rows = lax.broadcasted_iota(i32, (owners, 256), 0)
    lane = lax.broadcasted_iota(i32, (1, 256), 1)
    center_v = place_ref[0].astype(f32) * 16.0 + 8.0

    def one_tile(tile, carry):
        live_count = counts_ref[tile]
        live_blocks = (live_count + 255) // 256
        center_u = tile.astype(f32) * 16.0 + 8.0
        d_rows = d_image_ref[tile]
        d_pieces = split_two(d_rows)
        d_upper, d_lower = d_pieces[0].astype(f32), d_pieces[1].astype(f32)
        zeros = jnp.zeros((4, pixels), f32)
        d_stack = jnp.concatenate([d_upper, d_lower, d_upper, d_lower, zeros], axis=0)
        d_columns = jnp.transpose(d_stack).astype(bf16)
        d_left = jnp.concatenate(
            [d_upper, d_lower, jnp.zeros((10, pixels), f32)], axis=0
        ).astype(bf16)

        def owner_and_rank(block):
            at = pl.multiple_of(block * 256, 256)
            owner = lists_ref[pl.ds(tile, 1), pl.ds(at, 256)] >> shift
            return owner, rank_ref[pl.ds(tile, 1), pl.ds(at, 256)]

        def forward(block, carried):
            earlier, picture = carried
            at = pl.multiple_of(block * 256, 256)
            owner, rank = owner_and_rank(block)
            live = rank >= 0
            at_rank = jnp.where(rank_rows == rank, 1.0, 0.0).astype(bf16)
            at_rank_ref[:, pl.ds(at, 256)] = at_rank
            fetched = jnp.dot(fetch_ref[...], at_rank, preferred_element_type=f32)
            mask = owner_rows == owner
            found = []
            for field in range(fields):
                values = fetched[field * owners : (field + 1) * owners]
                low = (fields + field) * owners
                values = values + fetched[low : low + owners]
                if field < 2:
                    low = (2 * fields + field) * owners
                    values = values + fetched[low : low + owners]
                found.append(jnp.sum(jnp.where(mask, values, 0.0), axis=0, keepdims=True))
            pos_u = found[0] - center_u
            pos_v = found[1] - center_v
            coef_a, coef_b, coef_c, log_opacity = found[2:6]
            log_opacity = jnp.where(live, log_opacity, -1.0e4)
            value_ref[0:1, pl.ds(at, 256)] = pos_u
            value_ref[1:2, pl.ds(at, 256)] = pos_v
            for field in range(2, 5):
                value_ref[field : field + 1, pl.ds(at, 256)] = found[field]
            slope_u = coef_a * pos_u * 2.0 + coef_b * pos_v
            slope_v = coef_c * pos_v * 2.0 + coef_b * pos_u
            constant = log_opacity + 0.5 * (slope_u * pos_u + slope_v * pos_v)
            blank = jnp.zeros((2, 256), f32)
            polynomial = jnp.concatenate(
                [constant, -slope_u, -slope_v, coef_a, coef_b, coef_c, blank], axis=0
            )
            pieces = [piece.astype(f32) for piece in split_three(polynomial)]
            exponent = jnp.dot(
                monomials,
                jnp.concatenate(pieces, axis=0).astype(bf16),
                preferred_element_type=f32,
            )
            alpha = jnp.exp2(exponent)
            keep = 1.0 - alpha
            log_keep = jnp.log2(keep)
            upper, lower = split_two(log_keep)
            within = jnp.dot(upper, before, preferred_element_type=f32) + jnp.dot(
                lower, before, preferred_element_type=f32
            )
            weight = jnp.exp2(within + earlier) * alpha
            earlier = earlier + within[:, 255:256] + log_keep[:, 255:256]
            colors = jnp.concatenate(found[6:9], axis=0)
            color_pieces = [piece.astype(f32) for piece in split_two(colors)]
            blank = jnp.zeros((4, 256), f32)
            color_rows = jnp.concatenate(
                [
                    color_pieces[0],
                    color_pieces[0],
                    color_pieces[1],
                    color_pieces[1],
                    blank,
                ],
                axis=0,
            ).astype(bf16)
            color_left = jnp.concatenate(
                [color_pieces[0], color_pieces[1], jnp.zeros((10, 256), f32)], axis=0
            ).astype(bf16)
            pull = jnp.dot(d_columns, color_rows, preferred_element_type=f32)
            blend_ref[:, pl.ds(at, 256)] = weight * pull
            ratio_ref[:, pl.ds(at, 256)] = alpha / keep
            upper, lower = split_two(weight)
            one = jnp.dot(d_left, upper, preferred_element_type=f32)
            two = jnp.dot(d_left, lower, preferred_element_type=f32)
            color_grad_ref[0:3, pl.ds(at, 256)] = one[0:3] + one[3:6] + two[0:3]
            one = lax.dot_general(color_left, upper, nt_dims, preferred_element_type=f32)
            two = lax.dot_general(color_left, lower, nt_dims, preferred_element_type=f32)
            picture = picture + one[0:3] + one[3:6] + two[0:3]
            return earlier, picture

        _, picture = lax.fori_loop(
            0,
            live_blocks,
            forward,
            (jnp.zeros((pixels, 1), f32), jnp.zeros((3, pixels), f32)),
        )
        image_ref[tile] = picture

        def backward(step, later):
            block = live_blocks - 1 - step
            at = pl.multiple_of(block * 256, 256)
            owner, rank = owner_and_rank(block)
            blend = blend_ref[:, pl.ds(at, 256)]
            upper, lower = split_two(blend)
            within = jnp.dot(upper, after, preferred_element_type=f32) + jnp.dot(
                lower, after, preferred_element_type=f32
            )
            gradient = blend - (within + later) * ratio_ref[:, pl.ds(at, 256)]
            later = later + within[:, 0:1] + blend[:, 0:1]
            pieces = split_three(gradient)
            moments = (
                jnp.dot(moments_of, pieces[0], preferred_element_type=f32)
                + jnp.dot(moments_of, pieces[1], preferred_element_type=f32)
                + jnp.dot(moments_of, pieces[2], preferred_element_type=f32)
            ) * ln_2
            plain, first_x, first_y = moments[0:1], moments[1:2], moments[2:3]
            pos_u = value_ref[0:1, pl.ds(at, 256)]
            pos_v = value_ref[1:2, pl.ds(at, 256)]
            coef_a = value_ref[2:3, pl.ds(at, 256)]
            coef_b = value_ref[3:4, pl.ds(at, 256)]
            coef_c = value_ref[4:5, pl.ds(at, 256)]
            from_u = first_x - pos_u * plain
            from_v = first_y - pos_v * plain
            outputs = [
                -2.0 * coef_a * from_u - coef_b * from_v,
                -2.0 * coef_c * from_v - coef_b * from_u,
                moments[3:4] - pos_u * (first_x + from_u),
                moments[4:5] - pos_v * first_x - pos_u * from_v,
                moments[5:6] - pos_v * (first_y + from_v),
                plain,
            ] + [color_grad_ref[k : k + 1, pl.ds(at, 256)] for k in range(3)]
            mask = owner_rows == jnp.where(rank >= 0, owner, -1)
            for field, values in enumerate(outputs):
                upper = values.astype(bf16).astype(f32)
                row = field * owners
                placed_ref[row : row + owners, pl.ds(at, 256)] = jnp.where(mask, upper, 0.0).astype(bf16)
                row = (fields + field) * owners
                placed_ref[row : row + owners, pl.ds(at, 256)] = jnp.where(
                    mask, values - upper, 0.0
                ).astype(bf16)
            return later

        lax.fori_loop(0, live_blocks, backward, jnp.zeros((pixels, 1), f32))

        def send(block, carried):
            at = pl.multiple_of(block * 256, 256)
            outgo_ref[...] += lax.dot_general(
                placed_ref[:, pl.ds(at, 256)],
                at_rank_ref[:, pl.ds(at, 256)],
                nt_dims,
                preferred_element_type=f32,
            )
            return carried

        return lax.fori_loop(0, live_blocks, send, carry)

    lax.fori_loop(0, tiles, one_tile, 0)
    for owner in range(owners):
        for field in range(fields):
            row = field * owners + owner
            low = fields * owners + row
            outgoing_ref[owner, :, field * capacity : (field + 1) * capacity] = (
                outgo_ref[row : row + 1, :] + outgo_ref[low : low + 1, :]
            )


def body(params, camera, tile_lists, tile_counts, d_image):
    owners = lax.axis_size("tiles")
    views = lax.axis_size("views")
    channels, shard_size = params.shape
    shift = shard_size.bit_length() - 1
    tiles, slots = tile_lists.shape[1:]
    pixels = d_image.shape[3]
    capacity = 3 * tiles * slots // (2 * owners)
    rows = shard_size // 256
    part_rows = rows // views
    center = jnp.array([tiles * 8.0, owners * 8.0, 0.0], f32)
    camera_row = jnp.concatenate([jnp.cos(camera[0, :1]), jnp.sin(camera[0, :1]), camera[0, 1:4], center])
    counts = tile_counts[0]
    lists = tile_lists[0]
    tile_row = lax.axis_index("tiles").astype(i32).reshape(1)
    view_here = lax.axis_index("views").astype(i32).reshape(1)
    smem = pl.BlockSpec(memory_space=pltpu.SMEM)
    vmem = pl.BlockSpec(memory_space=pltpu.VMEM)
    settings = pltpu.CompilerParams(vmem_limit_bytes=vmem_bytes)

    requests, rank = pl.pallas_call(
        functools.partial(bucket_kernel, owners=owners, capacity=capacity, shift=shift),
        out_shape=(
            jax.ShapeDtypeStruct((owners, 1, capacity), i32),
            jax.ShapeDtypeStruct((tiles, slots), i32),
        ),
        in_specs=[smem, vmem],
        out_specs=(vmem, vmem),
        scratch_shapes=[
            pltpu.VMEM((tiles * slots // 256 * owners, 256), bf16),
            pltpu.VMEM((tiles * slots // 256 * owners, 256), f32),
        ],
        compiler_params=settings,
        name="bucket",
    )(counts, lists)
    asked = lax.all_to_all(requests, "tiles", split_axis=0, concat_axis=0, tiled=True)
    dense_params = params.reshape(channels, rows, 256)
    table = pl.pallas_call(
        project_kernel,
        out_shape=jax.ShapeDtypeStruct(((2 * fields + 2) * rows, 256), bf16),
        in_specs=[smem, vmem],
        out_specs=vmem,
        compiler_params=settings,
        name="project",
    )(camera_row, dense_params)
    found = pl.pallas_call(
        functools.partial(lookup_kernel, group=4),
        out_shape=jax.ShapeDtypeStruct((owners, 1, fields * capacity), f32),
        in_specs=[vmem, vmem],
        out_specs=vmem,
        compiler_params=settings,
        name="lookup",
    )(asked, table)
    fetched = lax.all_to_all(found, "tiles", split_axis=0, concat_axis=0, tiled=True)
    picture, outgoing = pl.pallas_call(
        functools.partial(render_kernel, shift=shift),
        out_shape=(
            jax.ShapeDtypeStruct((tiles, 3, pixels), f32),
            jax.ShapeDtypeStruct((owners, 1, fields * capacity), f32),
        ),
        in_specs=[smem, smem, vmem, vmem, vmem, vmem],
        out_specs=(vmem, vmem),
        scratch_shapes=[
            pltpu.VMEM(((2 * fields + 2) * owners, capacity), bf16),
            pltpu.VMEM((8, slots), f32),
            pltpu.VMEM((pixels, slots), f32),
            pltpu.VMEM((pixels, slots), f32),
            pltpu.VMEM((8, slots), f32),
            pltpu.VMEM((2 * fields * owners, slots), bf16),
            pltpu.VMEM((capacity, slots), bf16),
            pltpu.VMEM((2 * fields * owners, capacity), f32),
        ],
        compiler_params=settings,
        name="render",
    )(counts, tile_row, lists, rank, fetched, d_image[0])
    returned = lax.all_to_all(outgoing, "tiles", split_axis=0, concat_axis=0, tiled=True)
    sums = pl.pallas_call(
        functools.partial(collect_kernel, rows=rows, group=2),
        out_shape=jax.ShapeDtypeStruct((views, fields * part_rows + 8, 256), f32),
        in_specs=[smem, vmem, vmem],
        out_specs=vmem,
        scratch_shapes=[pltpu.VMEM((2 * fields * rows, 256), f32)],
        compiler_params=settings,
        name="collect",
    )(camera_row, asked, returned)
    all_sums = lax.all_to_all(sums, "views", split_axis=0, concat_axis=0, tiled=True)
    grads = pl.pallas_call(
        pull_kernel,
        out_shape=jax.ShapeDtypeStruct((channels, part_rows * 256), f32),
        grid_spec=pltpu.PrefetchScalarGridSpec(
            num_scalar_prefetch=1,
            grid=(1,),
            in_specs=[
                pl.BlockSpec((views, fields * part_rows + 8, 256), lambda step, place: (0, 0, 0)),
                pl.BlockSpec((channels, part_rows, 256), lambda step, place: (0, place[0], 0)),
            ],
            out_specs=pl.BlockSpec((channels, part_rows * 256), lambda step, place: (0, 0)),
        ),
        compiler_params=settings,
        name="pull",
    )(view_here, all_sums, dense_params)
    return picture[None], grads


def solution(mesh):
    placed = (
        P(None, "tiles"),
        P("views", None),
        P("views", "tiles", None),
        P("views", "tiles"),
        P("views", "tiles", None, None),
    )
    return jax.shard_map(
        body,
        mesh=mesh,
        in_specs=placed,
        out_specs=(P("views", "tiles", None, None), P(None, ("tiles", "views"))),
        check_vma=False,
    )
```

```python
import functools
import math

import jax
import jax.numpy as jnp
from jax import lax
from jax.experimental import pallas as pl
from jax.experimental.pallas import tpu as pltpu
from jax.sharding import PartitionSpec as P

focal_px = 600.0
lowpass = 0.3
harmonic_zero = 0.28209479177387814
harmonic_one = 0.4886025119029199
harmonic_two = (
    1.0925484305920792,
    -1.0925484305920792,
    0.31539156525252005,
    -1.0925484305920792,
    0.5462742152960396,
)
harmonic_three = (
    -0.5900435899266435,
    2.890611442640554,
    -0.4570457994644658,
    0.3731763325901154,
    -0.4570457994644658,
    1.445305721320277,
    -0.5900435899266435,
)
bf16 = jnp.bfloat16
f32 = jnp.float32
i32 = jnp.int32
log2_e = 1.0 / math.log(2.0)
ln_2 = math.log(2.0)
nt_dims = (((1,), (1,)), ((), ()))
vmem_bytes = 56 * 1024 * 1024
fields = 9


def split_two(values):
    upper = values.astype(bf16)
    lower = (values - upper.astype(f32)).astype(bf16)
    return upper, lower


def split_three(values):
    upper = values.astype(bf16)
    rest = values - upper.astype(f32)
    middle = rest.astype(bf16)
    lower = (rest - middle.astype(f32)).astype(bf16)
    return upper, middle, lower


def project(gauss_rows, camera_row, center_x, center_y):
    cosine, sine_val, shift_x, shift_y, shift_z = camera_row
    cam_x = cosine * gauss_rows[0] + sine_val * gauss_rows[2] + shift_x
    cam_y = gauss_rows[1] + shift_y
    cam_z = cosine * gauss_rows[2] - sine_val * gauss_rows[0] + shift_z
    inverse_z = 1.0 / cam_z
    jac_a = focal_px * inverse_z
    pos_u = jac_a * cam_x + center_x
    pos_v = jac_a * cam_y + center_y
    jac_b = -jac_a * cam_x * inverse_z
    jac_c = -jac_a * cam_y * inverse_z
    first_row = (jac_a * cosine - jac_b * sine_val, jac_a * sine_val + jac_b * cosine)
    second_row = (-jac_c * sine_val, jac_a, jac_c * cosine)
    quaternion = gauss_rows[6:10]
    inv_norm = lax.rsqrt(
        quaternion[0] * quaternion[0]
        + quaternion[1] * quaternion[1]
        + quaternion[2] * quaternion[2]
        + quaternion[3] * quaternion[3]
    )
    quat_w, quat_x, quat_y, quat_z = (entry * inv_norm for entry in quaternion)
    rotation = (
        (
            1.0 - 2.0 * (quat_y * quat_y + quat_z * quat_z),
            2.0 * (quat_x * quat_y - quat_w * quat_z),
            2.0 * (quat_x * quat_z + quat_w * quat_y),
        ),
        (
            2.0 * (quat_x * quat_y + quat_w * quat_z),
            1.0 - 2.0 * (quat_x * quat_x + quat_z * quat_z),
            2.0 * (quat_y * quat_z - quat_w * quat_x),
        ),
        (
            2.0 * (quat_x * quat_z - quat_w * quat_y),
            2.0 * (quat_y * quat_z + quat_w * quat_x),
            1.0 - 2.0 * (quat_x * quat_x + quat_y * quat_y),
        ),
    )
    scales = [jnp.exp(entry) for entry in gauss_rows[3:6]]
    upper_a = [
        (first_row[0] * rotation[0][entry] + first_row[1] * rotation[2][entry]) * scales[entry]
        for entry in range(3)
    ]
    lower_a = [
        (
            second_row[0] * rotation[0][entry]
            + second_row[1] * rotation[1][entry]
            + second_row[2] * rotation[2][entry]
        )
        * scales[entry]
        for entry in range(3)
    ]
    cov_a = upper_a[0] * upper_a[0] + upper_a[1] * upper_a[1] + upper_a[2] * upper_a[2] + lowpass
    cov_b = upper_a[0] * lower_a[0] + upper_a[1] * lower_a[1] + upper_a[2] * lower_a[2]
    cov_c = lower_a[0] * lower_a[0] + lower_a[1] * lower_a[1] + lower_a[2] * lower_a[2] + lowpass
    inv_det = 1.0 / (cov_a * cov_c - cov_b * cov_b)
    coef_a = (-0.5 * log2_e) * cov_c * inv_det
    coef_b = log2_e * cov_b * inv_det
    coef_c = (-0.5 * log2_e) * cov_a * inv_det
    log_opacity = -log2_e * jnp.log(1.0 + jnp.exp(-gauss_rows[10]))
    dir_x = cosine * cam_x - sine_val * cam_z
    dir_y = cam_y
    dir_z = sine_val * cam_x + cosine * cam_z
    inv_len = lax.rsqrt(dir_x * dir_x + dir_y * dir_y + dir_z * dir_z)
    dir_x = dir_x * inv_len
    dir_y = dir_y * inv_len
    dir_z = dir_z * inv_len
    sq_x = dir_x * dir_x
    sq_y = dir_y * dir_y
    sq_z = dir_z * dir_z
    harmonics = (
        harmonic_zero,
        -harmonic_one * dir_y,
        harmonic_one * dir_z,
        -harmonic_one * dir_x,
        harmonic_two[0] * dir_x * dir_y,
        harmonic_two[1] * dir_y * dir_z,
        harmonic_two[2] * (2.0 * sq_z - sq_x - sq_y),
        harmonic_two[3] * dir_x * dir_z,
        harmonic_two[4] * (sq_x - sq_y),
        harmonic_three[0] * dir_y * (3.0 * sq_x - sq_y),
        harmonic_three[1] * dir_x * dir_y * dir_z,
        harmonic_three[2] * dir_y * (4.0 * sq_z - sq_x - sq_y),
        harmonic_three[3] * dir_z * (2.0 * sq_z - 3.0 * sq_x - 3.0 * sq_y),
        harmonic_three[4] * dir_x * (4.0 * sq_z - sq_x - sq_y),
        harmonic_three[5] * dir_z * (sq_x - sq_y),
        harmonic_three[6] * dir_x * (sq_x - 3.0 * sq_y),
    )
    colors = []
    for channel in range(3):
        total = harmonics[0] * gauss_rows[11 + channel] + 0.5
        for basis in range(1, 16):
            total = total + harmonics[basis] * gauss_rows[11 + 3 * basis + channel]
        colors.append(total)
    return (pos_u, pos_v, coef_a, coef_b, coef_c, log_opacity, *colors)


def project_kernel(camera_ref, params_ref, table_ref):
    rows = params_ref.shape[1]
    camera_row = [camera_ref[entry] for entry in range(5)]
    center_x, center_y = camera_ref[5], camera_ref[6]

    def step(part, carry):
        at = pl.multiple_of(part * 16, 16)
        gauss_rows = [params_ref[channel, pl.ds(at, 16), :] for channel in range(params_ref.shape[0])]
        outputs = project(gauss_rows, camera_row, center_x, center_y)
        for field, values in enumerate(outputs):
            pieces = split_three(values)
            table_ref[pl.ds(field * rows + at, 16), :] = pieces[0]
            table_ref[pl.ds((fields + field) * rows + at, 16), :] = pieces[1]
            if field < 2:
                table_ref[pl.ds((2 * fields + field) * rows + at, 16), :] = pieces[2]
        return carry

    lax.fori_loop(0, rows // 16, step, 0)


def bucket_kernel(counts_ref, lists_ref, requests_ref, rank_ref, hits_ref, earlier_ref, *, owners, capacity, shift):
    tiles, slots = lists_ref.shape
    blocks = slots // 256
    upper = (
        lax.broadcasted_iota(i32, (256, 256), 0) < lax.broadcasted_iota(i32, (256, 256), 1)
    ).astype(f32).astype(bf16)
    owner_rows = lax.broadcasted_iota(i32, (owners, 256), 0)
    lane = lax.broadcasted_iota(i32, (1, 256), 1)
    for tile in range(tiles):
        for block in range(blocks):
            ids = lists_ref[tile : tile + 1, block * 256 : block * 256 + 256]
            owner = jnp.where(lane + block * 256 < counts_ref[tile], ids >> shift, -1)
            at = (tile * blocks + block) * owners
            hits_ref[at : at + owners, :] = jnp.where(owner_rows == owner, 1.0, 0.0).astype(bf16)
    earlier_ref[...] = jnp.dot(hits_ref[...], upper, preferred_element_type=f32)
    rank_rows = lax.broadcasted_iota(i32, (capacity, 256), 0)
    carry = jnp.zeros((owners, 1), f32)
    total = jnp.zeros((2 * owners, capacity), f32)
    for tile in range(tiles):
        for block in range(blocks):
            at = (tile * blocks + block) * owners
            hits = hits_ref[at : at + owners, :].astype(f32)
            earlier = earlier_ref[at : at + owners, :]
            rank = jnp.sum(hits * (earlier + carry), axis=0, keepdims=True)
            live = lane + block * 256 < counts_ref[tile]
            rank = jnp.where(live, rank, -1.0).astype(i32)
            rank_ref[tile : tile + 1, block * 256 : block * 256 + 256] = rank
            carry = carry + earlier[:, 255:256] + hits[:, 255:256]
            ids = lists_ref[tile : tile + 1, block * 256 : block * 256 + 256]
            local = (ids & ((1 << shift) - 1)) + 1
            coarse = (local >> 7).astype(f32)
            fine = (local & 127).astype(f32)
            placed = jnp.concatenate([hits * coarse, hits * fine], axis=0).astype(bf16)
            at_rank = jnp.where(rank_rows == rank, 1.0, 0.0).astype(bf16)
            total = total + lax.dot_general(placed, at_rank, nt_dims, preferred_element_type=f32)
    requests = (total[:owners] * 128.0 + total[owners:]).astype(i32) - 1
    for owner in range(owners):
        requests_ref[owner] = requests[owner : owner + 1]


def lookup_kernel(asked_ref, table_ref, found_ref, *, group):
    askers, _, capacity = asked_ref.shape
    rows = table_ref.shape[0] // (2 * fields + 2)
    width = group * capacity
    low_rows = lax.broadcasted_iota(i32, (256, width), 0)
    high_rows = lax.broadcasted_iota(i32, (rows, width), 0)

    def step(part, carry):
        asked = jnp.concatenate([asked_ref[group * part + k] for k in range(group)], axis=1)
        pick = jnp.where(low_rows == (asked & 255), 1.0, 0.0).astype(bf16)
        mask = high_rows == (asked >> 8)
        result = jnp.dot(table_ref[...], pick, preferred_element_type=f32)
        for field in range(fields):
            values = result[field * rows : (field + 1) * rows]
            values = values + result[(fields + field) * rows : (fields + field + 1) * rows]
            if field < 2:
                at = (2 * fields + field) * rows
                values = values + result[at : at + rows]
            found = jnp.sum(jnp.where(mask, values, 0.0), axis=0, keepdims=True)
            for k in range(group):
                found_ref[group * part + k, :, field * capacity : (field + 1) * capacity] = found[
                    :, k * capacity : (k + 1) * capacity
                ]
        return carry

    lax.fori_loop(0, askers // group, step, 0)


def collect_kernel(camera_ref, asked_ref, returned_ref, sums_ref, total_ref, *, rows, group):
    askers, _, capacity = asked_ref.shape
    views = sums_ref.shape[0]
    width = group * capacity
    low_rows = lax.broadcasted_iota(i32, (256, width), 0)
    high_rows = lax.broadcasted_iota(i32, (rows, width), 0)
    total_ref[...] = jnp.zeros_like(total_ref)

    def step(part, carry):
        asked = jnp.concatenate([asked_ref[group * part + k] for k in range(group)], axis=1)
        pick = jnp.where(low_rows == (asked & 255), 1.0, 0.0).astype(bf16)
        mask = high_rows == (asked >> 8)
        uppers = []
        lowers = []
        for field in range(fields):
            values = jnp.concatenate(
                [
                    returned_ref[group * part + k, :, field * capacity : (field + 1) * capacity]
                    for k in range(group)
                ],
                axis=1,
            )
            upper = values.astype(bf16).astype(f32)
            uppers.append(jnp.where(mask, upper, 0.0).astype(bf16))
            lowers.append(jnp.where(mask, values - upper, 0.0).astype(bf16))
        placed = jnp.concatenate(uppers + lowers, axis=0)
        total_ref[...] += lax.dot_general(placed, pick, nt_dims, preferred_element_type=f32)
        return carry

    lax.fori_loop(0, askers // group, step, 0)
    part_rows = rows // views
    for view in range(views):
        for field in range(fields):
            at = field * rows + view * part_rows
            sums_ref[view, field * part_rows : (field + 1) * part_rows, :] = (
                total_ref[at : at + part_rows, :]
                + total_ref[fields * rows + at : fields * rows + at + part_rows, :]
            )
        for entry in range(8):
            at = fields * part_rows + entry
            sums_ref[view, at : at + 1, :] = jnp.full((1, 256), camera_ref[entry], f32)


def pull_kernel(place_ref, sums_ref, params_ref, grads_ref):
    views = sums_ref.shape[0]
    part_rows = params_ref.shape[1]
    channels = params_ref.shape[0]
    gauss_rows = [params_ref[channel] for channel in range(channels)]
    totals = None
    for view in range(views):
        at = fields * part_rows
        camera_row = [
            jnp.broadcast_to(sums_ref[view, at + entry : at + entry + 1, :], (part_rows, 256))
            for entry in range(5)
        ]
        _, pull = jax.vjp(lambda rows_in: project(rows_in, camera_row, 0.0, 0.0), gauss_rows)
        (one,) = pull(
            tuple(
                sums_ref[view, field * part_rows : (field + 1) * part_rows, :]
                for field in range(fields)
            )
        )
        totals = one if totals is None else [x + y for x, y in zip(totals, one)]
    for channel in range(channels):
        for row in range(part_rows):
            grads_ref[channel : channel + 1, row * 256 : row * 256 + 256] = totals[channel][
                row : row + 1
            ]


def monomial(index, pix_x, pix_y):
    pix_x = pix_x.astype(f32) - 7.5
    pix_y = pix_y.astype(f32) - 7.5
    values = jnp.where(index == 0, 1.0, 0.0)
    values = jnp.where(index == 1, pix_x, values)
    values = jnp.where(index == 2, pix_y, values)
    values = jnp.where(index == 3, pix_x * pix_x, values)
    values = jnp.where(index == 4, pix_x * pix_y, values)
    return jnp.where(index == 5, pix_y * pix_y, values)


def render_kernel(
    counts_ref,
    place_ref,
    lists_ref,
    rank_ref,
    fetched_ref,
    d_image_ref,
    image_ref,
    outgoing_ref,
    item_ref,
    rows_ref,
    fetch_ref,
    value_ref,
    polynomial_ref,
    color_rows_ref,
    color_left_ref,
    d_columns_ref,
    d_left_ref,
    earlier_ref,
    later_ref,
    picture_ref,
    blend_ref,
    ratio_ref,
    color_grad_ref,
    placed_ref,
    at_rank_ref,
    outgo_ref,
    *,
    shift,
):
    tiles, slots = lists_ref.shape
    owners, _, width = fetched_ref.shape
    capacity = width // fields
    spare = tiles * slots // 256
    pixels = d_image_ref.shape[2]

    def list_tile(tile, base):
        live_blocks = (counts_ref[tile] + 255) // 256

        def list_block(block, carry):
            item_ref[0, base + block] = tile
            item_ref[1, base + block] = block
            item_ref[2, base + block] = base + live_blocks - 1 - block
            return carry

        lax.fori_loop(0, live_blocks, list_block, 0)
        return base + live_blocks

    items = lax.fori_loop(0, tiles, list_tile, 0)
    for owner in range(owners):
        for field in range(fields):
            row = field * owners + owner
            rows_ref[row : row + 1, :] = fetched_ref[owner, :, field * capacity : (field + 1) * capacity]
    center_v = place_ref[0].astype(f32) * 16.0 + 8.0
    for field in range(fields):
        values = rows_ref[field * owners : (field + 1) * owners, :]
        if field == 1:
            values = values - center_v
        pieces = split_three(values)
        fetch_ref[field * owners : (field + 1) * owners, :] = pieces[0]
        fetch_ref[(fields + field) * owners : (fields + field + 1) * owners, :] = pieces[1]
        if field < 2:
            at = (2 * fields + field) * owners
            fetch_ref[at : at + owners, :] = pieces[2]
    for tile in range(tiles):
        d_rows = d_image_ref[tile]
        d_upper, d_lower = [piece.astype(f32) for piece in split_two(d_rows)]
        d_stack = jnp.concatenate([d_upper, d_lower, d_upper, d_lower, jnp.zeros((4, pixels), f32)], axis=0)
        d_columns_ref[tile] = jnp.transpose(d_stack).astype(bf16)
        d_left_ref[tile] = jnp.concatenate([d_upper, d_lower, jnp.zeros((10, pixels), f32)], axis=0).astype(bf16)
    outgo_ref[...] = jnp.zeros_like(outgo_ref)
    placed_ref[spare] = jnp.zeros(placed_ref.shape[1:], bf16)
    at_rank_ref[spare] = jnp.zeros(at_rank_ref.shape[1:], bf16)
    row_index = lax.broadcasted_iota(i32, (256, 256), 0)
    lane_index = lax.broadcasted_iota(i32, (256, 256), 1)
    before = (row_index < lane_index).astype(f32).astype(bf16)
    after = (row_index > lane_index).astype(f32).astype(bf16)
    pixel_row = lax.broadcasted_iota(i32, (pixels, 24), 0)
    monomials = monomial(
        lax.broadcasted_iota(i32, (pixels, 24), 1) & 7, pixel_row & 15, pixel_row >> 4
    ).astype(bf16)
    pixel_lane = lax.broadcasted_iota(i32, (16, pixels), 1)
    moments_of = monomial(
        lax.broadcasted_iota(i32, (16, pixels), 0), pixel_lane & 15, pixel_lane >> 4
    ).astype(bf16)
    rank_rows = lax.broadcasted_iota(i32, (capacity, 256), 0)
    owner_rows = lax.broadcasted_iota(i32, (owners, 256), 0)

    def owner_and_rank(item):
        tile = item_ref[0, item]
        at = pl.multiple_of(item_ref[1, item] * 256, 256)
        owner = lists_ref[pl.ds(tile, 1), pl.ds(at, 256)] >> shift
        rank = rank_ref[pl.ds(tile, 1), pl.ds(at, 256)]
        return owner, rank

    def fetch(item):
        owner, rank = owner_and_rank(item)
        tile = item_ref[0, item]
        at_rank = jnp.where(rank_rows == rank, 1.0, 0.0).astype(bf16)
        at_rank_ref[item] = at_rank
        fetched = jnp.dot(fetch_ref[...], at_rank, preferred_element_type=f32)
        mask = owner_rows == owner
        found = []
        for field in range(fields):
            values = fetched[field * owners : (field + 1) * owners]
            low = (fields + field) * owners
            values = values + fetched[low : low + owners]
            if field < 2:
                low = (2 * fields + field) * owners
                values = values + fetched[low : low + owners]
            found.append(jnp.sum(jnp.where(mask, values, 0.0), axis=0, keepdims=True))
        pos_u = found[0] - (tile.astype(f32) * 16.0 + 8.0)
        pos_v = found[1]
        coef_a, coef_b, coef_c, log_opacity = found[2:6]
        log_opacity = jnp.where(rank >= 0, log_opacity, -1.0e4)
        slope_u = coef_a * pos_u * 2.0 + coef_b * pos_v
        slope_v = coef_c * pos_v * 2.0 + coef_b * pos_u
        constant = log_opacity + 0.5 * (slope_u * pos_u + slope_v * pos_v)
        blank = jnp.zeros((3, 256), f32)
        value_ref[item] = jnp.concatenate([pos_u, pos_v, coef_a, coef_b, coef_c, blank], axis=0)
        polynomial = jnp.concatenate(
            [constant, -slope_u, -slope_v, coef_a, coef_b, coef_c, blank[0:2]], axis=0
        )
        pieces = [piece.astype(f32) for piece in split_three(polynomial)]
        polynomial_ref[item] = jnp.concatenate(pieces, axis=0).astype(bf16)
        upper, lower = [piece.astype(f32) for piece in split_two(jnp.concatenate(found[6:9], axis=0))]
        color_rows_ref[item] = jnp.concatenate(
            [upper, upper, lower, lower, jnp.zeros((4, 256), f32)], axis=0
        ).astype(bf16)
        color_left_ref[item] = jnp.concatenate(
            [upper, lower, jnp.zeros((10, 256), f32)], axis=0
        ).astype(bf16)

    def forward(item):
        live = item >= 0
        at = jnp.where(live, item, spare)
        item = jnp.maximum(item, 0)
        tile = item_ref[0, item]
        first = item_ref[1, item] == 0
        exponent = jnp.dot(monomials, polynomial_ref[at], preferred_element_type=f32)
        earlier = jnp.where(first, 0.0, earlier_ref[...])
        earlier = jnp.concatenate([earlier, earlier], axis=1)
        alpha = jnp.exp2(exponent)
        keep = 1.0 - alpha
        log_keep = jnp.log2(keep)
        upper, lower = split_two(log_keep)
        within = jnp.dot(upper, before, preferred_element_type=f32) + jnp.dot(
            lower, before, preferred_element_type=f32
        )
        within = within + earlier
        weight = jnp.exp2(within) * alpha
        earlier_ref[...] = jnp.broadcast_to(within[:, 255:256] + log_keep[:, 255:256], (pixels, 128))
        pull = jnp.dot(d_columns_ref[tile], color_rows_ref[at], preferred_element_type=f32)
        blend_ref[at] = weight * pull
        ratio_ref[at] = alpha / keep
        upper, lower = split_two(weight)
        d_left = d_left_ref[tile]
        one = jnp.dot(d_left, upper, preferred_element_type=f32)
        two = jnp.dot(d_left, lower, preferred_element_type=f32)
        color_grad_ref[at, 0:3] = one[0:3] + one[3:6] + two[0:3]
        color_left = color_left_ref[at]
        one = lax.dot_general(color_left, upper, nt_dims, preferred_element_type=f32)
        two = lax.dot_general(color_left, lower, nt_dims, preferred_element_type=f32)
        picture = one[0:3] + one[3:6] + two[0:3]
        at_tile = jnp.where(live, tile, tiles)
        picture_ref[at_tile, 0:3] = jnp.where(first, 0.0, picture_ref[at_tile, 0:3]) + picture

    def backward(step):
        step = jnp.minimum(step, items)
        live = step < items
        at = jnp.where(live, item_ref[2, jnp.minimum(step, items - 1)], spare)
        item = jnp.where(live, at, 0)
        first = item_ref[1, jnp.minimum(step, items - 1)] == 0
        owner, rank = owner_and_rank(item)
        blend = blend_ref[at]
        upper, lower = split_two(blend)
        within = jnp.dot(upper, after, preferred_element_type=f32) + jnp.dot(
            lower, after, preferred_element_type=f32
        )
        later = jnp.where(first, 0.0, later_ref[...])
        within = within + jnp.concatenate([later, later], axis=1)
        later_ref[...] = jnp.broadcast_to(within[:, 0:1] + blend[:, 0:1], (pixels, 128))
        gradient = blend - within * ratio_ref[at]
        pieces = split_two(gradient)
        moments = (
            jnp.dot(moments_of, pieces[0], preferred_element_type=f32)
            + jnp.dot(moments_of, pieces[1], preferred_element_type=f32)
        ) * ln_2
        plain, first_x, first_y = moments[0:1], moments[1:2], moments[2:3]
        pos_u, pos_v, coef_a, coef_b, coef_c = (value_ref[at, k : k + 1] for k in range(5))
        from_u = first_x - pos_u * plain
        from_v = first_y - pos_v * plain
        outputs = [
            -2.0 * coef_a * from_u - coef_b * from_v,
            -2.0 * coef_c * from_v - coef_b * from_u,
            moments[3:4] - pos_u * (first_x + from_u),
            moments[4:5] - pos_v * first_x - pos_u * from_v,
            moments[5:6] - pos_v * (first_y + from_v),
            plain,
        ] + [color_grad_ref[at, k : k + 1] for k in range(3)]
        mask = owner_rows == jnp.where(rank >= 0, owner, -1)
        for field, values in enumerate(outputs):
            upper = values.astype(bf16).astype(f32)
            row = field * owners
            placed_ref[at, row : row + owners, :] = jnp.where(mask, upper, 0.0).astype(bf16)
            row = (fields + field) * owners
            placed_ref[at, row : row + owners, :] = jnp.where(mask, values - upper, 0.0).astype(bf16)

    def send(item):
        at = jnp.where(item < 0, spare, item)
        outgo_ref[...] += lax.dot_general(
            placed_ref[at], at_rank_ref[at], nt_dims, preferred_element_type=f32
        )

    def send_step(step):
        send(jnp.where(step < 0, -1, item_ref[2, jnp.maximum(step, 0)]))

    lag = 6

    def ramp_up(step, carry):
        forward(step - 1)
        fetch(step)
        return carry

    def steady(step, carry):
        send_step(step - lag - 1)
        backward(step - lag)
        forward(step - 1)
        fetch(step)
        return carry

    def ramp_down(step, carry):
        send_step(step - lag - 1)
        backward(step - lag)
        return carry

    lax.fori_loop(0, lag, ramp_up, 0)
    lax.fori_loop(lag, items, steady, 0)
    send_step(items - lag - 1)
    backward(items - lag)
    forward(items - 1)
    lax.fori_loop(items + 1, items + lag + 1, ramp_down, 0)
    for tile in range(tiles):
        image_ref[tile] = picture_ref[tile, 0:3]
    for owner in range(owners):
        for field in range(fields):
            row = field * owners + owner
            low = fields * owners + row
            outgoing_ref[owner, :, field * capacity : (field + 1) * capacity] = (
                outgo_ref[row : row + 1, :] + outgo_ref[low : low + 1, :]
            )


def render_call(counts, tile_row, lists, rank, fetched, d_image, shift):
    owners, _, width = fetched.shape
    capacity = width // fields
    tiles, slots = lists.shape
    pixels = d_image.shape[2]
    kept = tiles * slots // 256 + 1
    smem = pl.BlockSpec(memory_space=pltpu.SMEM)
    vmem = pl.BlockSpec(memory_space=pltpu.VMEM)
    return pl.pallas_call(
        functools.partial(render_kernel, shift=shift),
        out_shape=(
            jax.ShapeDtypeStruct((tiles, 3, pixels), f32),
            jax.ShapeDtypeStruct((owners, 1, fields * capacity), f32),
        ),
        in_specs=[smem, smem, vmem, vmem, vmem, vmem],
        out_specs=(vmem, vmem),
        scratch_shapes=[
            pltpu.SMEM((3, kept), i32),
            pltpu.VMEM((fields * owners, capacity), f32),
            pltpu.VMEM(((2 * fields + 2) * owners, capacity), bf16),
            pltpu.VMEM((kept, 8, 256), f32),
            pltpu.VMEM((kept, 24, 256), bf16),
            pltpu.VMEM((kept, 16, 256), bf16),
            pltpu.VMEM((kept, 16, 256), bf16),
            pltpu.VMEM((tiles, pixels, 16), bf16),
            pltpu.VMEM((tiles, 16, pixels), bf16),
            pltpu.VMEM((pixels, 128), f32),
            pltpu.VMEM((pixels, 128), f32),
            pltpu.VMEM((tiles + 1, 8, pixels), f32),
            pltpu.VMEM((kept, pixels, 256), f32),
            pltpu.VMEM((kept, pixels, 256), f32),
            pltpu.VMEM((kept, 8, 256), f32),
            pltpu.VMEM((kept, 2 * fields * owners, 256), bf16),
            pltpu.VMEM((kept, capacity, 256), bf16),
            pltpu.VMEM((2 * fields * owners, capacity), f32),
        ],
        compiler_params=pltpu.CompilerParams(vmem_limit_bytes=vmem_bytes),
        name="render",
    )(counts, tile_row, lists, rank, fetched, d_image)


def body(params, camera, tile_lists, tile_counts, d_image):
    owners = lax.axis_size("tiles")
    views = lax.axis_size("views")
    channels, shard_size = params.shape
    shift = shard_size.bit_length() - 1
    tiles, slots = tile_lists.shape[1:]
    pixels = d_image.shape[3]
    capacity = 3 * tiles * slots // (2 * owners)
    rows = shard_size // 256
    part_rows = rows // views
    center = jnp.array([tiles * 8.0, owners * 8.0, 0.0], f32)
    camera_row = jnp.concatenate([jnp.cos(camera[0, :1]), jnp.sin(camera[0, :1]), camera[0, 1:4], center])
    counts = tile_counts[0]
    lists = tile_lists[0]
    tile_row = lax.axis_index("tiles").astype(i32).reshape(1)
    view_here = lax.axis_index("views").astype(i32).reshape(1)
    smem = pl.BlockSpec(memory_space=pltpu.SMEM)
    vmem = pl.BlockSpec(memory_space=pltpu.VMEM)
    settings = pltpu.CompilerParams(vmem_limit_bytes=vmem_bytes)

    requests, rank = pl.pallas_call(
        functools.partial(bucket_kernel, owners=owners, capacity=capacity, shift=shift),
        out_shape=(
            jax.ShapeDtypeStruct((owners, 1, capacity), i32),
            jax.ShapeDtypeStruct((tiles, slots), i32),
        ),
        in_specs=[smem, vmem],
        out_specs=(vmem, vmem),
        scratch_shapes=[
            pltpu.VMEM((tiles * slots // 256 * owners, 256), bf16),
            pltpu.VMEM((tiles * slots // 256 * owners, 256), f32),
        ],
        compiler_params=settings,
        name="bucket",
    )(counts, lists)
    asked = lax.all_to_all(requests, "tiles", split_axis=0, concat_axis=0, tiled=True)
    dense_params = params.reshape(channels, rows, 256)
    table = pl.pallas_call(
        project_kernel,
        out_shape=jax.ShapeDtypeStruct(((2 * fields + 2) * rows, 256), bf16),
        in_specs=[smem, vmem],
        out_specs=vmem,
        compiler_params=settings,
        name="project",
    )(camera_row, dense_params)
    found = pl.pallas_call(
        functools.partial(lookup_kernel, group=4),
        out_shape=jax.ShapeDtypeStruct((owners, 1, fields * capacity), f32),
        in_specs=[vmem, vmem],
        out_specs=vmem,
        compiler_params=settings,
        name="lookup",
    )(asked, table)
    fetched = lax.all_to_all(found, "tiles", split_axis=0, concat_axis=0, tiled=True)
    picture, outgoing = render_call(counts, tile_row, lists, rank, fetched, d_image[0], shift)
    returned = lax.all_to_all(outgoing, "tiles", split_axis=0, concat_axis=0, tiled=True)
    sums = pl.pallas_call(
        functools.partial(collect_kernel, rows=rows, group=2),
        out_shape=jax.ShapeDtypeStruct((views, fields * part_rows + 8, 256), f32),
        in_specs=[smem, vmem, vmem],
        out_specs=vmem,
        scratch_shapes=[pltpu.VMEM((2 * fields * rows, 256), f32)],
        compiler_params=settings,
        name="collect",
    )(camera_row, asked, returned)
    all_sums = lax.all_to_all(sums, "views", split_axis=0, concat_axis=0, tiled=True)
    grads = pl.pallas_call(
        pull_kernel,
        out_shape=jax.ShapeDtypeStruct((channels, part_rows * 256), f32),
        grid_spec=pltpu.PrefetchScalarGridSpec(
            num_scalar_prefetch=1,
            grid=(1,),
            in_specs=[
                pl.BlockSpec((views, fields * part_rows + 8, 256), lambda step, place: (0, 0, 0)),
                pl.BlockSpec((channels, part_rows, 256), lambda step, place: (0, place[0], 0)),
            ],
            out_specs=pl.BlockSpec((channels, part_rows * 256), lambda step, place: (0, 0)),
        ),
        compiler_params=settings,
        name="pull",
    )(view_here, all_sums, dense_params)
    return picture[None], grads


def solution(mesh):
    placed = (
        P(None, "tiles"),
        P("views", None),
        P("views", "tiles", None),
        P("views", "tiles"),
        P("views", "tiles", None, None),
    )
    return jax.shard_map(
        body,
        mesh=mesh,
        in_specs=placed,
        out_specs=(P("views", "tiles", None, None), P(None, ("tiles", "views"))),
        check_vma=False,
    )
```

```python
import functools
import math

import jax
import jax.numpy as jnp
from jax import lax
from jax.experimental import pallas as pl
from jax.experimental.pallas import tpu as pltpu
from jax.sharding import PartitionSpec as P

focal_px = 600.0
lowpass = 0.3
harmonic_zero = 0.28209479177387814
harmonic_one = 0.4886025119029199
harmonic_two = (
    1.0925484305920792,
    -1.0925484305920792,
    0.31539156525252005,
    -1.0925484305920792,
    0.5462742152960396,
)
harmonic_three = (
    -0.5900435899266435,
    2.890611442640554,
    -0.4570457994644658,
    0.3731763325901154,
    -0.4570457994644658,
    1.445305721320277,
    -0.5900435899266435,
)
bf16 = jnp.bfloat16
f32 = jnp.float32
i32 = jnp.int32
log2_e = 1.0 / math.log(2.0)
ln_2 = math.log(2.0)
nt_dims = (((1,), (1,)), ((), ()))
render_vmem_bytes = 48 * 1024 * 1024
fields = 9


def split_two(values):
    upper = values.astype(bf16)
    lower = (values - upper.astype(f32)).astype(bf16)
    return upper, lower


def split_three(values):
    upper = values.astype(bf16)
    rest = values - upper.astype(f32)
    middle = rest.astype(bf16)
    lower = (rest - middle.astype(f32)).astype(bf16)
    return upper, middle, lower


def project(gauss_rows, camera_row, center_x, center_y):
    cosine, sine_val, shift_x, shift_y, shift_z = camera_row
    cam_x = cosine * gauss_rows[0] + sine_val * gauss_rows[2] + shift_x
    cam_y = gauss_rows[1] + shift_y
    cam_z = cosine * gauss_rows[2] - sine_val * gauss_rows[0] + shift_z
    inverse_z = 1.0 / cam_z
    jac_a = focal_px * inverse_z
    pos_u = jac_a * cam_x + center_x
    pos_v = jac_a * cam_y + center_y
    jac_b = -jac_a * cam_x * inverse_z
    jac_c = -jac_a * cam_y * inverse_z
    first_row = (jac_a * cosine - jac_b * sine_val, jac_a * sine_val + jac_b * cosine)
    second_row = (-jac_c * sine_val, jac_a, jac_c * cosine)
    quaternion = gauss_rows[6:10]
    inv_norm = lax.rsqrt(
        quaternion[0] * quaternion[0]
        + quaternion[1] * quaternion[1]
        + quaternion[2] * quaternion[2]
        + quaternion[3] * quaternion[3]
    )
    quat_w, quat_x, quat_y, quat_z = (entry * inv_norm for entry in quaternion)
    rotation = (
        (
            1.0 - 2.0 * (quat_y * quat_y + quat_z * quat_z),
            2.0 * (quat_x * quat_y - quat_w * quat_z),
            2.0 * (quat_x * quat_z + quat_w * quat_y),
        ),
        (
            2.0 * (quat_x * quat_y + quat_w * quat_z),
            1.0 - 2.0 * (quat_x * quat_x + quat_z * quat_z),
            2.0 * (quat_y * quat_z - quat_w * quat_x),
        ),
        (
            2.0 * (quat_x * quat_z - quat_w * quat_y),
            2.0 * (quat_y * quat_z + quat_w * quat_x),
            1.0 - 2.0 * (quat_x * quat_x + quat_y * quat_y),
        ),
    )
    scales = [jnp.exp(entry) for entry in gauss_rows[3:6]]
    upper_a = [
        (first_row[0] * rotation[0][entry] + first_row[1] * rotation[2][entry]) * scales[entry]
        for entry in range(3)
    ]
    lower_a = [
        (
            second_row[0] * rotation[0][entry]
            + second_row[1] * rotation[1][entry]
            + second_row[2] * rotation[2][entry]
        )
        * scales[entry]
        for entry in range(3)
    ]
    cov_a = upper_a[0] * upper_a[0] + upper_a[1] * upper_a[1] + upper_a[2] * upper_a[2] + lowpass
    cov_b = upper_a[0] * lower_a[0] + upper_a[1] * lower_a[1] + upper_a[2] * lower_a[2]
    cov_c = lower_a[0] * lower_a[0] + lower_a[1] * lower_a[1] + lower_a[2] * lower_a[2] + lowpass
    inv_det = 1.0 / (cov_a * cov_c - cov_b * cov_b)
    coef_a = (-0.5 * log2_e) * cov_c * inv_det
    coef_b = log2_e * cov_b * inv_det
    coef_c = (-0.5 * log2_e) * cov_a * inv_det
    log_opacity = -log2_e * jnp.log(1.0 + jnp.exp(-gauss_rows[10]))
    dir_x = cosine * cam_x - sine_val * cam_z
    dir_y = cam_y
    dir_z = sine_val * cam_x + cosine * cam_z
    inv_len = lax.rsqrt(dir_x * dir_x + dir_y * dir_y + dir_z * dir_z)
    dir_x = dir_x * inv_len
    dir_y = dir_y * inv_len
    dir_z = dir_z * inv_len
    sq_x = dir_x * dir_x
    sq_y = dir_y * dir_y
    sq_z = dir_z * dir_z
    harmonics = (
        harmonic_zero,
        -harmonic_one * dir_y,
        harmonic_one * dir_z,
        -harmonic_one * dir_x,
        harmonic_two[0] * dir_x * dir_y,
        harmonic_two[1] * dir_y * dir_z,
        harmonic_two[2] * (2.0 * sq_z - sq_x - sq_y),
        harmonic_two[3] * dir_x * dir_z,
        harmonic_two[4] * (sq_x - sq_y),
        harmonic_three[0] * dir_y * (3.0 * sq_x - sq_y),
        harmonic_three[1] * dir_x * dir_y * dir_z,
        harmonic_three[2] * dir_y * (4.0 * sq_z - sq_x - sq_y),
        harmonic_three[3] * dir_z * (2.0 * sq_z - 3.0 * sq_x - 3.0 * sq_y),
        harmonic_three[4] * dir_x * (4.0 * sq_z - sq_x - sq_y),
        harmonic_three[5] * dir_z * (sq_x - sq_y),
        harmonic_three[6] * dir_x * (sq_x - 3.0 * sq_y),
    )
    colors = []
    for channel in range(3):
        total = harmonics[0] * gauss_rows[11 + channel] + 0.5
        for basis in range(1, 16):
            total = total + harmonics[basis] * gauss_rows[11 + 3 * basis + channel]
        colors.append(total)
    return (pos_u, pos_v, coef_a, coef_b, coef_c, log_opacity, *colors)


def project_kernel(camera_ref, place_ref, params_ref, table_ref, third_ref, part_ref, dense_ref):
    channels, rows, _ = dense_ref.shape
    part_rows = part_ref.shape[1]
    camera_row = [camera_ref[entry] for entry in range(5)]
    center_x, center_y = camera_ref[5], camera_ref[6]
    for channel in range(channels):
        for row in range(rows):
            dense_ref[channel, row : row + 1, :] = params_ref[channel : channel + 1, row * 256 : row * 256 + 256]

    def step(part, carry):
        at = pl.multiple_of(part * 16, 16)
        gauss_rows = [dense_ref[channel, pl.ds(at, 16), :] for channel in range(channels)]
        outputs = project(gauss_rows, camera_row, center_x, center_y)
        for field, values in enumerate(outputs):
            pieces = split_three(values)
            table_ref[pl.ds(field * rows + at, 16), :256] = pieces[0]
            table_ref[pl.ds(field * rows + at, 16), 256:] = pieces[1]
            if field < 2:
                third_ref[pl.ds(field * rows + at, 16), :] = pieces[2]
        return carry

    lax.fori_loop(0, rows // 16, step, 0)
    at = pl.multiple_of(place_ref[0] * part_rows, part_rows)
    for channel in range(channels):
        part_ref[channel] = dense_ref[channel, pl.ds(at, part_rows), :]


def bucket_kernel(counts_ref, lists_ref, requests_ref, rank_ref, hits_ref, earlier_ref, *, owners, capacity, shift):
    tiles, slots = lists_ref.shape
    blocks = slots // 256
    upper = (
        lax.broadcasted_iota(i32, (256, 256), 0) < lax.broadcasted_iota(i32, (256, 256), 1)
    ).astype(f32).astype(bf16)
    owner_rows = lax.broadcasted_iota(i32, (owners, 256), 0)
    lane = lax.broadcasted_iota(i32, (1, 256), 1)
    for tile in range(tiles):
        for block in range(blocks):
            ids = lists_ref[tile : tile + 1, block * 256 : block * 256 + 256]
            owner = jnp.where(lane + block * 256 < counts_ref[tile], ids >> shift, -1)
            at = (tile * blocks + block) * owners
            hits_ref[at : at + owners, :] = jnp.where(owner_rows == owner, 1.0, 0.0).astype(bf16)
    earlier_ref[...] = jnp.dot(hits_ref[...], upper, preferred_element_type=f32)
    rank_rows = lax.broadcasted_iota(i32, (capacity, 256), 0)
    carry = jnp.zeros((owners, 1), f32)
    total = jnp.zeros((2 * owners, capacity), f32)
    for tile in range(tiles):
        for block in range(blocks):
            at = (tile * blocks + block) * owners
            hits = hits_ref[at : at + owners, :].astype(f32)
            earlier = earlier_ref[at : at + owners, :]
            rank = jnp.sum(hits * (earlier + carry), axis=0, keepdims=True)
            live = lane + block * 256 < counts_ref[tile]
            rank = jnp.where(live, rank, -1.0).astype(i32)
            rank_ref[tile : tile + 1, block * 256 : block * 256 + 256] = rank
            carry = carry + earlier[:, 255:256] + hits[:, 255:256]
            ids = lists_ref[tile : tile + 1, block * 256 : block * 256 + 256]
            local = (ids & ((1 << shift) - 1)) + 1
            coarse = (local >> 7).astype(f32)
            fine = (local & 127).astype(f32)
            placed = jnp.concatenate([hits * coarse, hits * fine], axis=0).astype(bf16)
            at_rank = jnp.where(rank_rows == rank, 1.0, 0.0).astype(bf16)
            total = total + lax.dot_general(placed, at_rank, nt_dims, preferred_element_type=f32)
    requests = (total[:owners] * 128.0 + total[owners:]).astype(i32) - 1
    for owner in range(owners):
        requests_ref[owner] = requests[owner : owner + 1]


def lookup_kernel(asked_ref, table_ref, third_ref, found_ref, *, group):
    askers, _, capacity = asked_ref.shape
    rows = table_ref.shape[0] // fields
    width = group * capacity
    low_rows = lax.broadcasted_iota(i32, (256, width), 0)
    high_rows = lax.broadcasted_iota(i32, (rows, width), 0)

    def step(part, carry):
        asked = jnp.concatenate([asked_ref[group * part + k] for k in range(group)], axis=1)
        pick = jnp.where(low_rows == (asked & 255), 1.0, 0.0).astype(bf16)
        mask = high_rows == (asked >> 8)
        result = jnp.dot(
            table_ref[...], jnp.concatenate([pick, pick], axis=0), preferred_element_type=f32
        )
        third = jnp.dot(third_ref[...], pick, preferred_element_type=f32)
        for field in range(fields):
            values = result[field * rows : (field + 1) * rows]
            if field < 2:
                values = values + third[field * rows : (field + 1) * rows]
            found = jnp.sum(jnp.where(mask, values, 0.0), axis=0, keepdims=True)
            for k in range(group):
                found_ref[group * part + k, :, field * capacity : (field + 1) * capacity] = found[
                    :, k * capacity : (k + 1) * capacity
                ]
        return carry

    lax.fori_loop(0, askers // group, step, 0)


def collect_kernel(camera_ref, place_ref, asked_ref, returned_ref, *rest, rows, group):
    *sums_refs, total_ref = rest
    askers, _, capacity = asked_ref.shape
    views = len(sums_refs)
    width = group * capacity
    low_rows = lax.broadcasted_iota(i32, (256, width), 0)
    high_rows = lax.broadcasted_iota(i32, (rows, width), 0)
    total_ref[...] = jnp.zeros_like(total_ref)

    def step(part, carry):
        asked = jnp.concatenate([asked_ref[group * part + k] for k in range(group)], axis=1)
        pick = jnp.where(low_rows == (asked & 255), 1.0, 0.0).astype(bf16)
        mask = high_rows == (asked >> 8)
        uppers = []
        lowers = []
        for field in range(fields):
            values = jnp.concatenate(
                [
                    returned_ref[group * part + k, :, field * capacity : (field + 1) * capacity]
                    for k in range(group)
                ],
                axis=1,
            )
            upper = values.astype(bf16).astype(f32)
            uppers.append(jnp.where(mask, upper, 0.0).astype(bf16))
            lowers.append(jnp.where(mask, values - upper, 0.0).astype(bf16))
        placed = jnp.concatenate(
            [jnp.concatenate(uppers, axis=0), jnp.concatenate(lowers, axis=0)], axis=1
        )
        total_ref[...] += lax.dot_general(
            placed, jnp.concatenate([pick, pick], axis=1), nt_dims, preferred_element_type=f32
        )
        return carry

    lax.fori_loop(0, askers // group, step, 0)
    part_rows = rows // views
    for offset, sums_ref in enumerate(sums_refs):
        view = lax.rem(place_ref[0] + offset, views)
        for field in range(fields):
            at = pl.multiple_of(field * rows + view * part_rows, part_rows)
            sums_ref[field * part_rows : (field + 1) * part_rows, :] = total_ref[pl.ds(at, part_rows), :]
        for entry in range(8):
            at = fields * part_rows + entry
            sums_ref[at : at + 1, :] = jnp.full((1, 256), camera_ref[entry], f32)


def pull_kernel(*refs):
    *sums_refs, params_ref, grads_ref = refs
    channels, part_rows, _ = params_ref.shape
    gauss_rows = [params_ref[channel] for channel in range(channels)]
    totals = None
    for sums_ref in sums_refs:
        at = fields * part_rows
        camera_row = [
            jnp.broadcast_to(sums_ref[at + entry : at + entry + 1, :], (part_rows, 256))
            for entry in range(5)
        ]
        _, pull = jax.vjp(lambda rows_in: project(rows_in, camera_row, 0.0, 0.0), gauss_rows)
        (one,) = pull(
            tuple(
                sums_ref[field * part_rows : (field + 1) * part_rows, :]
                for field in range(fields)
            )
        )
        totals = one if totals is None else [x + y for x, y in zip(totals, one)]
    for channel in range(channels):
        for row in range(part_rows):
            grads_ref[channel : channel + 1, row * 256 : row * 256 + 256] = totals[channel][
                row : row + 1
            ]


def monomial(index, pix_x, pix_y):
    pix_x = pix_x.astype(f32) - 7.5
    pix_y = pix_y.astype(f32) - 7.5
    values = jnp.where(index == 0, 1.0, 0.0)
    values = jnp.where(index == 1, pix_x, values)
    values = jnp.where(index == 2, pix_y, values)
    values = jnp.where(index == 3, pix_x * pix_x, values)
    values = jnp.where(index == 4, pix_x * pix_y, values)
    return jnp.where(index == 5, pix_y * pix_y, values)


def render_kernel(
    counts_ref,
    place_ref,
    lists_ref,
    rank_ref,
    fetched_ref,
    d_image_ref,
    image_ref,
    outgoing_ref,
    item_ref,
    rows_ref,
    fetch_ref,
    value_ref,
    polynomial_ref,
    color_rows_ref,
    color_left_ref,
    d_columns_ref,
    d_left_ref,
    earlier_ref,
    later_ref,
    picture_ref,
    blend_ref,
    ratio_ref,
    color_grad_ref,
    placed_ref,
    at_rank_ref,
    outgo_ref,
    *,
    shift,
):
    tiles, slots = lists_ref.shape
    owners, _, width = fetched_ref.shape
    capacity = width // fields
    spare = tiles * slots // 256
    pixels = d_image_ref.shape[2]

    def list_tile(tile, base):
        live_blocks = (counts_ref[tile] + 255) // 256

        def list_block(block, carry):
            item_ref[0, base + block] = tile
            item_ref[1, base + block] = block
            item_ref[2, base + block] = base + live_blocks - 1 - block
            return carry

        lax.fori_loop(0, live_blocks, list_block, 0)
        return base + live_blocks

    items = lax.fori_loop(0, tiles, list_tile, 0)
    for owner in range(owners):
        for field in range(fields):
            row = field * owners + owner
            rows_ref[row : row + 1, :] = fetched_ref[owner, :, field * capacity : (field + 1) * capacity]
    center_v = place_ref[0].astype(f32) * 16.0 + 8.0
    for field in range(fields):
        values = rows_ref[field * owners : (field + 1) * owners, :]
        if field == 1:
            values = values - center_v
        upper, lower = split_two(values)
        fetch_ref[field * owners : (field + 1) * owners, :capacity] = upper
        fetch_ref[field * owners : (field + 1) * owners, capacity:] = lower
    for tile in range(tiles):
        d_rows = d_image_ref[tile]
        d_upper, d_lower = [piece.astype(f32) for piece in split_two(d_rows)]
        d_stack = jnp.concatenate([d_upper, d_lower, d_upper, d_lower, jnp.zeros((4, pixels), f32)], axis=0)
        d_columns_ref[tile] = jnp.transpose(d_stack).astype(bf16)
        d_left_ref[tile] = jnp.concatenate([d_upper, d_lower, jnp.zeros((10, pixels), f32)], axis=0).astype(bf16)
    outgo_ref[...] = jnp.zeros_like(outgo_ref)
    placed_ref[spare] = jnp.zeros(placed_ref.shape[1:], bf16)
    at_rank_ref[spare] = jnp.zeros(at_rank_ref.shape[1:], bf16)
    row_index = lax.broadcasted_iota(i32, (256, 256), 0)
    lane_index = lax.broadcasted_iota(i32, (256, 256), 1)
    before = (row_index < lane_index).astype(f32).astype(bf16)
    after = (row_index > lane_index).astype(f32).astype(bf16)
    pixel_row = lax.broadcasted_iota(i32, (pixels, 24), 0)
    monomials = monomial(
        lax.broadcasted_iota(i32, (pixels, 24), 1) & 7, pixel_row & 15, pixel_row >> 4
    ).astype(bf16)
    pixel_lane = lax.broadcasted_iota(i32, (16, pixels), 1)
    moments_of = monomial(
        lax.broadcasted_iota(i32, (16, pixels), 0), pixel_lane & 15, pixel_lane >> 4
    ).astype(bf16)
    rank_rows = lax.broadcasted_iota(i32, (capacity, 256), 0)
    owner_rows = lax.broadcasted_iota(i32, (owners, 256), 0)

    def owner_and_rank(item):
        tile = item_ref[0, item]
        at = pl.multiple_of(item_ref[1, item] * 256, 256)
        owner = lists_ref[pl.ds(tile, 1), pl.ds(at, 256)] >> shift
        rank = rank_ref[pl.ds(tile, 1), pl.ds(at, 256)]
        return owner, rank

    def fetch(item):
        owner, rank = owner_and_rank(item)
        tile = item_ref[0, item]
        at_rank = jnp.where(rank_rows == rank, 1.0, 0.0).astype(bf16)
        at_rank_ref[item] = at_rank
        yield
        fetched = jnp.dot(
            fetch_ref[...], jnp.concatenate([at_rank, at_rank], axis=0), preferred_element_type=f32
        )
        yield
        mask = owner_rows == owner
        found = []
        for field in range(fields):
            values = fetched[field * owners : (field + 1) * owners]
            found.append(jnp.sum(jnp.where(mask, values, 0.0), axis=0, keepdims=True))
        pos_u = found[0] - (tile.astype(f32) * 16.0 + 8.0)
        pos_v = found[1]
        coef_a, coef_b, coef_c, log_opacity = found[2:6]
        log_opacity = jnp.where(rank >= 0, log_opacity, -1.0e4)
        slope_u = coef_a * pos_u * 2.0 + coef_b * pos_v
        slope_v = coef_c * pos_v * 2.0 + coef_b * pos_u
        constant = log_opacity + 0.5 * (slope_u * pos_u + slope_v * pos_v)
        blank = jnp.zeros((3, 256), f32)
        value_ref[item] = jnp.concatenate([pos_u, pos_v, coef_a, coef_b, coef_c, blank], axis=0)
        polynomial = jnp.concatenate(
            [constant, -slope_u, -slope_v, coef_a, coef_b, coef_c, blank[0:2]], axis=0
        )
        pieces = [piece.astype(f32) for piece in split_three(polynomial)]
        polynomial_ref[item] = jnp.concatenate(pieces, axis=0).astype(bf16)
        upper, lower = [piece.astype(f32) for piece in split_two(jnp.concatenate(found[6:9], axis=0))]
        color_rows_ref[item] = jnp.concatenate(
            [upper, upper, lower, lower, jnp.zeros((4, 256), f32)], axis=0
        ).astype(bf16)
        color_left_ref[item] = jnp.concatenate(
            [upper, lower, jnp.zeros((10, 256), f32)], axis=0
        ).astype(bf16)
        yield

    def forward(item):
        live = item >= 0
        at = jnp.where(live, item, spare)
        item = jnp.maximum(item, 0)
        tile = item_ref[0, item]
        first = item_ref[1, item] == 0
        exponent = jnp.dot(monomials, polynomial_ref[at], preferred_element_type=f32)
        yield
        earlier = jnp.where(first, 0.0, earlier_ref[...])
        earlier = jnp.concatenate([earlier, earlier], axis=1)
        alpha = jnp.exp2(exponent)
        keep = 1.0 - alpha
        log_keep = jnp.log2(keep)
        upper, lower = split_two(log_keep)
        yield
        within = jnp.dot(upper, before, preferred_element_type=f32) + jnp.dot(
            lower, before, preferred_element_type=f32
        )
        pull = jnp.dot(d_columns_ref[tile], color_rows_ref[at], preferred_element_type=f32)
        yield
        within = within + earlier
        weight = jnp.exp2(within) * alpha
        earlier_ref[...] = jnp.broadcast_to(within[:, 255:256] + log_keep[:, 255:256], (pixels, 128))
        blend_ref[at] = weight * pull
        ratio_ref[at] = alpha / keep
        upper, lower = split_two(weight)
        yield
        d_left = d_left_ref[tile]
        one = jnp.dot(d_left, upper, preferred_element_type=f32)
        two = jnp.dot(d_left, lower, preferred_element_type=f32)
        color_grad_ref[at, 0:3] = one[0:3] + one[3:6] + two[0:3]
        color_left = color_left_ref[at]
        one = lax.dot_general(color_left, upper, nt_dims, preferred_element_type=f32)
        two = lax.dot_general(color_left, lower, nt_dims, preferred_element_type=f32)
        picture = one[0:3] + one[3:6] + two[0:3]
        at_tile = jnp.where(live, tile, tiles)
        picture_ref[at_tile, 0:3] = jnp.where(first, 0.0, picture_ref[at_tile, 0:3]) + picture
        yield

    def backward(step):
        step = jnp.minimum(step, items)
        live = step < items
        at = jnp.where(live, item_ref[2, jnp.minimum(step, items - 1)], spare)
        item = jnp.where(live, at, 0)
        first = item_ref[1, jnp.minimum(step, items - 1)] == 0
        owner, rank = owner_and_rank(item)
        blend = blend_ref[at]
        upper, lower = split_two(blend)
        within = jnp.dot(upper, after, preferred_element_type=f32) + jnp.dot(
            lower, after, preferred_element_type=f32
        )
        yield
        later = jnp.where(first, 0.0, later_ref[...])
        within = within + jnp.concatenate([later, later], axis=1)
        later_ref[...] = jnp.broadcast_to(within[:, 0:1] + blend[:, 0:1], (pixels, 128))
        gradient = blend - within * ratio_ref[at]
        pieces = split_two(gradient)
        yield
        moments = (
            jnp.dot(moments_of, pieces[0], preferred_element_type=f32)
            + jnp.dot(moments_of, pieces[1], preferred_element_type=f32)
        ) * ln_2
        yield
        plain, first_x, first_y = moments[0:1], moments[1:2], moments[2:3]
        pos_u, pos_v, coef_a, coef_b, coef_c = (value_ref[at, k : k + 1] for k in range(5))
        from_u = first_x - pos_u * plain
        from_v = first_y - pos_v * plain
        outputs = [
            -2.0 * coef_a * from_u - coef_b * from_v,
            -2.0 * coef_c * from_v - coef_b * from_u,
            moments[3:4] - pos_u * (first_x + from_u),
            moments[4:5] - pos_v * first_x - pos_u * from_v,
            moments[5:6] - pos_v * (first_y + from_v),
            plain,
        ] + [color_grad_ref[at, k : k + 1] for k in range(3)]
        mask = owner_rows == jnp.where(rank >= 0, owner, -1)
        for field, values in enumerate(outputs):
            upper = values.astype(bf16).astype(f32)
            row = field * owners
            placed_ref[at, row : row + owners, :256] = jnp.where(mask, upper, 0.0).astype(bf16)
            placed_ref[at, row : row + owners, 256:] = jnp.where(mask, values - upper, 0.0).astype(bf16)
        yield

    def send(item):
        at = jnp.where(item < 0, spare, item)
        outgo_ref[...] += lax.dot_general(
            placed_ref[at],
            jnp.concatenate([at_rank_ref[at], at_rank_ref[at]], axis=1),
            nt_dims,
            preferred_element_type=f32,
        )
        yield

    def send_step(step):
        return send(jnp.where(step < 0, -1, item_ref[2, jnp.maximum(step, 0)]))

    lag = 6

    def run(order, **stages):
        for name in order:
            next(stages[name])
        for left in stages.values():
            for _ in left:
                raise ValueError(order)

    def ramp_up(step, carry):
        run("mmmmmfff", m=forward(step - 1), f=fetch(step))
        return carry

    def steady(step, carry):
        run(
            "mbsmfmbfmbmbf",
            s=send_step(step - lag - 1),
            b=backward(step - lag),
            m=forward(step - 1),
            f=fetch(step),
        )
        return carry

    def ramp_down(step, carry):
        run("sbbbb", s=send_step(step - lag - 1), b=backward(step - lag))
        return carry

    lax.fori_loop(0, lag, ramp_up, 0)
    lax.fori_loop(lag, items, steady, 0)
    run("sbbbbmmmmm", s=send_step(items - lag - 1), b=backward(items - lag), m=forward(items - 1))
    lax.fori_loop(items + 1, items + lag + 1, ramp_down, 0)
    for tile in range(tiles):
        image_ref[tile] = picture_ref[tile, 0:3]
    for owner in range(owners):
        for field in range(fields):
            row = field * owners + owner
            outgoing_ref[owner, :, field * capacity : (field + 1) * capacity] = outgo_ref[row : row + 1, :]


def render_call(counts, tile_row, lists, rank, fetched, d_image, shift):
    owners, _, width = fetched.shape
    capacity = width // fields
    tiles, slots = lists.shape
    pixels = d_image.shape[2]
    kept = tiles * slots // 256 + 1
    smem = pl.BlockSpec(memory_space=pltpu.SMEM)
    vmem = pl.BlockSpec(memory_space=pltpu.VMEM)
    return pl.pallas_call(
        functools.partial(render_kernel, shift=shift),
        out_shape=(
            jax.ShapeDtypeStruct((tiles, 3, pixels), f32),
            jax.ShapeDtypeStruct((owners, 1, fields * capacity), f32),
        ),
        in_specs=[smem, smem, vmem, vmem, vmem, vmem],
        out_specs=(vmem, vmem),
        scratch_shapes=[
            pltpu.SMEM((3, kept), i32),
            pltpu.VMEM((fields * owners, capacity), f32),
            pltpu.VMEM((fields * owners, 2 * capacity), bf16),
            pltpu.VMEM((kept, 8, 256), f32),
            pltpu.VMEM((kept, 24, 256), bf16),
            pltpu.VMEM((kept, 16, 256), bf16),
            pltpu.VMEM((kept, 16, 256), bf16),
            pltpu.VMEM((tiles, pixels, 16), bf16),
            pltpu.VMEM((tiles, 16, pixels), bf16),
            pltpu.VMEM((pixels, 128), f32),
            pltpu.VMEM((pixels, 128), f32),
            pltpu.VMEM((tiles + 1, 8, pixels), f32),
            pltpu.VMEM((kept, pixels, 256), f32),
            pltpu.VMEM((kept, pixels, 256), f32),
            pltpu.VMEM((kept, 8, 256), f32),
            pltpu.VMEM((kept, fields * owners, 512), bf16),
            pltpu.VMEM((kept, capacity, 256), bf16),
            pltpu.VMEM((fields * owners, capacity), f32),
        ],
        compiler_params=pltpu.CompilerParams(vmem_limit_bytes=render_vmem_bytes),
        name="render",
    )(counts, tile_row, lists, rank, fetched, d_image)


def body(params, camera, tile_lists, tile_counts, d_image):
    owners = lax.axis_size("tiles")
    views = lax.axis_size("views")
    channels, shard_size = params.shape
    shift = shard_size.bit_length() - 1
    tiles, slots = tile_lists.shape[1:]
    pixels = d_image.shape[3]
    capacity = 3 * tiles * slots // (2 * owners)
    rows = shard_size // 256
    part_rows = rows // views
    center = jnp.array([tiles * 8.0, owners * 8.0, 0.0], f32)
    camera_row = jnp.concatenate([jnp.cos(camera[0, :1]), jnp.sin(camera[0, :1]), camera[0, 1:4], center])
    counts = tile_counts[0]
    lists = tile_lists[0]
    tile_row = lax.axis_index("tiles").astype(i32).reshape(1)
    view_here = lax.axis_index("views").astype(i32).reshape(1)
    smem = pl.BlockSpec(memory_space=pltpu.SMEM)
    vmem = pl.BlockSpec(memory_space=pltpu.VMEM)

    def settings(mebibytes):
        return pltpu.CompilerParams(vmem_limit_bytes=mebibytes * 1024 * 1024)

    requests, rank = pl.pallas_call(
        functools.partial(bucket_kernel, owners=owners, capacity=capacity, shift=shift),
        out_shape=(
            jax.ShapeDtypeStruct((owners, 1, capacity), i32),
            jax.ShapeDtypeStruct((tiles, slots), i32),
        ),
        in_specs=[smem, vmem],
        out_specs=(vmem, vmem),
        scratch_shapes=[
            pltpu.VMEM((tiles * slots // 256 * owners, 256), bf16),
            pltpu.VMEM((tiles * slots // 256 * owners, 256), f32),
        ],
        compiler_params=settings(16),
        name="bucket",
    )(counts, lists)
    asked = lax.all_to_all(requests, "tiles", split_axis=0, concat_axis=0, tiled=True)
    table, third, part_params = pl.pallas_call(
        project_kernel,
        out_shape=(
            jax.ShapeDtypeStruct((fields * rows, 512), bf16),
            jax.ShapeDtypeStruct((2 * rows, 256), bf16),
            jax.ShapeDtypeStruct((channels, part_rows, 256), f32),
        ),
        in_specs=[smem, smem, vmem],
        out_specs=(vmem, vmem, vmem),
        scratch_shapes=[pltpu.VMEM((channels, rows, 256), f32)],
        compiler_params=settings(16),
        name="project",
    )(camera_row, view_here, params)
    found = pl.pallas_call(
        functools.partial(lookup_kernel, group=4),
        out_shape=jax.ShapeDtypeStruct((owners, 1, fields * capacity), f32),
        in_specs=[vmem, vmem, vmem],
        out_specs=vmem,
        compiler_params=settings(16),
        name="lookup",
    )(asked, table, third)
    fetched = lax.all_to_all(found, "tiles", split_axis=0, concat_axis=0, tiled=True)
    picture, outgoing = render_call(counts, tile_row, lists, rank, fetched, d_image[0], shift)
    returned = lax.all_to_all(outgoing, "tiles", split_axis=0, concat_axis=0, tiled=True)
    sums = pl.pallas_call(
        functools.partial(collect_kernel, rows=rows, group=2),
        out_shape=[jax.ShapeDtypeStruct((fields * part_rows + 8, 256), f32)] * views,
        in_specs=[smem, smem, vmem, vmem],
        out_specs=[vmem] * views,
        scratch_shapes=[pltpu.VMEM((fields * rows, 256), f32)],
        compiler_params=settings(16),
        name="collect",
    )(camera_row, view_here, asked, returned)
    all_sums = [sums[0]] + [
        lax.ppermute(sums[offset], "views", [(view, (view + offset) % views) for view in range(views)])
        for offset in range(1, views)
    ]
    grads = pl.pallas_call(
        pull_kernel,
        out_shape=jax.ShapeDtypeStruct((channels, part_rows * 256), f32),
        in_specs=[vmem] * (views + 1),
        out_specs=vmem,
        compiler_params=settings(16),
        name="pull",
    )(*all_sums, part_params)
    return picture[None], grads


def solution(mesh):
    placed = (
        P(None, "tiles"),
        P("views", None),
        P("views", "tiles", None),
        P("views", "tiles"),
        P("views", "tiles", None, None),
    )
    return jax.shard_map(
        body,
        mesh=mesh,
        in_specs=placed,
        out_specs=(P("views", "tiles", None, None), P(None, ("tiles", "views"))),
        check_vma=False,
    )
```

```python
import functools
import math

import jax
import jax.numpy as jnp
from jax import lax
from jax.experimental import pallas as pl
from jax.experimental.pallas import tpu as pltpu
from jax.sharding import PartitionSpec as P

focal_px = 600.0
lowpass = 0.3
harmonic_zero = 0.28209479177387814
harmonic_one = 0.4886025119029199
harmonic_two = (
    1.0925484305920792,
    -1.0925484305920792,
    0.31539156525252005,
    -1.0925484305920792,
    0.5462742152960396,
)
harmonic_three = (
    -0.5900435899266435,
    2.890611442640554,
    -0.4570457994644658,
    0.3731763325901154,
    -0.4570457994644658,
    1.445305721320277,
    -0.5900435899266435,
)
bf16 = jnp.bfloat16
f32 = jnp.float32
i32 = jnp.int32
log2_e = 1.0 / math.log(2.0)
ln_2 = math.log(2.0)
nt_dims = (((1,), (1,)), ((), ()))
render_vmem_bytes = 48 * 1024 * 1024
fields = 9


def split_two(values):
    upper = values.astype(bf16)
    lower = (values - upper.astype(f32)).astype(bf16)
    return upper, lower


def split_three(values):
    upper = values.astype(bf16)
    rest = values - upper.astype(f32)
    middle = rest.astype(bf16)
    lower = (rest - middle.astype(f32)).astype(bf16)
    return upper, middle, lower


def project(gauss_rows, camera_row, center_x, center_y):
    cosine, sine_val, shift_x, shift_y, shift_z = camera_row
    cam_x = cosine * gauss_rows[0] + sine_val * gauss_rows[2] + shift_x
    cam_y = gauss_rows[1] + shift_y
    cam_z = cosine * gauss_rows[2] - sine_val * gauss_rows[0] + shift_z
    inverse_z = 1.0 / cam_z
    jac_a = focal_px * inverse_z
    pos_u = jac_a * cam_x + center_x
    pos_v = jac_a * cam_y + center_y
    jac_b = -jac_a * cam_x * inverse_z
    jac_c = -jac_a * cam_y * inverse_z
    first_row = (jac_a * cosine - jac_b * sine_val, jac_a * sine_val + jac_b * cosine)
    second_row = (-jac_c * sine_val, jac_a, jac_c * cosine)
    quaternion = gauss_rows[6:10]
    inv_norm = lax.rsqrt(
        quaternion[0] * quaternion[0]
        + quaternion[1] * quaternion[1]
        + quaternion[2] * quaternion[2]
        + quaternion[3] * quaternion[3]
    )
    quat_w, quat_x, quat_y, quat_z = (entry * inv_norm for entry in quaternion)
    rotation = (
        (
            1.0 - 2.0 * (quat_y * quat_y + quat_z * quat_z),
            2.0 * (quat_x * quat_y - quat_w * quat_z),
            2.0 * (quat_x * quat_z + quat_w * quat_y),
        ),
        (
            2.0 * (quat_x * quat_y + quat_w * quat_z),
            1.0 - 2.0 * (quat_x * quat_x + quat_z * quat_z),
            2.0 * (quat_y * quat_z - quat_w * quat_x),
        ),
        (
            2.0 * (quat_x * quat_z - quat_w * quat_y),
            2.0 * (quat_y * quat_z + quat_w * quat_x),
            1.0 - 2.0 * (quat_x * quat_x + quat_y * quat_y),
        ),
    )
    scales = [jnp.exp(entry) for entry in gauss_rows[3:6]]
    upper_a = [
        (first_row[0] * rotation[0][entry] + first_row[1] * rotation[2][entry]) * scales[entry]
        for entry in range(3)
    ]
    lower_a = [
        (
            second_row[0] * rotation[0][entry]
            + second_row[1] * rotation[1][entry]
            + second_row[2] * rotation[2][entry]
        )
        * scales[entry]
        for entry in range(3)
    ]
    cov_a = upper_a[0] * upper_a[0] + upper_a[1] * upper_a[1] + upper_a[2] * upper_a[2] + lowpass
    cov_b = upper_a[0] * lower_a[0] + upper_a[1] * lower_a[1] + upper_a[2] * lower_a[2]
    cov_c = lower_a[0] * lower_a[0] + lower_a[1] * lower_a[1] + lower_a[2] * lower_a[2] + lowpass
    inv_det = 1.0 / (cov_a * cov_c - cov_b * cov_b)
    coef_a = (-0.5 * log2_e) * cov_c * inv_det
    coef_b = log2_e * cov_b * inv_det
    coef_c = (-0.5 * log2_e) * cov_a * inv_det
    log_opacity = -log2_e * jnp.log(1.0 + jnp.exp(-gauss_rows[10]))
    dir_x = cosine * cam_x - sine_val * cam_z
    dir_y = cam_y
    dir_z = sine_val * cam_x + cosine * cam_z
    inv_len = lax.rsqrt(dir_x * dir_x + dir_y * dir_y + dir_z * dir_z)
    dir_x = dir_x * inv_len
    dir_y = dir_y * inv_len
    dir_z = dir_z * inv_len
    sq_x = dir_x * dir_x
    sq_y = dir_y * dir_y
    sq_z = dir_z * dir_z
    harmonics = (
        harmonic_zero,
        -harmonic_one * dir_y,
        harmonic_one * dir_z,
        -harmonic_one * dir_x,
        harmonic_two[0] * dir_x * dir_y,
        harmonic_two[1] * dir_y * dir_z,
        harmonic_two[2] * (2.0 * sq_z - sq_x - sq_y),
        harmonic_two[3] * dir_x * dir_z,
        harmonic_two[4] * (sq_x - sq_y),
        harmonic_three[0] * dir_y * (3.0 * sq_x - sq_y),
        harmonic_three[1] * dir_x * dir_y * dir_z,
        harmonic_three[2] * dir_y * (4.0 * sq_z - sq_x - sq_y),
        harmonic_three[3] * dir_z * (2.0 * sq_z - 3.0 * sq_x - 3.0 * sq_y),
        harmonic_three[4] * dir_x * (4.0 * sq_z - sq_x - sq_y),
        harmonic_three[5] * dir_z * (sq_x - sq_y),
        harmonic_three[6] * dir_x * (sq_x - 3.0 * sq_y),
    )
    colors = []
    for channel in range(3):
        total = harmonics[0] * gauss_rows[11 + channel] + 0.5
        for basis in range(1, 16):
            total = total + harmonics[basis] * gauss_rows[11 + 3 * basis + channel]
        colors.append(total)
    return (pos_u, pos_v, coef_a, coef_b, coef_c, log_opacity, *colors)


def project_kernel(camera_ref, place_ref, params_ref, table_ref, third_ref, part_ref, dense_ref):
    channels, rows, _ = dense_ref.shape
    part_rows = part_ref.shape[1]
    camera_row = [camera_ref[entry] for entry in range(5)]
    center_x, center_y = camera_ref[5], camera_ref[6]
    for channel in range(channels):
        for row in range(rows):
            dense_ref[channel, row : row + 1, :] = params_ref[channel : channel + 1, row * 256 : row * 256 + 256]

    def step(part, carry):
        at = pl.multiple_of(part * 16, 16)
        gauss_rows = [dense_ref[channel, pl.ds(at, 16), :] for channel in range(channels)]
        outputs = project(gauss_rows, camera_row, center_x, center_y)
        for field, values in enumerate(outputs):
            pieces = split_three(values)
            table_ref[pl.ds(field * rows + at, 16), :256] = pieces[0]
            table_ref[pl.ds(field * rows + at, 16), 256:] = pieces[1]
            if field < 2:
                third_ref[pl.ds(field * rows + at, 16), :] = pieces[2]
        return carry

    lax.fori_loop(0, rows // 16, step, 0)
    at = pl.multiple_of(place_ref[0] * part_rows, part_rows)
    for channel in range(channels):
        part_ref[channel] = dense_ref[channel, pl.ds(at, part_rows), :]


def bucket_kernel(counts_ref, lists_ref, requests_ref, rank_ref, hits_ref, earlier_ref, *, owners, capacity, shift):
    tiles, slots = lists_ref.shape
    blocks = slots // 256
    thirds = capacity // 128
    upper = (
        lax.broadcasted_iota(i32, (256, 256), 0) < lax.broadcasted_iota(i32, (256, 256), 1)
    ).astype(f32).astype(bf16)
    owner_rows = lax.broadcasted_iota(i32, (owners, 256), 0)
    lane = lax.broadcasted_iota(i32, (1, 256), 1)
    for tile in range(tiles):
        for block in range(blocks):
            ids = lists_ref[tile : tile + 1, block * 256 : block * 256 + 256]
            owner = jnp.where(lane + block * 256 < counts_ref[tile], ids >> shift, -1)
            at = (tile * blocks + block) * owners
            hits_ref[at : at + owners, :] = jnp.where(owner_rows == owner, 1.0, 0.0).astype(bf16)
    earlier_ref[...] = jnp.dot(hits_ref[...], upper, preferred_element_type=f32)
    low_rows = lax.broadcasted_iota(i32, (128, 256), 0)
    high_rows = lax.broadcasted_iota(i32, (owners * thirds, 256), 0)
    carry = jnp.zeros((owners, 1), f32)
    total = jnp.zeros((2 * owners * thirds, 128), f32)
    for tile in range(tiles):
        for block in range(blocks):
            at = (tile * blocks + block) * owners
            hits = hits_ref[at : at + owners, :].astype(f32)
            earlier = earlier_ref[at : at + owners, :]
            rank = jnp.sum(hits * (earlier + carry), axis=0, keepdims=True).astype(i32)
            live = lane + block * 256 < counts_ref[tile]
            rank_ref[tile : tile + 1, block * 256 : block * 256 + 256] = jnp.where(live, rank, -1)
            carry = carry + earlier[:, 255:256] + hits[:, 255:256]
            ids = lists_ref[tile : tile + 1, block * 256 : block * 256 + 256]
            local = (ids & ((1 << shift) - 1)) + 1
            coarse = (local >> 7).astype(f32)
            fine = (local & 127).astype(f32)
            place = jnp.where(live, (ids >> shift) * thirds + (rank >> 7), -1)
            mask = high_rows == place
            placed = jnp.concatenate(
                [jnp.where(mask, coarse, 0.0), jnp.where(mask, fine, 0.0)], axis=0
            ).astype(bf16)
            at_rank = jnp.where(low_rows == (rank & 127), 1.0, 0.0).astype(bf16)
            total = total + lax.dot_general(placed, at_rank, nt_dims, preferred_element_type=f32)
    requests = (total[: owners * thirds] * 128.0 + total[owners * thirds :]).astype(i32) - 1
    for owner in range(owners):
        for third in range(thirds):
            row = owner * thirds + third
            requests_ref[owner, :, third * 128 : third * 128 + 128] = requests[row : row + 1]


def lookup_kernel(asked_ref, table_ref, third_ref, found_ref, pick_ref, *, group):
    askers, _, capacity = asked_ref.shape
    rows = table_ref.shape[0] // fields
    width = group * capacity
    steps = askers // group
    low_rows = lax.broadcasted_iota(i32, (256, width), 0)
    high_rows = lax.broadcasted_iota(i32, (rows, width), 0)

    def asked_of(part):
        return jnp.concatenate([asked_ref[group * part + k] for k in range(group)], axis=1)

    def prepare(part):
        pick_ref[part % 2] = jnp.where(low_rows == (asked_of(part) & 255), 1.0, 0.0).astype(bf16)

    def multiply(part):
        pick = pick_ref[part % 2]
        result = jnp.dot(
            table_ref[...], jnp.concatenate([pick, pick], axis=0), preferred_element_type=f32
        )
        third = jnp.dot(third_ref[...], pick, preferred_element_type=f32)
        return result, third

    def choose(part, result, third):
        mask = high_rows == (asked_of(part) >> 8)
        for field in range(fields):
            values = result[field * rows : (field + 1) * rows]
            if field < 2:
                values = values + third[field * rows : (field + 1) * rows]
            found = jnp.sum(jnp.where(mask, values, 0.0), axis=0, keepdims=True)
            for k in range(group):
                found_ref[group * part + k, :, field * capacity : (field + 1) * capacity] = found[
                    :, k * capacity : (k + 1) * capacity
                ]

    prepare(0)
    for part in range(steps):
        result, third = multiply(part)
        if part + 1 < steps:
            prepare(part + 1)
        choose(part, result, third)


def collect_kernel(camera_ref, place_ref, asked_ref, returned_ref, *rest, rows, group):
    *sums_refs, total_ref, pick_ref, placed_ref = rest
    askers, _, capacity = asked_ref.shape
    views = len(sums_refs)
    width = group * capacity
    steps = askers // group
    low_rows = lax.broadcasted_iota(i32, (256, width), 0)
    high_rows = lax.broadcasted_iota(i32, (rows, width), 0)

    def prepare(part):
        at = part % 2
        asked = jnp.concatenate([asked_ref[group * part + k] for k in range(group)], axis=1)
        pick_ref[at] = jnp.where(low_rows == (asked & 255), 1.0, 0.0).astype(bf16)
        mask = high_rows == (asked >> 8)
        for field in range(fields):
            values = jnp.concatenate(
                [
                    returned_ref[group * part + k, :, field * capacity : (field + 1) * capacity]
                    for k in range(group)
                ],
                axis=1,
            )
            upper = values.astype(bf16).astype(f32)
            row = field * rows
            placed_ref[at, row : row + rows, :width] = jnp.where(mask, upper, 0.0).astype(bf16)
            placed_ref[at, row : row + rows, width:] = jnp.where(mask, values - upper, 0.0).astype(bf16)

    def multiply(part):
        at = part % 2
        pick = pick_ref[at]
        return lax.dot_general(
            placed_ref[at], jnp.concatenate([pick, pick], axis=1), nt_dims, preferred_element_type=f32
        )

    prepare(0)
    for part in range(steps):
        product = multiply(part)
        if part + 1 < steps:
            prepare(part + 1)
        total_ref[...] = product if part == 0 else total_ref[...] + product

    part_rows = rows // views
    for offset, sums_ref in enumerate(sums_refs):
        view = lax.rem(place_ref[0] + offset, views)
        for field in range(fields):
            at = pl.multiple_of(field * rows + view * part_rows, part_rows)
            sums_ref[field * part_rows : (field + 1) * part_rows, :] = total_ref[pl.ds(at, part_rows), :]
        for entry in range(8):
            at = fields * part_rows + entry
            sums_ref[at : at + 1, :] = jnp.full((1, 256), camera_ref[entry], f32)


def collect_scratch(group, rows, capacity):
    return [
        pltpu.VMEM((fields * rows, 256), f32),
        pltpu.VMEM((2, 256, group * capacity), bf16),
        pltpu.VMEM((2, fields * rows, 2 * group * capacity), bf16),
    ]


def pull_kernel(*refs):
    *sums_refs, params_ref, grads_ref = refs
    channels, part_rows, _ = params_ref.shape
    gauss_rows = [params_ref[channel] for channel in range(channels)]
    totals = None
    for sums_ref in sums_refs:
        at = fields * part_rows
        camera_row = [
            jnp.broadcast_to(sums_ref[at + entry : at + entry + 1, :], (part_rows, 256))
            for entry in range(5)
        ]
        _, pull = jax.vjp(lambda rows_in: project(rows_in, camera_row, 0.0, 0.0), gauss_rows)
        (one,) = pull(
            tuple(
                sums_ref[field * part_rows : (field + 1) * part_rows, :]
                for field in range(fields)
            )
        )
        totals = one if totals is None else [x + y for x, y in zip(totals, one)]
    for channel in range(channels):
        for row in range(part_rows):
            grads_ref[channel : channel + 1, row * 256 : row * 256 + 256] = totals[channel][
                row : row + 1
            ]


def monomial(index, pix_x, pix_y):
    pix_x = pix_x.astype(f32) - 7.5
    pix_y = pix_y.astype(f32) - 7.5
    values = jnp.where(index == 0, 1.0, 0.0)
    values = jnp.where(index == 1, pix_x, values)
    values = jnp.where(index == 2, pix_y, values)
    values = jnp.where(index == 3, pix_x * pix_x, values)
    values = jnp.where(index == 4, pix_x * pix_y, values)
    return jnp.where(index == 5, pix_y * pix_y, values)


def render_kernel(
    counts_ref,
    place_ref,
    lists_ref,
    rank_ref,
    fetched_ref,
    d_image_ref,
    image_ref,
    outgoing_ref,
    item_ref,
    rows_ref,
    fetch_ref,
    value_ref,
    polynomial_ref,
    color_rows_ref,
    color_left_ref,
    d_columns_ref,
    d_left_ref,
    earlier_ref,
    later_ref,
    picture_ref,
    blend_ref,
    ratio_ref,
    color_grad_ref,
    placed_ref,
    at_rank_ref,
    outgo_ref,
    *,
    shift,
):
    tiles, slots = lists_ref.shape
    owners, _, width = fetched_ref.shape
    capacity = width // fields
    spare = tiles * slots // 256
    pixels = d_image_ref.shape[2]

    def list_tile(tile, base):
        live_blocks = (counts_ref[tile] + 255) // 256

        def list_block(block, carry):
            item_ref[0, base + block] = tile
            item_ref[1, base + block] = block
            item_ref[2, base + block] = base + live_blocks - 1 - block
            return carry

        lax.fori_loop(0, live_blocks, list_block, 0)
        return base + live_blocks

    items = lax.fori_loop(0, tiles, list_tile, 0)
    for owner in range(owners):
        for field in range(fields):
            row = field * owners + owner
            rows_ref[row : row + 1, :] = fetched_ref[owner, :, field * capacity : (field + 1) * capacity]
    center_v = place_ref[0].astype(f32) * 16.0 + 8.0
    for field in range(fields):
        values = rows_ref[field * owners : (field + 1) * owners, :]
        if field == 1:
            values = values - center_v
        upper, lower = split_two(values)
        fetch_ref[field * owners : (field + 1) * owners, :capacity] = upper
        fetch_ref[field * owners : (field + 1) * owners, capacity:] = lower
    for tile in range(tiles):
        d_rows = d_image_ref[tile]
        d_upper, d_lower = [piece.astype(f32) for piece in split_two(d_rows)]
        d_stack = jnp.concatenate([d_upper, d_lower, d_upper, d_lower, jnp.zeros((4, pixels), f32)], axis=0)
        d_columns_ref[tile] = jnp.transpose(d_stack).astype(bf16)
        d_left_ref[tile] = jnp.concatenate([d_upper, d_lower, jnp.zeros((10, pixels), f32)], axis=0).astype(bf16)
    outgo_ref[...] = jnp.zeros_like(outgo_ref)
    placed_ref[spare] = jnp.zeros(placed_ref.shape[1:], bf16)
    at_rank_ref[spare] = jnp.zeros(at_rank_ref.shape[1:], bf16)
    row_index = lax.broadcasted_iota(i32, (256, 256), 0)
    lane_index = lax.broadcasted_iota(i32, (256, 256), 1)
    before = (row_index < lane_index).astype(f32).astype(bf16)
    after = (row_index > lane_index).astype(f32).astype(bf16)
    pixel_row = lax.broadcasted_iota(i32, (pixels, 24), 0)
    monomials = monomial(
        lax.broadcasted_iota(i32, (pixels, 24), 1) & 7, pixel_row & 15, pixel_row >> 4
    ).astype(bf16)
    pixel_lane = lax.broadcasted_iota(i32, (16, pixels), 1)
    moments_of = monomial(
        lax.broadcasted_iota(i32, (16, pixels), 0), pixel_lane & 15, pixel_lane >> 4
    ).astype(bf16)
    rank_rows = lax.broadcasted_iota(i32, (capacity, 256), 0)
    owner_rows = lax.broadcasted_iota(i32, (owners, 256), 0)

    def owner_and_rank(item):
        tile = item_ref[0, item]
        at = pl.multiple_of(item_ref[1, item] * 256, 256)
        owner = lists_ref[pl.ds(tile, 1), pl.ds(at, 256)] >> shift
        rank = rank_ref[pl.ds(tile, 1), pl.ds(at, 256)]
        return owner, rank

    def fetch(item):
        owner, rank = owner_and_rank(item)
        tile = item_ref[0, item]
        at_rank = jnp.where(rank_rows == rank, 1.0, 0.0).astype(bf16)
        at_rank_ref[item] = at_rank
        yield
        fetched = jnp.dot(
            fetch_ref[...], jnp.concatenate([at_rank, at_rank], axis=0), preferred_element_type=f32
        )
        mask = owner_rows == owner
        found = []
        for field in range(fields):
            if field in (0, 5):
                yield
            values = fetched[field * owners : (field + 1) * owners]
            found.append(jnp.sum(jnp.where(mask, values, 0.0), axis=0, keepdims=True))
        yield
        pos_u = found[0] - (tile.astype(f32) * 16.0 + 8.0)
        pos_v = found[1]
        coef_a, coef_b, coef_c, log_opacity = found[2:6]
        log_opacity = jnp.where(rank >= 0, log_opacity, -1.0e4)
        slope_u = coef_a * pos_u * 2.0 + coef_b * pos_v
        slope_v = coef_c * pos_v * 2.0 + coef_b * pos_u
        constant = log_opacity + 0.5 * (slope_u * pos_u + slope_v * pos_v)
        blank = jnp.zeros((3, 256), f32)
        value_ref[item] = jnp.concatenate([pos_u, pos_v, coef_a, coef_b, coef_c, blank], axis=0)
        polynomial = jnp.concatenate(
            [constant, -slope_u, -slope_v, coef_a, coef_b, coef_c, blank[0:2]], axis=0
        )
        pieces = [piece.astype(f32) for piece in split_three(polynomial)]
        polynomial_ref[item] = jnp.concatenate(pieces, axis=0).astype(bf16)
        upper, lower = [piece.astype(f32) for piece in split_two(jnp.concatenate(found[6:9], axis=0))]
        color_rows_ref[item] = jnp.concatenate(
            [upper, upper, lower, lower, jnp.zeros((4, 256), f32)], axis=0
        ).astype(bf16)
        color_left_ref[item] = jnp.concatenate(
            [upper, lower, jnp.zeros((10, 256), f32)], axis=0
        ).astype(bf16)
        yield

    def forward(item):
        live = item >= 0
        at = jnp.where(live, item, spare)
        item = jnp.maximum(item, 0)
        tile = item_ref[0, item]
        first = item_ref[1, item] == 0
        exponent = jnp.dot(monomials, polynomial_ref[at], preferred_element_type=f32)
        yield
        earlier = jnp.where(first, 0.0, earlier_ref[...])
        earlier = jnp.concatenate([earlier, earlier], axis=1)
        alpha = jnp.exp2(exponent)
        keep = 1.0 - alpha
        log_keep = jnp.log2(keep)
        upper, lower = split_two(log_keep)
        yield
        within = jnp.dot(upper, before, preferred_element_type=f32) + jnp.dot(
            lower, before, preferred_element_type=f32
        )
        pull = jnp.dot(d_columns_ref[tile], color_rows_ref[at], preferred_element_type=f32)
        yield
        within = within + earlier
        weight = jnp.exp2(within) * alpha
        earlier_ref[...] = jnp.broadcast_to(within[:, 255:256] + log_keep[:, 255:256], (pixels, 128))
        blend_ref[at] = weight * pull
        ratio_ref[at] = alpha / keep
        upper, lower = split_two(weight)
        yield
        d_left = d_left_ref[tile]
        one = jnp.dot(d_left, upper, preferred_element_type=f32)
        two = jnp.dot(d_left, lower, preferred_element_type=f32)
        color_grad_ref[at, 0:3] = one[0:3] + one[3:6] + two[0:3]
        color_left = color_left_ref[at]
        one = lax.dot_general(color_left, upper, nt_dims, preferred_element_type=f32)
        two = lax.dot_general(color_left, lower, nt_dims, preferred_element_type=f32)
        picture = one[0:3] + one[3:6] + two[0:3]
        at_tile = jnp.where(live, tile, tiles)
        picture_ref[at_tile, 0:3] = jnp.where(first, 0.0, picture_ref[at_tile, 0:3]) + picture
        yield

    def backward(step):
        step = jnp.minimum(step, items)
        live = step < items
        at = jnp.where(live, item_ref[2, jnp.minimum(step, items - 1)], spare)
        item = jnp.where(live, at, 0)
        first = item_ref[1, jnp.minimum(step, items - 1)] == 0
        owner, rank = owner_and_rank(item)
        blend = blend_ref[at]
        upper, lower = split_two(blend)
        within = jnp.dot(upper, after, preferred_element_type=f32) + jnp.dot(
            lower, after, preferred_element_type=f32
        )
        yield
        later = jnp.where(first, 0.0, later_ref[...])
        within = within + jnp.concatenate([later, later], axis=1)
        later_ref[...] = jnp.broadcast_to(within[:, 0:1] + blend[:, 0:1], (pixels, 128))
        gradient = blend - within * ratio_ref[at]
        pieces = split_two(gradient)
        yield
        moments = (
            jnp.dot(moments_of, pieces[0], preferred_element_type=f32)
            + jnp.dot(moments_of, pieces[1], preferred_element_type=f32)
        ) * ln_2
        yield
        plain, first_x, first_y = moments[0:1], moments[1:2], moments[2:3]
        pos_u, pos_v, coef_a, coef_b, coef_c = (value_ref[at, k : k + 1] for k in range(5))
        from_u = first_x - pos_u * plain
        from_v = first_y - pos_v * plain
        outputs = [
            -2.0 * coef_a * from_u - coef_b * from_v,
            -2.0 * coef_c * from_v - coef_b * from_u,
            moments[3:4] - pos_u * (first_x + from_u),
            moments[4:5] - pos_v * first_x - pos_u * from_v,
            moments[5:6] - pos_v * (first_y + from_v),
            plain,
        ] + [color_grad_ref[at, k : k + 1] for k in range(3)]
        mask = owner_rows == jnp.where(rank >= 0, owner, -1)
        for field, values in enumerate(outputs):
            upper = values.astype(bf16).astype(f32)
            row = field * owners
            placed_ref[at, row : row + owners, :256] = jnp.where(mask, upper, 0.0).astype(bf16)
            placed_ref[at, row : row + owners, 256:] = jnp.where(mask, values - upper, 0.0).astype(bf16)
        yield

    def send(item):
        at = jnp.where(item < 0, spare, item)
        outgo_ref[...] += lax.dot_general(
            placed_ref[at],
            jnp.concatenate([at_rank_ref[at], at_rank_ref[at]], axis=1),
            nt_dims,
            preferred_element_type=f32,
        )
        yield

    def send_step(step):
        return send(jnp.where(step < 0, -1, item_ref[2, jnp.maximum(step, 0)]))

    lag = 6

    def run(order, **stages):
        for name in order:
            next(stages[name])
        for left in stages.values():
            for _ in left:
                raise ValueError(order)

    def ramp_up(step, carry):
        run("mfmmffmfmf", m=forward(step - 1), f=fetch(step))
        return carry

    def steady(step, carry):
        run(
            "mbmsfmbfmfbmbff",
            s=send_step(step - lag - 1),
            b=backward(step - lag),
            m=forward(step - 1),
            f=fetch(step),
        )
        return carry

    def ramp_down(step, carry):
        run("bsbbb", s=send_step(step - lag - 1), b=backward(step - lag))
        return carry

    lax.fori_loop(0, lag, ramp_up, 0)
    lax.fori_loop(lag, items, steady, 0)
    run("mbsmmbmbmb", s=send_step(items - lag - 1), b=backward(items - lag), m=forward(items - 1))
    lax.fori_loop(items + 1, items + lag + 1, ramp_down, 0)
    for tile in range(tiles):
        image_ref[tile] = picture_ref[tile, 0:3]
    for owner in range(owners):
        for field in range(fields):
            row = field * owners + owner
            outgoing_ref[owner, :, field * capacity : (field + 1) * capacity] = outgo_ref[row : row + 1, :]


def render_call(counts, tile_row, lists, rank, fetched, d_image, shift):
    owners, _, width = fetched.shape
    capacity = width // fields
    tiles, slots = lists.shape
    pixels = d_image.shape[2]
    kept = tiles * slots // 256 + 1
    smem = pl.BlockSpec(memory_space=pltpu.SMEM)
    vmem = pl.BlockSpec(memory_space=pltpu.VMEM)
    return pl.pallas_call(
        functools.partial(render_kernel, shift=shift),
        out_shape=(
            jax.ShapeDtypeStruct((tiles, 3, pixels), f32),
            jax.ShapeDtypeStruct((owners, 1, fields * capacity), f32),
        ),
        in_specs=[smem, smem, vmem, vmem, vmem, vmem],
        out_specs=(vmem, vmem),
        scratch_shapes=[
            pltpu.SMEM((3, kept), i32),
            pltpu.VMEM((fields * owners, capacity), f32),
            pltpu.VMEM((fields * owners, 2 * capacity), bf16),
            pltpu.VMEM((kept, 8, 256), f32),
            pltpu.VMEM((kept, 24, 256), bf16),
            pltpu.VMEM((kept, 16, 256), bf16),
            pltpu.VMEM((kept, 16, 256), bf16),
            pltpu.VMEM((tiles, pixels, 16), bf16),
            pltpu.VMEM((tiles, 16, pixels), bf16),
            pltpu.VMEM((pixels, 128), f32),
            pltpu.VMEM((pixels, 128), f32),
            pltpu.VMEM((tiles + 1, 8, pixels), f32),
            pltpu.VMEM((kept, pixels, 256), f32),
            pltpu.VMEM((kept, pixels, 256), f32),
            pltpu.VMEM((kept, 8, 256), f32),
            pltpu.VMEM((kept, fields * owners, 512), bf16),
            pltpu.VMEM((kept, capacity, 256), bf16),
            pltpu.VMEM((fields * owners, capacity), f32),
        ],
        compiler_params=pltpu.CompilerParams(vmem_limit_bytes=render_vmem_bytes),
        name="render",
    )(counts, tile_row, lists, rank, fetched, d_image)


def body(params, camera, tile_lists, tile_counts, d_image):
    owners = lax.axis_size("tiles")
    views = lax.axis_size("views")
    channels, shard_size = params.shape
    shift = shard_size.bit_length() - 1
    tiles, slots = tile_lists.shape[1:]
    pixels = d_image.shape[3]
    capacity = 3 * tiles * slots // (2 * owners)
    rows = shard_size // 256
    part_rows = rows // views
    center = jnp.array([tiles * 8.0, owners * 8.0, 0.0], f32)
    camera_row = jnp.concatenate([jnp.cos(camera[0, :1]), jnp.sin(camera[0, :1]), camera[0, 1:4], center])
    counts = tile_counts[0]
    lists = tile_lists[0]
    tile_row = lax.axis_index("tiles").astype(i32).reshape(1)
    view_here = lax.axis_index("views").astype(i32).reshape(1)
    smem = pl.BlockSpec(memory_space=pltpu.SMEM)
    vmem = pl.BlockSpec(memory_space=pltpu.VMEM)

    def settings(mebibytes):
        return pltpu.CompilerParams(vmem_limit_bytes=mebibytes * 1024 * 1024)

    requests, rank = pl.pallas_call(
        functools.partial(bucket_kernel, owners=owners, capacity=capacity, shift=shift),
        out_shape=(
            jax.ShapeDtypeStruct((owners, 1, capacity), i32),
            jax.ShapeDtypeStruct((tiles, slots), i32),
        ),
        in_specs=[smem, vmem],
        out_specs=(vmem, vmem),
        scratch_shapes=[
            pltpu.VMEM((tiles * slots // 256 * owners, 256), bf16),
            pltpu.VMEM((tiles * slots // 256 * owners, 256), f32),
        ],
        compiler_params=settings(56),
        name="bucket",
    )(counts, lists)
    asked = lax.all_to_all(requests, "tiles", split_axis=0, concat_axis=0, tiled=True)
    table, third, part_params = pl.pallas_call(
        project_kernel,
        out_shape=(
            jax.ShapeDtypeStruct((fields * rows, 512), bf16),
            jax.ShapeDtypeStruct((2 * rows, 256), bf16),
            jax.ShapeDtypeStruct((channels, part_rows, 256), f32),
        ),
        in_specs=[smem, smem, vmem],
        out_specs=(vmem, vmem, vmem),
        scratch_shapes=[pltpu.VMEM((channels, rows, 256), f32)],
        compiler_params=settings(16),
        name="project",
    )(camera_row, view_here, params)
    found = pl.pallas_call(
        functools.partial(lookup_kernel, group=2),
        out_shape=jax.ShapeDtypeStruct((owners, 1, fields * capacity), f32),
        in_specs=[vmem, vmem, vmem],
        out_specs=vmem,
        scratch_shapes=[pltpu.VMEM((2, 256, 2 * capacity), bf16)],
        compiler_params=settings(16),
        name="lookup",
    )(asked, table, third)
    fetched = lax.all_to_all(found, "tiles", split_axis=0, concat_axis=0, tiled=True)
    picture, outgoing = render_call(counts, tile_row, lists, rank, fetched, d_image[0], shift)
    returned = lax.all_to_all(outgoing, "tiles", split_axis=0, concat_axis=0, tiled=True)
    sums = pl.pallas_call(
        functools.partial(collect_kernel, rows=rows, group=2),
        out_shape=[jax.ShapeDtypeStruct((fields * part_rows + 8, 256), f32)] * views,
        in_specs=[smem, smem, vmem, vmem],
        out_specs=[vmem] * views,
        scratch_shapes=collect_scratch(2, rows, capacity),
        compiler_params=settings(16),
        name="collect",
    )(camera_row, view_here, asked, returned)
    all_sums = [sums[0]] + [
        lax.ppermute(sums[offset], "views", [(view, (view + offset) % views) for view in range(views)])
        for offset in range(1, views)
    ]
    grads = pl.pallas_call(
        pull_kernel,
        out_shape=jax.ShapeDtypeStruct((channels, part_rows * 256), f32),
        in_specs=[vmem] * (views + 1),
        out_specs=vmem,
        compiler_params=settings(16),
        name="pull",
    )(*all_sums, part_params)
    return picture[None], grads


def solution(mesh):
    placed = (
        P(None, "tiles"),
        P("views", None),
        P("views", "tiles", None),
        P("views", "tiles"),
        P("views", "tiles", None, None),
    )
    return jax.shard_map(
        body,
        mesh=mesh,
        in_specs=placed,
        out_specs=(P("views", "tiles", None, None), P(None, ("tiles", "views"))),
        check_vma=False,
    )
```

```python
import functools
import math

import jax
import jax.numpy as jnp
from jax import lax
from jax.experimental import pallas as pl
from jax.experimental.pallas import tpu as pltpu
from jax.sharding import PartitionSpec as P

focal_px = 600.0
lowpass = 0.3
harmonic_zero = 0.28209479177387814
harmonic_one = 0.4886025119029199
harmonic_two = (
    1.0925484305920792,
    -1.0925484305920792,
    0.31539156525252005,
    -1.0925484305920792,
    0.5462742152960396,
)
harmonic_three = (
    -0.5900435899266435,
    2.890611442640554,
    -0.4570457994644658,
    0.3731763325901154,
    -0.4570457994644658,
    1.445305721320277,
    -0.5900435899266435,
)
bf16 = jnp.bfloat16
f32 = jnp.float32
i32 = jnp.int32
log2_e = 1.0 / math.log(2.0)
ln_2 = math.log(2.0)
nt_dims = (((1,), (1,)), ((), ()))
render_vmem_bytes = 36 * 1024 * 1024
fields = 9


def split_two(values):
    upper = values.astype(bf16)
    lower = (values - upper.astype(f32)).astype(bf16)
    return upper, lower


def split_three(values):
    upper = values.astype(bf16)
    rest = values - upper.astype(f32)
    middle = rest.astype(bf16)
    lower = (rest - middle.astype(f32)).astype(bf16)
    return upper, middle, lower


def project(gauss_rows, camera_row, center_x, center_y):
    cosine, sine_val, shift_x, shift_y, shift_z = camera_row
    cam_x = cosine * gauss_rows[0] + sine_val * gauss_rows[2] + shift_x
    cam_y = gauss_rows[1] + shift_y
    cam_z = cosine * gauss_rows[2] - sine_val * gauss_rows[0] + shift_z
    inverse_z = 1.0 / cam_z
    jac_a = focal_px * inverse_z
    pos_u = jac_a * cam_x + center_x
    pos_v = jac_a * cam_y + center_y
    jac_b = -jac_a * cam_x * inverse_z
    jac_c = -jac_a * cam_y * inverse_z
    first_row = (jac_a * cosine - jac_b * sine_val, jac_a * sine_val + jac_b * cosine)
    second_row = (-jac_c * sine_val, jac_a, jac_c * cosine)
    quaternion = gauss_rows[6:10]
    inv_norm = lax.rsqrt(
        quaternion[0] * quaternion[0]
        + quaternion[1] * quaternion[1]
        + quaternion[2] * quaternion[2]
        + quaternion[3] * quaternion[3]
    )
    quat_w, quat_x, quat_y, quat_z = (entry * inv_norm for entry in quaternion)
    rotation = (
        (
            1.0 - 2.0 * (quat_y * quat_y + quat_z * quat_z),
            2.0 * (quat_x * quat_y - quat_w * quat_z),
            2.0 * (quat_x * quat_z + quat_w * quat_y),
        ),
        (
            2.0 * (quat_x * quat_y + quat_w * quat_z),
            1.0 - 2.0 * (quat_x * quat_x + quat_z * quat_z),
            2.0 * (quat_y * quat_z - quat_w * quat_x),
        ),
        (
            2.0 * (quat_x * quat_z - quat_w * quat_y),
            2.0 * (quat_y * quat_z + quat_w * quat_x),
            1.0 - 2.0 * (quat_x * quat_x + quat_y * quat_y),
        ),
    )
    scales = [jnp.exp(entry) for entry in gauss_rows[3:6]]
    upper_a = [
        (first_row[0] * rotation[0][entry] + first_row[1] * rotation[2][entry]) * scales[entry]
        for entry in range(3)
    ]
    lower_a = [
        (
            second_row[0] * rotation[0][entry]
            + second_row[1] * rotation[1][entry]
            + second_row[2] * rotation[2][entry]
        )
        * scales[entry]
        for entry in range(3)
    ]
    cov_a = upper_a[0] * upper_a[0] + upper_a[1] * upper_a[1] + upper_a[2] * upper_a[2] + lowpass
    cov_b = upper_a[0] * lower_a[0] + upper_a[1] * lower_a[1] + upper_a[2] * lower_a[2]
    cov_c = lower_a[0] * lower_a[0] + lower_a[1] * lower_a[1] + lower_a[2] * lower_a[2] + lowpass
    inv_det = 1.0 / (cov_a * cov_c - cov_b * cov_b)
    coef_a = (-0.5 * log2_e) * cov_c * inv_det
    coef_b = log2_e * cov_b * inv_det
    coef_c = (-0.5 * log2_e) * cov_a * inv_det
    log_opacity = -log2_e * jnp.log(1.0 + jnp.exp(-gauss_rows[10]))
    dir_x = cosine * cam_x - sine_val * cam_z
    dir_y = cam_y
    dir_z = sine_val * cam_x + cosine * cam_z
    inv_len = lax.rsqrt(dir_x * dir_x + dir_y * dir_y + dir_z * dir_z)
    dir_x = dir_x * inv_len
    dir_y = dir_y * inv_len
    dir_z = dir_z * inv_len
    sq_x = dir_x * dir_x
    sq_y = dir_y * dir_y
    sq_z = dir_z * dir_z
    harmonics = (
        harmonic_zero,
        -harmonic_one * dir_y,
        harmonic_one * dir_z,
        -harmonic_one * dir_x,
        harmonic_two[0] * dir_x * dir_y,
        harmonic_two[1] * dir_y * dir_z,
        harmonic_two[2] * (2.0 * sq_z - sq_x - sq_y),
        harmonic_two[3] * dir_x * dir_z,
        harmonic_two[4] * (sq_x - sq_y),
        harmonic_three[0] * dir_y * (3.0 * sq_x - sq_y),
        harmonic_three[1] * dir_x * dir_y * dir_z,
        harmonic_three[2] * dir_y * (4.0 * sq_z - sq_x - sq_y),
        harmonic_three[3] * dir_z * (2.0 * sq_z - 3.0 * sq_x - 3.0 * sq_y),
        harmonic_three[4] * dir_x * (4.0 * sq_z - sq_x - sq_y),
        harmonic_three[5] * dir_z * (sq_x - sq_y),
        harmonic_three[6] * dir_x * (sq_x - 3.0 * sq_y),
    )
    colors = []
    for channel in range(3):
        total = harmonics[0] * gauss_rows[11 + channel] + 0.5
        for basis in range(1, 16):
            total = total + harmonics[basis] * gauss_rows[11 + 3 * basis + channel]
        colors.append(total)
    return (pos_u, pos_v, coef_a, coef_b, coef_c, log_opacity, *colors)


def project_kernel(camera_ref, place_ref, params_ref, table_ref, third_ref, part_ref, dense_ref):
    channels, rows, _ = dense_ref.shape
    part_rows = part_ref.shape[1]
    camera_row = [camera_ref[entry] for entry in range(5)]
    center_x, center_y = camera_ref[5], camera_ref[6]
    for channel in range(channels):
        for row in range(rows):
            dense_ref[channel, row : row + 1, :] = params_ref[channel : channel + 1, row * 256 : row * 256 + 256]

    def step(part, carry):
        at = pl.multiple_of(part * 16, 16)
        gauss_rows = [dense_ref[channel, pl.ds(at, 16), :] for channel in range(channels)]
        outputs = project(gauss_rows, camera_row, center_x, center_y)
        for field, values in enumerate(outputs):
            pieces = split_three(values)
            table_ref[pl.ds(field * rows + at, 16), :256] = pieces[0]
            table_ref[pl.ds(field * rows + at, 16), 256:] = pieces[1]
            if field < 2:
                third_ref[pl.ds(field * rows + at, 16), :] = pieces[2]
        return carry

    lax.fori_loop(0, rows // 16, step, 0)
    at = pl.multiple_of(place_ref[0] * part_rows, part_rows)
    for channel in range(channels):
        part_ref[channel] = dense_ref[channel, pl.ds(at, part_rows), :]


def bucket_kernel(counts_ref, lists_ref, requests_ref, rank_ref, hits_ref, earlier_ref, *, owners, capacity, shift):
    tiles, slots = lists_ref.shape
    blocks = slots // 256
    thirds = capacity // 128
    upper = (
        lax.broadcasted_iota(i32, (256, 256), 0) < lax.broadcasted_iota(i32, (256, 256), 1)
    ).astype(f32).astype(bf16)
    owner_rows = lax.broadcasted_iota(i32, (owners, 256), 0)
    lane = lax.broadcasted_iota(i32, (1, 256), 1)
    for tile in range(tiles):
        for block in range(blocks):
            ids = lists_ref[tile : tile + 1, block * 256 : block * 256 + 256]
            owner = jnp.where(lane + block * 256 < counts_ref[tile], ids >> shift, -1)
            at = (tile * blocks + block) * owners
            hits_ref[at : at + owners, :] = jnp.where(owner_rows == owner, 1.0, 0.0).astype(bf16)
    earlier_ref[...] = jnp.dot(hits_ref[...], upper, preferred_element_type=f32)
    low_rows = lax.broadcasted_iota(i32, (128, 256), 0)
    high_rows = lax.broadcasted_iota(i32, (owners * thirds, 256), 0)
    carry = jnp.zeros((owners, 1), f32)
    total = jnp.zeros((2 * owners * thirds, 128), f32)
    for tile in range(tiles):
        for block in range(blocks):
            at = (tile * blocks + block) * owners
            hits = hits_ref[at : at + owners, :].astype(f32)
            earlier = earlier_ref[at : at + owners, :]
            rank = jnp.sum(hits * (earlier + carry), axis=0, keepdims=True).astype(i32)
            live = lane + block * 256 < counts_ref[tile]
            rank_ref[tile : tile + 1, block * 256 : block * 256 + 256] = jnp.where(live, rank, -1)
            carry = carry + earlier[:, 255:256] + hits[:, 255:256]
            ids = lists_ref[tile : tile + 1, block * 256 : block * 256 + 256]
            local = (ids & ((1 << shift) - 1)) + 1
            coarse = (local >> 7).astype(f32)
            fine = (local & 127).astype(f32)
            place = jnp.where(live, (ids >> shift) * thirds + (rank >> 7), -1)
            mask = high_rows == place
            placed = jnp.concatenate(
                [jnp.where(mask, coarse, 0.0), jnp.where(mask, fine, 0.0)], axis=0
            ).astype(bf16)
            at_rank = jnp.where(low_rows == (rank & 127), 1.0, 0.0).astype(bf16)
            total = total + lax.dot_general(placed, at_rank, nt_dims, preferred_element_type=f32)
    requests = (total[: owners * thirds] * 128.0 + total[owners * thirds :]).astype(i32) - 1
    for owner in range(owners):
        for third in range(thirds):
            row = owner * thirds + third
            requests_ref[owner, :, third * 128 : third * 128 + 128] = requests[row : row + 1]


def rank_picks_kernel(rank_ref, at_rank_ref):
    kept, capacity, _ = at_rank_ref.shape
    blocks = rank_ref.shape[1] // 256
    rank_rows = lax.broadcasted_iota(i32, (capacity, 256), 0)

    def step(place, carry):
        at = pl.multiple_of(place % blocks * 256, 256)
        rank = rank_ref[pl.ds(place // blocks, 1), pl.ds(at, 256)]
        at_rank_ref[place] = jnp.where(rank_rows == rank, 1.0, 0.0).astype(bf16)
        return carry

    lax.fori_loop(0, kept - 1, step, 0)
    at_rank_ref[kept - 1] = jnp.zeros((capacity, 256), bf16)


def asked_picks_kernel(asked_ref, pick_ref, *, group):
    steps, _, width = pick_ref.shape
    low_rows = lax.broadcasted_iota(i32, (256, width), 0)

    def step(part, carry):
        asked = jnp.concatenate([asked_ref[group * part + k] for k in range(group)], axis=1)
        pick_ref[part] = jnp.where(low_rows == (asked & 255), 1.0, 0.0).astype(bf16)
        return carry

    lax.fori_loop(0, steps, step, 0)


def lookup_kernel(asked_ref, table_ref, third_ref, found_ref, pick_ref, *, group):
    askers, _, capacity = asked_ref.shape
    rows = table_ref.shape[0] // fields
    width = group * capacity
    steps = askers // group
    low_rows = lax.broadcasted_iota(i32, (256, width), 0)
    high_rows = lax.broadcasted_iota(i32, (rows, width), 0)

    def asked_of(part):
        return jnp.concatenate([asked_ref[group * part + k] for k in range(group)], axis=1)

    def prepare(part):
        pick_ref[part % 2] = jnp.where(low_rows == (asked_of(part) & 255), 1.0, 0.0).astype(bf16)

    def multiply(part):
        pick = pick_ref[part % 2]
        result = jnp.dot(
            table_ref[...], jnp.concatenate([pick, pick], axis=0), preferred_element_type=f32
        )
        third = jnp.dot(third_ref[...], pick, preferred_element_type=f32)
        return result, third

    def choose(part, result, third):
        mask = high_rows == (asked_of(part) >> 8)
        for field in range(fields):
            values = result[field * rows : (field + 1) * rows]
            if field < 2:
                values = values + third[field * rows : (field + 1) * rows]
            found = jnp.sum(jnp.where(mask, values, 0.0), axis=0, keepdims=True)
            for k in range(group):
                found_ref[group * part + k, :, field * capacity : (field + 1) * capacity] = found[
                    :, k * capacity : (k + 1) * capacity
                ]

    prepare(0)
    for part in range(steps):
        result, third = multiply(part)
        if part + 1 < steps:
            prepare(part + 1)
        choose(part, result, third)


def collect_kernel(camera_ref, place_ref, asked_ref, pick_ref, returned_ref, *rest, rows, group):
    *sums_refs, total_ref, placed_ref = rest
    askers, _, capacity = asked_ref.shape
    views = len(sums_refs)
    width = group * capacity
    steps = askers // group
    high_rows = lax.broadcasted_iota(i32, (rows, width), 0)

    def prepare(part):
        at = part % 2
        asked = jnp.concatenate([asked_ref[group * part + k] for k in range(group)], axis=1)
        mask = high_rows == (asked >> 8)
        for field in range(fields):
            values = jnp.concatenate(
                [
                    returned_ref[group * part + k, :, field * capacity : (field + 1) * capacity]
                    for k in range(group)
                ],
                axis=1,
            )
            upper = values.astype(bf16).astype(f32)
            row = field * rows
            placed_ref[at, row : row + rows, :width] = jnp.where(mask, upper, 0.0).astype(bf16)
            placed_ref[at, row : row + rows, width:] = jnp.where(mask, values - upper, 0.0).astype(bf16)

    def multiply(part):
        at = part % 2
        pick = pick_ref[part]
        return lax.dot_general(
            placed_ref[at], jnp.concatenate([pick, pick], axis=1), nt_dims, preferred_element_type=f32
        )

    prepare(0)
    for part in range(steps):
        product = multiply(part)
        if part + 1 < steps:
            prepare(part + 1)
        total_ref[...] = product if part == 0 else total_ref[...] + product

    part_rows = rows // views
    for offset, sums_ref in enumerate(sums_refs):
        view = lax.rem(place_ref[0] + offset, views)
        for field in range(fields):
            at = pl.multiple_of(field * rows + view * part_rows, part_rows)
            sums_ref[field * part_rows : (field + 1) * part_rows, :] = total_ref[pl.ds(at, part_rows), :]
        for entry in range(8):
            at = fields * part_rows + entry
            sums_ref[at : at + 1, :] = jnp.full((1, 256), camera_ref[entry], f32)


def collect_scratch(group, rows, capacity):
    return [
        pltpu.VMEM((fields * rows, 256), f32),
        pltpu.VMEM((2, fields * rows, 2 * group * capacity), bf16),
    ]


def pull_kernel(*refs):
    *sums_refs, params_ref, grads_ref = refs
    channels, part_rows, _ = params_ref.shape
    gauss_rows = [params_ref[channel] for channel in range(channels)]
    totals = None
    for sums_ref in sums_refs:
        at = fields * part_rows
        camera_row = [
            jnp.broadcast_to(sums_ref[at + entry : at + entry + 1, :], (part_rows, 256))
            for entry in range(5)
        ]
        _, pull = jax.vjp(lambda rows_in: project(rows_in, camera_row, 0.0, 0.0), gauss_rows)
        (one,) = pull(
            tuple(
                sums_ref[field * part_rows : (field + 1) * part_rows, :]
                for field in range(fields)
            )
        )
        totals = one if totals is None else [x + y for x, y in zip(totals, one)]
    for channel in range(channels):
        for row in range(part_rows):
            grads_ref[channel : channel + 1, row * 256 : row * 256 + 256] = totals[channel][
                row : row + 1
            ]


def monomial(index, pix_x, pix_y):
    pix_x = pix_x.astype(f32) - 7.5
    pix_y = pix_y.astype(f32) - 7.5
    values = jnp.where(index == 0, 1.0, 0.0)
    values = jnp.where(index == 1, pix_x, values)
    values = jnp.where(index == 2, pix_y, values)
    values = jnp.where(index == 3, pix_x * pix_x, values)
    values = jnp.where(index == 4, pix_x * pix_y, values)
    return jnp.where(index == 5, pix_y * pix_y, values)


def render_kernel(
    counts_ref,
    place_ref,
    lists_ref,
    rank_ref,
    at_rank_ref,
    fetched_ref,
    d_image_ref,
    image_ref,
    outgoing_ref,
    item_ref,
    rows_ref,
    fetch_ref,
    value_ref,
    polynomial_ref,
    color_rows_ref,
    color_left_ref,
    d_columns_ref,
    d_left_ref,
    earlier_ref,
    later_ref,
    blend_ref,
    ratio_ref,
    color_grad_ref,
    placed_ref,
    outgo_ref,
    *,
    shift,
):
    tiles, slots = lists_ref.shape
    owners, _, width = fetched_ref.shape
    capacity = width // fields
    spare = tiles * slots // 256
    pixels = d_image_ref.shape[2]

    def list_tile(tile, base):
        live_blocks = (counts_ref[tile] + 255) // 256

        def list_block(block, carry):
            item_ref[0, base + block] = tile
            item_ref[1, base + block] = block
            item_ref[2, base + block] = base + live_blocks - 1 - block
            return carry

        lax.fori_loop(0, live_blocks, list_block, 0)
        return base + live_blocks

    items = lax.fori_loop(0, tiles, list_tile, 0)
    for owner in range(owners):
        for field in range(fields):
            row = field * owners + owner
            rows_ref[row : row + 1, :] = fetched_ref[owner, :, field * capacity : (field + 1) * capacity]
    center_v = place_ref[0].astype(f32) * 16.0 + 8.0
    for field in range(fields):
        values = rows_ref[field * owners : (field + 1) * owners, :]
        if field == 1:
            values = values - center_v
        upper, lower = split_two(values)
        fetch_ref[field * owners : (field + 1) * owners, :capacity] = upper
        fetch_ref[field * owners : (field + 1) * owners, capacity:] = lower
    for tile in range(tiles):
        d_rows = d_image_ref[tile]
        d_upper, d_lower = [piece.astype(f32) for piece in split_two(d_rows)]
        d_stack = jnp.concatenate([d_upper, d_lower, d_upper, d_lower, jnp.zeros((4, pixels), f32)], axis=0)
        d_columns_ref[tile] = jnp.transpose(d_stack).astype(bf16)
        d_left_ref[tile] = jnp.concatenate([d_upper, d_lower, jnp.zeros((10, pixels), f32)], axis=0).astype(bf16)
    outgo_ref[...] = jnp.zeros_like(outgo_ref)
    placed_ref[spare] = jnp.zeros(placed_ref.shape[1:], bf16)
    blocks = slots // 256
    row_index = lax.broadcasted_iota(i32, (256, 256), 0)
    lane_index = lax.broadcasted_iota(i32, (256, 256), 1)
    before = (row_index < lane_index).astype(f32).astype(bf16)
    after = (row_index > lane_index).astype(f32).astype(bf16)
    pixel_row = lax.broadcasted_iota(i32, (pixels, 24), 0)
    monomials = monomial(
        lax.broadcasted_iota(i32, (pixels, 24), 1) & 7, pixel_row & 15, pixel_row >> 4
    ).astype(bf16)
    pixel_lane = lax.broadcasted_iota(i32, (16, pixels), 1)
    moments_of = monomial(
        lax.broadcasted_iota(i32, (16, pixels), 0), pixel_lane & 15, pixel_lane >> 4
    ).astype(bf16)
    owner_rows = lax.broadcasted_iota(i32, (owners, 256), 0)

    def place_of(item):
        return item_ref[0, item] * blocks + item_ref[1, item]

    def owner_and_rank(item):
        tile = item_ref[0, item]
        at = pl.multiple_of(item_ref[1, item] * 256, 256)
        owner = lists_ref[pl.ds(tile, 1), pl.ds(at, 256)] >> shift
        rank = rank_ref[pl.ds(tile, 1), pl.ds(at, 256)]
        return owner, rank

    def fetch(item):
        owner, rank = owner_and_rank(item)
        tile = item_ref[0, item]
        at_rank = at_rank_ref[place_of(item)]
        yield
        fetched = jnp.dot(
            fetch_ref[...], jnp.concatenate([at_rank, at_rank], axis=0), preferred_element_type=f32
        )
        mask = owner_rows == owner
        found = []
        for field in range(fields):
            if field in (0, 5):
                yield
            values = fetched[field * owners : (field + 1) * owners]
            found.append(jnp.sum(jnp.where(mask, values, 0.0), axis=0, keepdims=True))
        yield
        pos_u = found[0] - (tile.astype(f32) * 16.0 + 8.0)
        pos_v = found[1]
        coef_a, coef_b, coef_c, log_opacity = found[2:6]
        log_opacity = jnp.where(rank >= 0, log_opacity, -1.0e4)
        slope_u = coef_a * pos_u * 2.0 + coef_b * pos_v
        slope_v = coef_c * pos_v * 2.0 + coef_b * pos_u
        constant = log_opacity + 0.5 * (slope_u * pos_u + slope_v * pos_v)
        blank = jnp.zeros((3, 256), f32)
        value_ref[item] = jnp.concatenate([pos_u, pos_v, coef_a, coef_b, coef_c, blank], axis=0)
        polynomial = jnp.concatenate(
            [constant, -slope_u, -slope_v, coef_a, coef_b, coef_c, blank[0:2]], axis=0
        )
        pieces = [piece.astype(f32) for piece in split_three(polynomial)]
        polynomial_ref[item] = jnp.concatenate(pieces, axis=0).astype(bf16)
        upper, lower = [piece.astype(f32) for piece in split_two(jnp.concatenate(found[6:9], axis=0))]
        color_rows_ref[item] = jnp.concatenate(
            [upper, upper, lower, lower, jnp.zeros((4, 256), f32)], axis=0
        ).astype(bf16)
        color_left_ref[item] = jnp.concatenate(
            [upper, lower, jnp.zeros((10, 256), f32)], axis=0
        ).astype(bf16)
        yield

    def forward(item):
        at = item
        tile = item_ref[0, item]
        first = item_ref[1, item] == 0
        exponent = jnp.dot(monomials, polynomial_ref[at], preferred_element_type=f32)
        yield
        earlier = jnp.where(first, 0.0, earlier_ref[...])
        earlier = jnp.concatenate([earlier, earlier], axis=1)
        alpha = jnp.exp2(exponent)
        keep = 1.0 - alpha
        log_keep = jnp.log2(keep)
        upper, lower = split_two(log_keep)
        yield
        within = jnp.dot(upper, before, preferred_element_type=f32) + jnp.dot(
            lower, before, preferred_element_type=f32
        )
        pull = jnp.dot(d_columns_ref[tile], color_rows_ref[at], preferred_element_type=f32)
        yield
        within = within + earlier
        weight = jnp.exp2(within) * alpha
        earlier_ref[...] = jnp.broadcast_to(within[:, 255:256] + log_keep[:, 255:256], (pixels, 128))
        blend_ref[at] = weight * pull
        ratio_ref[at] = alpha / keep
        upper, lower = split_two(weight)
        yield
        d_left = d_left_ref[tile]
        one = jnp.dot(d_left, upper, preferred_element_type=f32)
        two = jnp.dot(d_left, lower, preferred_element_type=f32)
        color_grad_ref[at, 0:3] = one[0:3] + one[3:6] + two[0:3]
        color_left = color_left_ref[at]
        one = lax.dot_general(color_left, upper, nt_dims, preferred_element_type=f32)
        two = lax.dot_general(color_left, lower, nt_dims, preferred_element_type=f32)
        picture = one[0:3] + one[3:6] + two[0:3]
        image_ref[tile] = jnp.where(first, 0.0, image_ref[tile]) + picture
        yield

    def backward(step):
        at = item_ref[2, step]
        first = item_ref[1, step] == 0
        owner, rank = owner_and_rank(at)
        blend = blend_ref[at]
        upper, lower = split_two(blend)
        within = jnp.dot(upper, after, preferred_element_type=f32) + jnp.dot(
            lower, after, preferred_element_type=f32
        )
        yield
        later = jnp.where(first, 0.0, later_ref[...])
        within = within + jnp.concatenate([later, later], axis=1)
        later_ref[...] = jnp.broadcast_to(within[:, 0:1] + blend[:, 0:1], (pixels, 128))
        gradient = blend - within * ratio_ref[at]
        pieces = split_two(gradient)
        yield
        moments = (
            jnp.dot(moments_of, pieces[0], preferred_element_type=f32)
            + jnp.dot(moments_of, pieces[1], preferred_element_type=f32)
        ) * ln_2
        yield
        plain, first_x, first_y = moments[0:1], moments[1:2], moments[2:3]
        pos_u, pos_v, coef_a, coef_b, coef_c = (value_ref[at, k : k + 1] for k in range(5))
        from_u = first_x - pos_u * plain
        from_v = first_y - pos_v * plain
        outputs = [
            -2.0 * coef_a * from_u - coef_b * from_v,
            -2.0 * coef_c * from_v - coef_b * from_u,
            moments[3:4] - pos_u * (first_x + from_u),
            moments[4:5] - pos_v * first_x - pos_u * from_v,
            moments[5:6] - pos_v * (first_y + from_v),
            plain,
        ] + [color_grad_ref[at, k : k + 1] for k in range(3)]
        mask = owner_rows == jnp.where(rank >= 0, owner, -1)
        for field, values in enumerate(outputs):
            upper = values.astype(bf16).astype(f32)
            row = field * owners
            placed_ref[at, row : row + owners, :256] = jnp.where(mask, upper, 0.0).astype(bf16)
            placed_ref[at, row : row + owners, 256:] = jnp.where(mask, values - upper, 0.0).astype(bf16)
        yield

    def send(item):
        at = jnp.where(item < 0, spare, item)
        place = jnp.where(item < 0, spare, place_of(jnp.maximum(item, 0)))
        outgo_ref[...] += lax.dot_general(
            placed_ref[at],
            jnp.concatenate([at_rank_ref[place], at_rank_ref[place]], axis=1),
            nt_dims,
            preferred_element_type=f32,
        )
        yield

    def send_step(step):
        return send(jnp.where(step < 0, -1, item_ref[2, jnp.maximum(step, 0)]))

    lag = 5

    def run(order, **stages):
        for name in order:
            next(stages[name])
        for left in stages.values():
            for _ in left:
                raise ValueError(order)

    def ramp_up(step, carry):
        run("mfmmffmfmf", m=forward(step - 1), f=fetch(step))
        return carry

    def steady(step, carry):
        run(
            "bmmsfmbfmfbmbff",
            s=send_step(step - lag - 1),
            b=backward(step - lag),
            m=forward(step - 1),
            f=fetch(step),
        )
        return carry

    def ramp_down(step, carry):
        run("bsbbb", s=send_step(step - lag - 1), b=backward(step - lag))
        return carry

    run("fffff", f=fetch(0))
    lax.fori_loop(1, lag, ramp_up, 0)
    lax.fori_loop(lag, items, steady, 0)
    run("mbsmmbmbmb", s=send_step(items - lag - 1), b=backward(items - lag), m=forward(items - 1))
    lax.fori_loop(items + 1, items + lag, ramp_down, 0)
    run("s", s=send_step(items - 1))
    for owner in range(owners):
        for field in range(fields):
            row = field * owners + owner
            outgoing_ref[owner, :, field * capacity : (field + 1) * capacity] = outgo_ref[row : row + 1, :]


def render_call(counts, tile_row, lists, rank, at_rank, fetched, d_image, shift):
    owners, _, width = fetched.shape
    capacity = width // fields
    tiles, slots = lists.shape
    pixels = d_image.shape[2]
    kept = tiles * slots // 256 + 1
    smem = pl.BlockSpec(memory_space=pltpu.SMEM)
    vmem = pl.BlockSpec(memory_space=pltpu.VMEM)
    return pl.pallas_call(
        functools.partial(render_kernel, shift=shift),
        out_shape=(
            jax.ShapeDtypeStruct((tiles, 3, pixels), f32),
            jax.ShapeDtypeStruct((owners, 1, fields * capacity), f32),
        ),
        in_specs=[smem, smem, vmem, vmem, vmem, vmem, vmem],
        out_specs=(vmem, vmem),
        scratch_shapes=[
            pltpu.SMEM((3, kept), i32),
            pltpu.VMEM((fields * owners, capacity), f32),
            pltpu.VMEM((fields * owners, 2 * capacity), bf16),
            pltpu.VMEM((kept, 8, 256), f32),
            pltpu.VMEM((kept, 24, 256), bf16),
            pltpu.VMEM((kept, 16, 256), bf16),
            pltpu.VMEM((kept, 16, 256), bf16),
            pltpu.VMEM((tiles, pixels, 16), bf16),
            pltpu.VMEM((tiles, 16, pixels), bf16),
            pltpu.VMEM((pixels, 128), f32),
            pltpu.VMEM((pixels, 128), f32),
            pltpu.VMEM((kept, pixels, 256), f32),
            pltpu.VMEM((kept, pixels, 256), f32),
            pltpu.VMEM((kept, 8, 256), f32),
            pltpu.VMEM((kept, fields * owners, 512), bf16),
            pltpu.VMEM((fields * owners, capacity), f32),
        ],
        compiler_params=pltpu.CompilerParams(vmem_limit_bytes=render_vmem_bytes),
        name="render",
    )(counts, tile_row, lists, rank, at_rank, fetched, d_image)


def body(params, camera, tile_lists, tile_counts, d_image):
    owners = lax.axis_size("tiles")
    views = lax.axis_size("views")
    channels, shard_size = params.shape
    shift = shard_size.bit_length() - 1
    tiles, slots = tile_lists.shape[1:]
    pixels = d_image.shape[3]
    capacity = 3 * tiles * slots // (2 * owners)
    rows = shard_size // 256
    part_rows = rows // views
    center = jnp.array([tiles * 8.0, owners * 8.0, 0.0], f32)
    camera_row = jnp.concatenate([jnp.cos(camera[0, :1]), jnp.sin(camera[0, :1]), camera[0, 1:4], center])
    counts = tile_counts[0]
    lists = tile_lists[0]
    tile_row = lax.axis_index("tiles").astype(i32).reshape(1)
    view_here = lax.axis_index("views").astype(i32).reshape(1)
    smem = pl.BlockSpec(memory_space=pltpu.SMEM)
    vmem = pl.BlockSpec(memory_space=pltpu.VMEM)

    def settings(mebibytes):
        return pltpu.CompilerParams(vmem_limit_bytes=mebibytes * 1024 * 1024)

    requests, rank = pl.pallas_call(
        functools.partial(bucket_kernel, owners=owners, capacity=capacity, shift=shift),
        out_shape=(
            jax.ShapeDtypeStruct((owners, 1, capacity), i32),
            jax.ShapeDtypeStruct((tiles, slots), i32),
        ),
        in_specs=[smem, vmem],
        out_specs=(vmem, vmem),
        scratch_shapes=[
            pltpu.VMEM((tiles * slots // 256 * owners, 256), bf16),
            pltpu.VMEM((tiles * slots // 256 * owners, 256), f32),
        ],
        compiler_params=settings(56),
        name="bucket",
    )(counts, lists)
    asked = lax.all_to_all(requests, "tiles", split_axis=0, concat_axis=0, tiled=True)
    table, third, part_params = pl.pallas_call(
        project_kernel,
        out_shape=(
            jax.ShapeDtypeStruct((fields * rows, 512), bf16),
            jax.ShapeDtypeStruct((2 * rows, 256), bf16),
            jax.ShapeDtypeStruct((channels, part_rows, 256), f32),
        ),
        in_specs=[smem, smem, vmem],
        out_specs=(vmem, vmem, vmem),
        scratch_shapes=[pltpu.VMEM((channels, rows, 256), f32)],
        compiler_params=settings(16),
        name="project",
    )(camera_row, view_here, params)
    found = pl.pallas_call(
        functools.partial(lookup_kernel, group=2),
        out_shape=jax.ShapeDtypeStruct((owners, 1, fields * capacity), f32),
        in_specs=[vmem, vmem, vmem],
        out_specs=vmem,
        scratch_shapes=[pltpu.VMEM((2, 256, 2 * capacity), bf16)],
        compiler_params=settings(16),
        name="lookup",
    )(asked, table, third)
    late_rank, found = lax.optimization_barrier((rank, found))
    fetched = lax.all_to_all(found, "tiles", split_axis=0, concat_axis=0, tiled=True)
    at_rank = pl.pallas_call(
        rank_picks_kernel,
        out_shape=jax.ShapeDtypeStruct((tiles * slots // 256 + 1, capacity, 256), bf16),
        in_specs=[vmem],
        out_specs=vmem,
        compiler_params=settings(16),
        name="rank_picks",
    )(late_rank)
    picture, outgoing = render_call(counts, tile_row, lists, rank, at_rank, fetched, d_image[0], shift)
    late_asked, outgoing = lax.optimization_barrier((asked, outgoing))
    asked_pick = pl.pallas_call(
        functools.partial(asked_picks_kernel, group=2),
        out_shape=jax.ShapeDtypeStruct((owners // 2, 256, 2 * capacity), bf16),
        in_specs=[vmem],
        out_specs=vmem,
        compiler_params=settings(16),
        name="asked_picks",
    )(late_asked)
    returned = lax.all_to_all(outgoing, "tiles", split_axis=0, concat_axis=0, tiled=True)
    sums = pl.pallas_call(
        functools.partial(collect_kernel, rows=rows, group=2),
        out_shape=[jax.ShapeDtypeStruct((fields * part_rows + 8, 256), f32)] * views,
        in_specs=[smem, smem, vmem, vmem, vmem],
        out_specs=[vmem] * views,
        scratch_shapes=collect_scratch(2, rows, capacity),
        compiler_params=settings(16),
        name="collect",
    )(camera_row, view_here, asked, asked_pick, returned)
    all_sums = [sums[0]] + [
        lax.ppermute(sums[offset], "views", [(view, (view + offset) % views) for view in range(views)])
        for offset in range(1, views)
    ]
    grads = pl.pallas_call(
        pull_kernel,
        out_shape=jax.ShapeDtypeStruct((channels, part_rows * 256), f32),
        in_specs=[vmem] * (views + 1),
        out_specs=vmem,
        compiler_params=settings(16),
        name="pull",
    )(*all_sums, part_params)
    return picture[None], grads


def solution(mesh):
    placed = (
        P(None, "tiles"),
        P("views", None),
        P("views", "tiles", None),
        P("views", "tiles"),
        P("views", "tiles", None, None),
    )
    return jax.shard_map(
        body,
        mesh=mesh,
        in_specs=placed,
        out_specs=(P("views", "tiles", None, None), P(None, ("tiles", "views"))),
        check_vma=False,
    )
```

```python
import functools
import math

import jax
import jax.numpy as jnp
from jax import lax
from jax.experimental import pallas as pl
from jax.experimental.pallas import tpu as pltpu
from jax.sharding import PartitionSpec as P

focal_px = 600.0
lowpass = 0.3
harmonic_zero = 0.28209479177387814
harmonic_one = 0.4886025119029199
harmonic_two = (
    1.0925484305920792,
    -1.0925484305920792,
    0.31539156525252005,
    -1.0925484305920792,
    0.5462742152960396,
)
harmonic_three = (
    -0.5900435899266435,
    2.890611442640554,
    -0.4570457994644658,
    0.3731763325901154,
    -0.4570457994644658,
    1.445305721320277,
    -0.5900435899266435,
)
bf16 = jnp.bfloat16
f32 = jnp.float32
i32 = jnp.int32
log2_e = 1.0 / math.log(2.0)
ln_2 = math.log(2.0)
nt_dims = (((1,), (1,)), ((), ()))
render_vmem_bytes = 48 * 1024 * 1024
fields = 9


def split_two(values):
    upper = values.astype(bf16)
    lower = (values - upper.astype(f32)).astype(bf16)
    return upper, lower


def split_three(values):
    upper = values.astype(bf16)
    rest = values - upper.astype(f32)
    middle = rest.astype(bf16)
    lower = (rest - middle.astype(f32)).astype(bf16)
    return upper, middle, lower


def project(gauss_rows, camera_row, center_x, center_y):
    cosine, sine_val, shift_x, shift_y, shift_z = camera_row
    cam_x = cosine * gauss_rows[0] + sine_val * gauss_rows[2] + shift_x
    cam_y = gauss_rows[1] + shift_y
    cam_z = cosine * gauss_rows[2] - sine_val * gauss_rows[0] + shift_z
    inverse_z = 1.0 / cam_z
    jac_a = focal_px * inverse_z
    pos_u = jac_a * cam_x + center_x
    pos_v = jac_a * cam_y + center_y
    jac_b = -jac_a * cam_x * inverse_z
    jac_c = -jac_a * cam_y * inverse_z
    first_row = (jac_a * cosine - jac_b * sine_val, jac_a * sine_val + jac_b * cosine)
    second_row = (-jac_c * sine_val, jac_a, jac_c * cosine)
    quaternion = gauss_rows[6:10]
    inv_norm = lax.rsqrt(
        quaternion[0] * quaternion[0]
        + quaternion[1] * quaternion[1]
        + quaternion[2] * quaternion[2]
        + quaternion[3] * quaternion[3]
    )
    quat_w, quat_x, quat_y, quat_z = (entry * inv_norm for entry in quaternion)
    rotation = (
        (
            1.0 - 2.0 * (quat_y * quat_y + quat_z * quat_z),
            2.0 * (quat_x * quat_y - quat_w * quat_z),
            2.0 * (quat_x * quat_z + quat_w * quat_y),
        ),
        (
            2.0 * (quat_x * quat_y + quat_w * quat_z),
            1.0 - 2.0 * (quat_x * quat_x + quat_z * quat_z),
            2.0 * (quat_y * quat_z - quat_w * quat_x),
        ),
        (
            2.0 * (quat_x * quat_z - quat_w * quat_y),
            2.0 * (quat_y * quat_z + quat_w * quat_x),
            1.0 - 2.0 * (quat_x * quat_x + quat_y * quat_y),
        ),
    )
    scales = [jnp.exp(entry) for entry in gauss_rows[3:6]]
    upper_a = [
        (first_row[0] * rotation[0][entry] + first_row[1] * rotation[2][entry]) * scales[entry]
        for entry in range(3)
    ]
    lower_a = [
        (
            second_row[0] * rotation[0][entry]
            + second_row[1] * rotation[1][entry]
            + second_row[2] * rotation[2][entry]
        )
        * scales[entry]
        for entry in range(3)
    ]
    cov_a = upper_a[0] * upper_a[0] + upper_a[1] * upper_a[1] + upper_a[2] * upper_a[2] + lowpass
    cov_b = upper_a[0] * lower_a[0] + upper_a[1] * lower_a[1] + upper_a[2] * lower_a[2]
    cov_c = lower_a[0] * lower_a[0] + lower_a[1] * lower_a[1] + lower_a[2] * lower_a[2] + lowpass
    inv_det = 1.0 / (cov_a * cov_c - cov_b * cov_b)
    coef_a = (-0.5 * log2_e) * cov_c * inv_det
    coef_b = log2_e * cov_b * inv_det
    coef_c = (-0.5 * log2_e) * cov_a * inv_det
    log_opacity = -log2_e * jnp.log(1.0 + jnp.exp(-gauss_rows[10]))
    dir_x = cosine * cam_x - sine_val * cam_z
    dir_y = cam_y
    dir_z = sine_val * cam_x + cosine * cam_z
    inv_len = lax.rsqrt(dir_x * dir_x + dir_y * dir_y + dir_z * dir_z)
    dir_x = dir_x * inv_len
    dir_y = dir_y * inv_len
    dir_z = dir_z * inv_len
    sq_x = dir_x * dir_x
    sq_y = dir_y * dir_y
    sq_z = dir_z * dir_z
    harmonics = (
        harmonic_zero,
        -harmonic_one * dir_y,
        harmonic_one * dir_z,
        -harmonic_one * dir_x,
        harmonic_two[0] * dir_x * dir_y,
        harmonic_two[1] * dir_y * dir_z,
        harmonic_two[2] * (2.0 * sq_z - sq_x - sq_y),
        harmonic_two[3] * dir_x * dir_z,
        harmonic_two[4] * (sq_x - sq_y),
        harmonic_three[0] * dir_y * (3.0 * sq_x - sq_y),
        harmonic_three[1] * dir_x * dir_y * dir_z,
        harmonic_three[2] * dir_y * (4.0 * sq_z - sq_x - sq_y),
        harmonic_three[3] * dir_z * (2.0 * sq_z - 3.0 * sq_x - 3.0 * sq_y),
        harmonic_three[4] * dir_x * (4.0 * sq_z - sq_x - sq_y),
        harmonic_three[5] * dir_z * (sq_x - sq_y),
        harmonic_three[6] * dir_x * (sq_x - 3.0 * sq_y),
    )
    colors = []
    for channel in range(3):
        total = harmonics[0] * gauss_rows[11 + channel] + 0.5
        for basis in range(1, 16):
            total = total + harmonics[basis] * gauss_rows[11 + 3 * basis + channel]
        colors.append(total)
    return (pos_u, pos_v, coef_a, coef_b, coef_c, log_opacity, *colors)


def project_kernel(camera_ref, place_ref, params_ref, table_ref, third_ref, part_ref, dense_ref):
    channels, rows, _ = dense_ref.shape
    part_rows = part_ref.shape[1]
    camera_row = [camera_ref[entry] for entry in range(5)]
    center_x, center_y = camera_ref[5], camera_ref[6]
    for channel in range(channels):
        for row in range(rows):
            dense_ref[channel, row : row + 1, :] = params_ref[channel : channel + 1, row * 256 : row * 256 + 256]

    def step(part, carry):
        at = pl.multiple_of(part * 16, 16)
        gauss_rows = [dense_ref[channel, pl.ds(at, 16), :] for channel in range(channels)]
        outputs = project(gauss_rows, camera_row, center_x, center_y)
        for field, values in enumerate(outputs):
            pieces = split_three(values)
            table_ref[pl.ds(field * rows + at, 16), :256] = pieces[0]
            table_ref[pl.ds(field * rows + at, 16), 256:] = pieces[1]
            if field < 2:
                third_ref[pl.ds(field * rows + at, 16), :] = pieces[2]
        return carry

    lax.fori_loop(0, rows // 16, step, 0)
    at = pl.multiple_of(place_ref[0] * part_rows, part_rows)
    for channel in range(channels):
        part_ref[channel] = dense_ref[channel, pl.ds(at, part_rows), :]


def bucket_kernel(counts_ref, lists_ref, requests_ref, rank_ref, hits_ref, earlier_ref, *, owners, capacity, shift):
    tiles, slots = lists_ref.shape
    blocks = slots // 256
    thirds = capacity // 128
    upper = (
        lax.broadcasted_iota(i32, (256, 256), 0) < lax.broadcasted_iota(i32, (256, 256), 1)
    ).astype(f32).astype(bf16)
    owner_rows = lax.broadcasted_iota(i32, (owners, 256), 0)
    lane = lax.broadcasted_iota(i32, (1, 256), 1)
    for tile in range(tiles):
        for block in range(blocks):
            ids = lists_ref[tile : tile + 1, block * 256 : block * 256 + 256]
            owner = jnp.where(lane + block * 256 < counts_ref[tile], ids >> shift, -1)
            at = (tile * blocks + block) * owners
            hits_ref[at : at + owners, :] = jnp.where(owner_rows == owner, 1.0, 0.0).astype(bf16)
    earlier_ref[...] = jnp.dot(hits_ref[...], upper, preferred_element_type=f32)
    low_rows = lax.broadcasted_iota(i32, (128, 256), 0)
    high_rows = lax.broadcasted_iota(i32, (owners * thirds, 256), 0)
    carry = jnp.zeros((owners, 1), f32)
    total = jnp.zeros((2 * owners * thirds, 128), f32)
    for tile in range(tiles):
        for block in range(blocks):
            at = (tile * blocks + block) * owners
            hits = hits_ref[at : at + owners, :].astype(f32)
            earlier = earlier_ref[at : at + owners, :]
            rank = jnp.sum(hits * (earlier + carry), axis=0, keepdims=True).astype(i32)
            live = lane + block * 256 < counts_ref[tile]
            rank_ref[tile : tile + 1, block * 256 : block * 256 + 256] = jnp.where(live, rank, -1)
            carry = carry + earlier[:, 255:256] + hits[:, 255:256]
            ids = lists_ref[tile : tile + 1, block * 256 : block * 256 + 256]
            local = (ids & ((1 << shift) - 1)) + 1
            coarse = (local >> 7).astype(f32)
            fine = (local & 127).astype(f32)
            place = jnp.where(live, (ids >> shift) * thirds + (rank >> 7), -1)
            mask = high_rows == place
            placed = jnp.concatenate(
                [jnp.where(mask, coarse, 0.0), jnp.where(mask, fine, 0.0)], axis=0
            ).astype(bf16)
            at_rank = jnp.where(low_rows == (rank & 127), 1.0, 0.0).astype(bf16)
            total = total + lax.dot_general(placed, at_rank, nt_dims, preferred_element_type=f32)
    requests = (total[: owners * thirds] * 128.0 + total[owners * thirds :]).astype(i32) - 1
    for owner in range(owners):
        for third in range(thirds):
            row = owner * thirds + third
            requests_ref[owner, :, third * 128 : third * 128 + 128] = requests[row : row + 1]


def lookup_kernel(asked_ref, table_ref, third_ref, found_ref, pick_ref, *, group):
    askers, _, capacity = asked_ref.shape
    rows = table_ref.shape[0] // fields
    width = group * capacity
    steps = askers // group
    low_rows = lax.broadcasted_iota(i32, (256, width), 0)
    high_rows = lax.broadcasted_iota(i32, (rows, width), 0)

    def asked_of(part):
        return jnp.concatenate([asked_ref[group * part + k] for k in range(group)], axis=1)

    def prepare(part):
        pick_ref[part % 2] = jnp.where(low_rows == (asked_of(part) & 255), 1.0, 0.0).astype(bf16)

    def multiply(part):
        pick = pick_ref[part % 2]
        result = jnp.dot(
            table_ref[...], jnp.concatenate([pick, pick], axis=0), preferred_element_type=f32
        )
        third = jnp.dot(third_ref[...], pick, preferred_element_type=f32)
        return result, third

    def choose(part, result, third):
        mask = high_rows == (asked_of(part) >> 8)
        for field in range(fields):
            values = result[field * rows : (field + 1) * rows]
            if field < 2:
                values = values + third[field * rows : (field + 1) * rows]
            found = jnp.sum(jnp.where(mask, values, 0.0), axis=0, keepdims=True)
            for k in range(group):
                found_ref[group * part + k, :, field * capacity : (field + 1) * capacity] = found[
                    :, k * capacity : (k + 1) * capacity
                ]

    prepare(0)
    for part in range(steps):
        result, third = multiply(part)
        if part + 1 < steps:
            prepare(part + 1)
        choose(part, result, third)


def collect_kernel(camera_ref, place_ref, asked_ref, returned_ref, *rest, rows, group):
    *sums_refs, total_ref, pick_ref, placed_ref = rest
    askers, _, capacity = asked_ref.shape
    views = len(sums_refs)
    width = group * capacity
    steps = askers // group
    low_rows = lax.broadcasted_iota(i32, (256, width), 0)
    high_rows = lax.broadcasted_iota(i32, (rows, width), 0)

    def prepare(part):
        at = part % 2
        asked = jnp.concatenate([asked_ref[group * part + k] for k in range(group)], axis=1)
        pick_ref[at] = jnp.where(low_rows == (asked & 255), 1.0, 0.0).astype(bf16)
        mask = high_rows == (asked >> 8)
        for field in range(fields):
            values = jnp.concatenate(
                [
                    returned_ref[group * part + k, :, field * capacity : (field + 1) * capacity]
                    for k in range(group)
                ],
                axis=1,
            )
            upper = values.astype(bf16).astype(f32)
            row = field * rows
            placed_ref[at, row : row + rows, :width] = jnp.where(mask, upper, 0.0).astype(bf16)
            placed_ref[at, row : row + rows, width:] = jnp.where(mask, values - upper, 0.0).astype(bf16)

    def multiply(part):
        at = part % 2
        pick = pick_ref[at]
        return lax.dot_general(
            placed_ref[at], jnp.concatenate([pick, pick], axis=1), nt_dims, preferred_element_type=f32
        )

    prepare(0)
    for part in range(steps):
        product = multiply(part)
        if part + 1 < steps:
            prepare(part + 1)
        total_ref[...] = product if part == 0 else total_ref[...] + product

    part_rows = rows // views
    for offset, sums_ref in enumerate(sums_refs):
        view = lax.rem(place_ref[0] + offset, views)
        for field in range(fields):
            at = pl.multiple_of(field * rows + view * part_rows, part_rows)
            sums_ref[field * part_rows : (field + 1) * part_rows, :] = total_ref[pl.ds(at, part_rows), :]
        for entry in range(8):
            at = fields * part_rows + entry
            sums_ref[at : at + 1, :] = jnp.full((1, 256), camera_ref[entry], f32)


def collect_scratch(group, rows, capacity):
    return [
        pltpu.VMEM((fields * rows, 256), f32),
        pltpu.VMEM((2, 256, group * capacity), bf16),
        pltpu.VMEM((2, fields * rows, 2 * group * capacity), bf16),
    ]


def pull_kernel(*refs):
    *sums_refs, params_ref, grads_ref = refs
    channels, part_rows, _ = params_ref.shape
    gauss_rows = [params_ref[channel] for channel in range(channels)]
    totals = None
    for sums_ref in sums_refs:
        at = fields * part_rows
        camera_row = [
            jnp.broadcast_to(sums_ref[at + entry : at + entry + 1, :], (part_rows, 256))
            for entry in range(5)
        ]
        _, pull = jax.vjp(lambda rows_in: project(rows_in, camera_row, 0.0, 0.0), gauss_rows)
        (one,) = pull(
            tuple(
                sums_ref[field * part_rows : (field + 1) * part_rows, :]
                for field in range(fields)
            )
        )
        totals = one if totals is None else [x + y for x, y in zip(totals, one)]
    for channel in range(channels):
        for row in range(part_rows):
            grads_ref[channel : channel + 1, row * 256 : row * 256 + 256] = totals[channel][
                row : row + 1
            ]


def monomial(index, pix_x, pix_y):
    pix_x = pix_x.astype(f32) - 7.5
    pix_y = pix_y.astype(f32) - 7.5
    values = jnp.where(index == 0, 1.0, 0.0)
    values = jnp.where(index == 1, pix_x, values)
    values = jnp.where(index == 2, pix_y, values)
    values = jnp.where(index == 3, pix_x * pix_x, values)
    values = jnp.where(index == 4, pix_x * pix_y, values)
    return jnp.where(index == 5, pix_y * pix_y, values)


def render_kernel(
    counts_ref,
    place_ref,
    lists_ref,
    rank_ref,
    fetched_ref,
    d_image_ref,
    image_ref,
    outgoing_ref,
    item_ref,
    rows_ref,
    fetch_ref,
    value_ref,
    polynomial_ref,
    color_rows_ref,
    color_left_ref,
    d_columns_ref,
    d_left_ref,
    earlier_ref,
    later_ref,
    blend_ref,
    ratio_ref,
    color_grad_ref,
    placed_ref,
    at_rank_ref,
    outgo_ref,
    *,
    shift,
):
    tiles, slots = lists_ref.shape
    owners, _, width = fetched_ref.shape
    capacity = width // fields
    spare = tiles * slots // 256
    pixels = d_image_ref.shape[2]

    def list_tile(tile, base):
        live_blocks = (counts_ref[tile] + 255) // 256

        def list_block(block, carry):
            item_ref[0, base + block] = tile
            item_ref[1, base + block] = block
            item_ref[2, base + block] = base + live_blocks - 1 - block
            return carry

        lax.fori_loop(0, live_blocks, list_block, 0)
        return base + live_blocks

    items = lax.fori_loop(0, tiles, list_tile, 0)
    for owner in range(owners):
        for field in range(fields):
            row = field * owners + owner
            rows_ref[row : row + 1, :] = fetched_ref[owner, :, field * capacity : (field + 1) * capacity]
    center_v = place_ref[0].astype(f32) * 16.0 + 8.0
    for field in range(fields):
        values = rows_ref[field * owners : (field + 1) * owners, :]
        if field == 1:
            values = values - center_v
        upper, lower = split_two(values)
        fetch_ref[field * owners : (field + 1) * owners, :capacity] = upper
        fetch_ref[field * owners : (field + 1) * owners, capacity:] = lower
    for tile in range(tiles):
        d_rows = d_image_ref[tile]
        d_upper, d_lower = [piece.astype(f32) for piece in split_two(d_rows)]
        d_stack = jnp.concatenate([d_upper, d_lower, d_upper, d_lower, jnp.zeros((4, pixels), f32)], axis=0)
        d_columns_ref[tile] = jnp.transpose(d_stack).astype(bf16)
        d_left_ref[tile] = jnp.concatenate([d_upper, d_lower, jnp.zeros((10, pixels), f32)], axis=0).astype(bf16)
    outgo_ref[...] = jnp.zeros_like(outgo_ref)
    placed_ref[spare] = jnp.zeros(placed_ref.shape[1:], bf16)
    at_rank_ref[spare] = jnp.zeros(at_rank_ref.shape[1:], bf16)
    row_index = lax.broadcasted_iota(i32, (256, 256), 0)
    lane_index = lax.broadcasted_iota(i32, (256, 256), 1)
    before = (row_index < lane_index).astype(f32).astype(bf16)
    after = (row_index > lane_index).astype(f32).astype(bf16)
    pixel_row = lax.broadcasted_iota(i32, (pixels, 24), 0)
    monomials = monomial(
        lax.broadcasted_iota(i32, (pixels, 24), 1) & 7, pixel_row & 15, pixel_row >> 4
    ).astype(bf16)
    pixel_lane = lax.broadcasted_iota(i32, (16, pixels), 1)
    moments_of = monomial(
        lax.broadcasted_iota(i32, (16, pixels), 0), pixel_lane & 15, pixel_lane >> 4
    ).astype(bf16)
    rank_rows = lax.broadcasted_iota(i32, (capacity, 256), 0)
    owner_rows = lax.broadcasted_iota(i32, (owners, 256), 0)

    def owner_and_rank(item):
        tile = item_ref[0, item]
        at = pl.multiple_of(item_ref[1, item] * 256, 256)
        owner = lists_ref[pl.ds(tile, 1), pl.ds(at, 256)] >> shift
        rank = rank_ref[pl.ds(tile, 1), pl.ds(at, 256)]
        return owner, rank

    def fetch(item):
        owner, rank = owner_and_rank(item)
        tile = item_ref[0, item]
        at_rank = jnp.where(rank_rows == rank, 1.0, 0.0).astype(bf16)
        at_rank_ref[item] = at_rank
        yield
        fetched = jnp.dot(
            fetch_ref[...], jnp.concatenate([at_rank, at_rank], axis=0), preferred_element_type=f32
        )
        mask = owner_rows == owner
        found = []
        for field in range(fields):
            if field in (0, 5):
                yield
            values = fetched[field * owners : (field + 1) * owners]
            found.append(jnp.sum(jnp.where(mask, values, 0.0), axis=0, keepdims=True))
        yield
        pos_u = found[0] - (tile.astype(f32) * 16.0 + 8.0)
        pos_v = found[1]
        coef_a, coef_b, coef_c, log_opacity = found[2:6]
        log_opacity = jnp.where(rank >= 0, log_opacity, -1.0e4)
        slope_u = coef_a * pos_u * 2.0 + coef_b * pos_v
        slope_v = coef_c * pos_v * 2.0 + coef_b * pos_u
        constant = log_opacity + 0.5 * (slope_u * pos_u + slope_v * pos_v)
        blank = jnp.zeros((3, 256), f32)
        value_ref[item] = jnp.concatenate([pos_u, pos_v, coef_a, coef_b, coef_c, blank], axis=0)
        polynomial = jnp.concatenate(
            [constant, -slope_u, -slope_v, coef_a, coef_b, coef_c, blank[0:2]], axis=0
        )
        pieces = [piece.astype(f32) for piece in split_three(polynomial)]
        polynomial_ref[item] = jnp.concatenate(pieces, axis=0).astype(bf16)
        upper, lower = [piece.astype(f32) for piece in split_two(jnp.concatenate(found[6:9], axis=0))]
        color_rows_ref[item] = jnp.concatenate(
            [upper, upper, lower, lower, jnp.zeros((4, 256), f32)], axis=0
        ).astype(bf16)
        color_left_ref[item] = jnp.concatenate(
            [upper, lower, jnp.zeros((10, 256), f32)], axis=0
        ).astype(bf16)
        yield

    def forward(item):
        at = item
        tile = item_ref[0, item]
        first = item_ref[1, item] == 0
        exponent = jnp.dot(monomials, polynomial_ref[at], preferred_element_type=f32)
        yield
        earlier = jnp.where(first, 0.0, earlier_ref[...])
        earlier = jnp.concatenate([earlier, earlier], axis=1)
        alpha = jnp.exp2(exponent)
        keep = 1.0 - alpha
        log_keep = jnp.log2(keep)
        upper, lower = split_two(log_keep)
        yield
        within = jnp.dot(upper, before, preferred_element_type=f32) + jnp.dot(
            lower, before, preferred_element_type=f32
        )
        pull = jnp.dot(d_columns_ref[tile], color_rows_ref[at], preferred_element_type=f32)
        yield
        within = within + earlier
        weight = jnp.exp2(within) * alpha
        earlier_ref[...] = jnp.broadcast_to(within[:, 255:256] + log_keep[:, 255:256], (pixels, 128))
        blend_ref[at] = weight * pull
        ratio_ref[at] = alpha / keep
        upper, lower = split_two(weight)
        yield
        d_left = d_left_ref[tile]
        one = jnp.dot(d_left, upper, preferred_element_type=f32)
        two = jnp.dot(d_left, lower, preferred_element_type=f32)
        color_grad_ref[at, 0:3] = one[0:3] + one[3:6] + two[0:3]
        color_left = color_left_ref[at]
        one = lax.dot_general(color_left, upper, nt_dims, preferred_element_type=f32)
        two = lax.dot_general(color_left, lower, nt_dims, preferred_element_type=f32)
        picture = one[0:3] + one[3:6] + two[0:3]
        image_ref[tile] = jnp.where(first, 0.0, image_ref[tile]) + picture
        yield

    def backward(step):
        at = item_ref[2, step]
        first = item_ref[1, step] == 0
        owner, rank = owner_and_rank(at)
        blend = blend_ref[at]
        upper, lower = split_two(blend)
        within = jnp.dot(upper, after, preferred_element_type=f32) + jnp.dot(
            lower, after, preferred_element_type=f32
        )
        yield
        later = jnp.where(first, 0.0, later_ref[...])
        within = within + jnp.concatenate([later, later], axis=1)
        later_ref[...] = jnp.broadcast_to(within[:, 0:1] + blend[:, 0:1], (pixels, 128))
        gradient = blend - within * ratio_ref[at]
        pieces = split_two(gradient)
        yield
        moments = (
            jnp.dot(moments_of, pieces[0], preferred_element_type=f32)
            + jnp.dot(moments_of, pieces[1], preferred_element_type=f32)
        ) * ln_2
        yield
        plain, first_x, first_y = moments[0:1], moments[1:2], moments[2:3]
        pos_u, pos_v, coef_a, coef_b, coef_c = (value_ref[at, k : k + 1] for k in range(5))
        from_u = first_x - pos_u * plain
        from_v = first_y - pos_v * plain
        outputs = [
            -2.0 * coef_a * from_u - coef_b * from_v,
            -2.0 * coef_c * from_v - coef_b * from_u,
            moments[3:4] - pos_u * (first_x + from_u),
            moments[4:5] - pos_v * first_x - pos_u * from_v,
            moments[5:6] - pos_v * (first_y + from_v),
            plain,
        ] + [color_grad_ref[at, k : k + 1] for k in range(3)]
        mask = owner_rows == jnp.where(rank >= 0, owner, -1)
        for field, values in enumerate(outputs):
            upper = values.astype(bf16).astype(f32)
            row = field * owners
            placed_ref[at, row : row + owners, :256] = jnp.where(mask, upper, 0.0).astype(bf16)
            placed_ref[at, row : row + owners, 256:] = jnp.where(mask, values - upper, 0.0).astype(bf16)
        yield

    def send(item):
        at = jnp.where(item < 0, spare, item)
        outgo_ref[...] += lax.dot_general(
            placed_ref[at],
            jnp.concatenate([at_rank_ref[at], at_rank_ref[at]], axis=1),
            nt_dims,
            preferred_element_type=f32,
        )
        yield

    def send_step(step):
        return send(jnp.where(step < 0, -1, item_ref[2, jnp.maximum(step, 0)]))

    lag = 5

    def run(order, **stages):
        for name in order:
            next(stages[name])
        for left in stages.values():
            for _ in left:
                raise ValueError(order)

    def ramp_up(step, carry):
        run("mfmmffmfmf", m=forward(step - 1), f=fetch(step))
        return carry

    def steady(step, carry):
        run(
            "bmmsfmbfmfbmbff",
            s=send_step(step - lag - 1),
            b=backward(step - lag),
            m=forward(step - 1),
            f=fetch(step),
        )
        return carry

    def ramp_down(step, carry):
        run("bsbbb", s=send_step(step - lag - 1), b=backward(step - lag))
        return carry

    run("fffff", f=fetch(0))
    lax.fori_loop(1, lag, ramp_up, 0)
    lax.fori_loop(lag, items, steady, 0)
    run("mbsmmbmbmb", s=send_step(items - lag - 1), b=backward(items - lag), m=forward(items - 1))
    lax.fori_loop(items + 1, items + lag, ramp_down, 0)
    run("s", s=send_step(items - 1))
    for owner in range(owners):
        for field in range(fields):
            row = field * owners + owner
            outgoing_ref[owner, :, field * capacity : (field + 1) * capacity] = outgo_ref[row : row + 1, :]


def render_call(counts, tile_row, lists, rank, fetched, d_image, shift):
    owners, _, width = fetched.shape
    capacity = width // fields
    tiles, slots = lists.shape
    pixels = d_image.shape[2]
    kept = tiles * slots // 256 + 1
    smem = pl.BlockSpec(memory_space=pltpu.SMEM)
    vmem = pl.BlockSpec(memory_space=pltpu.VMEM)
    return pl.pallas_call(
        functools.partial(render_kernel, shift=shift),
        out_shape=(
            jax.ShapeDtypeStruct((tiles, 3, pixels), f32),
            jax.ShapeDtypeStruct((owners, 1, fields * capacity), f32),
        ),
        in_specs=[smem, smem, vmem, vmem, vmem, vmem],
        out_specs=(vmem, vmem),
        scratch_shapes=[
            pltpu.SMEM((3, kept), i32),
            pltpu.VMEM((fields * owners, capacity), f32),
            pltpu.VMEM((fields * owners, 2 * capacity), bf16),
            pltpu.VMEM((kept, 8, 256), f32),
            pltpu.VMEM((kept, 24, 256), bf16),
            pltpu.VMEM((kept, 16, 256), bf16),
            pltpu.VMEM((kept, 16, 256), bf16),
            pltpu.VMEM((tiles, pixels, 16), bf16),
            pltpu.VMEM((tiles, 16, pixels), bf16),
            pltpu.VMEM((pixels, 128), f32),
            pltpu.VMEM((pixels, 128), f32),
            pltpu.VMEM((kept, pixels, 256), f32),
            pltpu.VMEM((kept, pixels, 256), f32),
            pltpu.VMEM((kept, 8, 256), f32),
            pltpu.VMEM((kept, fields * owners, 512), bf16),
            pltpu.VMEM((kept, capacity, 256), bf16),
            pltpu.VMEM((fields * owners, capacity), f32),
        ],
        compiler_params=pltpu.CompilerParams(vmem_limit_bytes=render_vmem_bytes),
        name="render",
    )(counts, tile_row, lists, rank, fetched, d_image)


def body(params, camera, tile_lists, tile_counts, d_image):
    owners = lax.axis_size("tiles")
    views = lax.axis_size("views")
    channels, shard_size = params.shape
    shift = shard_size.bit_length() - 1
    tiles, slots = tile_lists.shape[1:]
    pixels = d_image.shape[3]
    capacity = 3 * tiles * slots // (2 * owners)
    rows = shard_size // 256
    part_rows = rows // views
    center = jnp.array([tiles * 8.0, owners * 8.0, 0.0], f32)
    camera_row = jnp.concatenate([jnp.cos(camera[0, :1]), jnp.sin(camera[0, :1]), camera[0, 1:4], center])
    counts = tile_counts[0]
    lists = tile_lists[0]
    tile_row = lax.axis_index("tiles").astype(i32).reshape(1)
    view_here = lax.axis_index("views").astype(i32).reshape(1)
    smem = pl.BlockSpec(memory_space=pltpu.SMEM)
    vmem = pl.BlockSpec(memory_space=pltpu.VMEM)

    def settings(mebibytes):
        return pltpu.CompilerParams(vmem_limit_bytes=mebibytes * 1024 * 1024)

    requests, rank = pl.pallas_call(
        functools.partial(bucket_kernel, owners=owners, capacity=capacity, shift=shift),
        out_shape=(
            jax.ShapeDtypeStruct((owners, 1, capacity), i32),
            jax.ShapeDtypeStruct((tiles, slots), i32),
        ),
        in_specs=[smem, vmem],
        out_specs=(vmem, vmem),
        scratch_shapes=[
            pltpu.VMEM((tiles * slots // 256 * owners, 256), bf16),
            pltpu.VMEM((tiles * slots // 256 * owners, 256), f32),
        ],
        compiler_params=settings(56),
        name="bucket",
    )(counts, lists)
    asked = lax.all_to_all(requests, "tiles", split_axis=0, concat_axis=0, tiled=True)
    table, third, part_params = pl.pallas_call(
        project_kernel,
        out_shape=(
            jax.ShapeDtypeStruct((fields * rows, 512), bf16),
            jax.ShapeDtypeStruct((2 * rows, 256), bf16),
            jax.ShapeDtypeStruct((channels, part_rows, 256), f32),
        ),
        in_specs=[smem, smem, vmem],
        out_specs=(vmem, vmem, vmem),
        scratch_shapes=[pltpu.VMEM((channels, rows, 256), f32)],
        compiler_params=settings(16),
        name="project",
    )(camera_row, view_here, params)
    found = pl.pallas_call(
        functools.partial(lookup_kernel, group=2),
        out_shape=jax.ShapeDtypeStruct((owners, 1, fields * capacity), f32),
        in_specs=[vmem, vmem, vmem],
        out_specs=vmem,
        scratch_shapes=[pltpu.VMEM((2, 256, 2 * capacity), bf16)],
        compiler_params=settings(16),
        name="lookup",
    )(asked, table, third)
    fetched = lax.all_to_all(found, "tiles", split_axis=0, concat_axis=0, tiled=True)
    picture, outgoing = render_call(counts, tile_row, lists, rank, fetched, d_image[0], shift)
    returned = lax.all_to_all(outgoing, "tiles", split_axis=0, concat_axis=0, tiled=True)
    sums = pl.pallas_call(
        functools.partial(collect_kernel, rows=rows, group=2),
        out_shape=[jax.ShapeDtypeStruct((fields * part_rows + 8, 256), f32)] * views,
        in_specs=[smem, smem, vmem, vmem],
        out_specs=[vmem] * views,
        scratch_shapes=collect_scratch(2, rows, capacity),
        compiler_params=settings(16),
        name="collect",
    )(camera_row, view_here, asked, returned)
    all_sums = [sums[0]] + [
        lax.ppermute(sums[offset], "views", [(view, (view + offset) % views) for view in range(views)])
        for offset in range(1, views)
    ]
    grads = pl.pallas_call(
        pull_kernel,
        out_shape=jax.ShapeDtypeStruct((channels, part_rows * 256), f32),
        in_specs=[vmem] * (views + 1),
        out_specs=vmem,
        compiler_params=settings(16),
        name="pull",
    )(*all_sums, part_params)
    return picture[None], grads


def solution(mesh):
    placed = (
        P(None, "tiles"),
        P("views", None),
        P("views", "tiles", None),
        P("views", "tiles"),
        P("views", "tiles", None, None),
    )
    return jax.shard_map(
        body,
        mesh=mesh,
        in_specs=placed,
        out_specs=(P("views", "tiles", None, None), P(None, ("tiles", "views"))),
        check_vma=False,
    )
```
